32 devices in a mesh: dp: 8 (over y, x, core), space: 4 (over z).
Axes of the slice: x: 2, y: 2, z: 4, core: 2. Of those that a mesh axis runs over, the one named last changes fastest.
Arguments:
- features: bfloat16 [8192, 256], P(('dp', 'space')), may hold values from -6 to 6
- weights: bfloat16 [27, 256, 256], replicated, may hold values from -0.125 to 0.125
- cotangent: bfloat16 [8192, 256], P(('dp', 'space')), may hold values from -6 to 6
- kernel_map: int32 [27, 8192], P(None, ('dp', 'space')), may hold values from 0 to 384, as said below
- live: int32 [32], P(('dp', 'space')), may hold values from 64 to 256, as said below
- send_up: int32 [32, 64], P(('dp', 'space')), may hold values from 0 to 255, as said below
- send_down: int32 [32, 64], P(('dp', 'space')), may hold values from 0 to 255, as said below
Outputs:
- out_features: bfloat16 [8192, 256], P(('dp', 'space'))
- grad_features: bfloat16 [8192, 256], P(('dp', 'space'))
- grad_weights: bfloat16 [27, 256, 256], replicated
The draws below stay inside these ranges and needn't reach their ends.
Inputs may be any that keep to these rules, and one draw needn't show every extreme that they name: In each group of 4 devices along space at least one device has all 256 slots live. `send_up`: each entry is a live row of its own device. `send_down`: each entry is a live row of its own device. `kernel_map`: at offset 27 // 2 a live row maps to itself. Rows that are not live map to slot 384 at every offset. Otherwise an entry is a live row of the same device, a slot from 256 to 383, or the zero slot 384.
All inputs are finite; a program needn't handle non-finite values.
Results may differ from the reference program's by a relative error of at most 0.001.
Values may be sent and summed in bfloat16 or wider, within the bound.
No kernel may reach another device: no remote copies, remote signals or barrier semaphores. Data moves between devices by JAX's collectives and lax.ppermute only.
A program may use at most 128 MiB of HBM per device.

```python
import math
import jax
import jax.numpy as jnp
from jax import lax

C = 256
OFFSETS = 27
ROWS_DEV = 256
HALO = 64
ROWS = 8192
N_DP = 8
N_SPACE = 4


def live_counts(key):
    key = jax.random.fold_in(key, 101)
    base = jax.random.randint(jax.random.fold_in(key, 1), (N_DP, N_SPACE), ROWS_DEV // 4, ROWS_DEV + 1)
    peak = jax.random.randint(jax.random.fold_in(key, 2), (N_DP, 1), 0, N_SPACE)
    peak_mask = jnp.arange(N_SPACE, dtype=jnp.int32)[None, :] == peak
    return jnp.where(peak_mask, ROWS_DEV, base).reshape(N_DP * N_SPACE).astype(jnp.int32)


def boundary_rows(key, counts):
    picked = jax.random.randint(key, (N_DP * N_SPACE, HALO), 0, counts[:, None])
    column = jnp.arange(HALO, dtype=jnp.int32)[None, :]
    picked = jnp.where(column == 0, counts[:, None] - 1, picked)
    picked = jnp.where(column == 1, 0, picked)
    return picked.astype(jnp.int32)


def draw_live(key, part):
    return live_counts(key)


def draw_send_up(key, part):
    counts = live_counts(key)
    key = jax.random.fold_in(key, 3)
    return boundary_rows(key, counts)


def draw_send_down(key, part):
    counts = live_counts(key)
    key = jax.random.fold_in(key, 4)
    return boundary_rows(key, counts)


def draw_kernel_map(key, part):
    counts = live_counts(key)
    key = jax.random.fold_in(key, 5)
    total_rows = N_DP * N_SPACE * ROWS_DEV
    columns = jnp.arange(total_rows, dtype=jnp.int32)
    owner = columns // ROWS_DEV
    row_ids = columns % ROWS_DEV
    owner_live = counts[owner]
    shape_all = (OFFSETS, total_rows)
    kinds = jax.random.randint(jax.random.fold_in(key, 1), shape_all, 0, 4)
    local_pick = jax.random.randint(jax.random.fold_in(key, 2), shape_all, 0, owner_live[None, :])
    halo_pick = jax.random.randint(jax.random.fold_in(key, 3), shape_all, ROWS_DEV, ROWS_DEV + 2 * HALO)
    empty_slot = ROWS_DEV + 2 * HALO
    chosen = jnp.where(kinds == 2, local_pick, jnp.where(kinds == 3, halo_pick, empty_slot))
    centre = (jnp.arange(OFFSETS, dtype=jnp.int32) == OFFSETS // 2)[:, None]
    chosen = jnp.where(centre, row_ids[None, :], chosen)
    chosen = jnp.where((row_ids < owner_live)[None, :], chosen, empty_slot)
    return chosen.astype(jnp.int32)


def block_scale(own_key, shape, pieces, smallest, largest):
    gain = 1.0
    for dim, parts in pieces:
        steps = jax.random.uniform(jax.random.fold_in(jax.random.fold_in(own_key, 6), dim), (parts,), jnp.float32, smallest / len(pieces), largest / len(pieces))
        gain = gain * jnp.repeat(jnp.exp(steps), shape[dim] // parts).reshape((-1,) + (1,) * (len(shape) - 1 - dim))
    return gain


def noise(own_key, dims, scale, reach, pieces=(), kind=jnp.bfloat16):
    entries = scale * jax.random.normal(own_key, dims, jnp.float32)
    if pieces:
        entries = entries * block_scale(own_key, dims, pieces, -0.22, 0.18)
    return jnp.clip(entries, -reach, reach).astype(kind)


def setup_inputs(seed: int = 0) -> dict:
    splits = jax.random.split(jax.random.key(seed), 8)
    features = noise(splits[0], (ROWS, C), 1.0, 6.0, ((0, 32),))
    weights = noise(splits[1], (OFFSETS, C, C), (C * 9) ** -0.5, 0.125)
    cotangent = noise(splits[2], (ROWS, C), 1.0, 6.0, ((0, 32),))
    kernel_map = draw_kernel_map(jax.random.fold_in(splits[7], 71), 0)
    live = draw_live(jax.random.fold_in(splits[7], 71), 0)
    send_up = draw_send_up(jax.random.fold_in(splits[7], 71), 0)
    send_down = draw_send_down(jax.random.fold_in(splits[7], 71), 0)
    return dict(features=features, weights=weights, cotangent=cotangent, kernel_map=kernel_map, live=live, send_up=send_up, send_down=send_down)


def one_device(weights, feat_rows, cot_rows, map_rows, rows_lower, rows_upper):
    width = feat_rows.shape[1]
    row_table = jnp.concatenate([feat_rows, rows_lower, rows_upper, jnp.zeros((1, width), feat_rows.dtype)], axis=0)

    def per_offset(carry, inputs):
        out_acc, grad_acc = carry
        weight_k, map_k = inputs
        picked = row_table[map_k]
        out_acc = out_acc + jnp.dot(picked, weight_k, preferred_element_type=jnp.float32)
        back = lax.dot_general(cot_rows, weight_k, (((1,), (1,)), ((), ())), preferred_element_type=jnp.float32)
        grad_acc = grad_acc.at[map_k].add(back)
        wgrad = lax.dot_general(picked, cot_rows, (((0,), (0,)), ((), ())), preferred_element_type=jnp.float32)
        return ((out_acc, grad_acc), wgrad)
    init = (jnp.zeros((feat_rows.shape[0], width), jnp.float32), jnp.zeros((row_table.shape[0], width), jnp.float32))
    (out_acc, grad_acc), wgrads = lax.scan(per_offset, init, (weights, map_rows))
    return (out_acc, grad_acc, wgrads)

def pick_rows(rows_all, index_all):
    return jax.vmap(lambda source, where_rows: source[where_rows])(rows_all, index_all)

def reference(features, weights, cotangent, kernel_map, live, send_up, send_down):
    devices_all = N_DP * N_SPACE
    row_ids = jnp.arange(ROWS_DEV, dtype=jnp.int32)
    live_mask = (row_ids[None, :] < live[:, None])[:, :, None]
    feat_all = jnp.where(live_mask, features.reshape(devices_all, ROWS_DEV, C), jnp.zeros((), features.dtype))
    cot_all = jnp.where(live_mask, cotangent.reshape(devices_all, ROWS_DEV, C), jnp.zeros((), cotangent.dtype))
    map_all = kernel_map.reshape(OFFSETS, devices_all, ROWS_DEV).transpose(1, 0, 2)
    sent_up = pick_rows(feat_all, send_up).reshape(N_DP, N_SPACE, HALO, C)
    sent_down = pick_rows(feat_all, send_down).reshape(N_DP, N_SPACE, HALO, C)
    zero_rows = jnp.zeros((N_DP, 1, HALO, C), features.dtype)
    rows_lower = jnp.concatenate([zero_rows, sent_up[:, :-1]], axis=1).reshape(devices_all, HALO, C)
    rows_upper = jnp.concatenate([sent_down[:, 1:], zero_rows], axis=1).reshape(devices_all, HALO, C)

    def device_step(weight_sum, inputs):
        feat_rows, cot_rows, map_rows, lower_rows, upper_rows = inputs
        out_acc, grad_acc, wgrads = one_device(weights, feat_rows, cot_rows, map_rows, lower_rows, upper_rows)
        return (weight_sum + wgrads, (out_acc, grad_acc))
    weight_sum, (outs, grads) = lax.scan(device_step, jnp.zeros((OFFSETS, C, C), jnp.float32), (feat_all, cot_all, map_all, rows_lower, rows_upper))
    out_features = jnp.where(live_mask, outs, 0.0).astype(jnp.bfloat16).reshape(ROWS, C)
    own_grads = grads[:, :ROWS_DEV]
    zero_grads = jnp.zeros((N_DP, 1, HALO, C), jnp.float32)
    lower_slots = grads[:, ROWS_DEV:ROWS_DEV + HALO].reshape(N_DP, N_SPACE, HALO, C)
    upper_slots = grads[:, ROWS_DEV + HALO:ROWS_DEV + 2 * HALO].reshape(N_DP, N_SPACE, HALO, C)
    back_up = jnp.concatenate([lower_slots[:, 1:], zero_grads], axis=1).reshape(devices_all, HALO, C)
    back_down = jnp.concatenate([zero_grads, upper_slots[:, :-1]], axis=1).reshape(devices_all, HALO, C)
    grad_in = jax.vmap(lambda own, up_rows, up_vals, down_rows, down_vals: own.at[up_rows].add(up_vals).at[down_rows].add(down_vals))(own_grads, send_up, back_up, send_down, back_down)
    grad_features = jnp.where(live_mask, grad_in, 0.0).astype(jnp.bfloat16).reshape(ROWS, C)
    grad_weights = (weight_sum * (1.0 / math.sqrt(ROWS))).astype(jnp.bfloat16)
    return (out_features, grad_features, grad_weights)
```

```python
import functools
import math

import jax
import jax.numpy as jnp
from jax import lax
from jax.experimental import pallas as pl
from jax.experimental.pallas import tpu as pltpu
from jax.sharding import PartitionSpec as P

BF = jnp.bfloat16
F32 = jnp.float32
VMEM_LIMIT = 48 * 1024 * 1024
VMEM = pl.BlockSpec(memory_space=pltpu.VMEM)
SMEM = pl.BlockSpec(memory_space=pltpu.SMEM)


def params():
    return pltpu.CompilerParams(vmem_limit_bytes=VMEM_LIMIT)


def dot(a, b):
    return jnp.dot(a, b, preferred_element_type=F32)


def split(value, terms):
    parts = []
    for _ in range(terms):
        part = value.astype(BF)
        parts.append(part)
        value = value - part.astype(F32)
    return parts


def prep_kernel(live_ref, x_ref, dy_ref, map_ref, up_ref, down_ref, pack_ref, up_rows_ref, down_rows_ref, map_scr):
    rows, width = x_ref.shape
    halo = up_ref.shape[1]
    keep = lax.broadcasted_iota(jnp.int32, (rows, width), 0) < live_ref[0]
    x_live = jnp.where(keep, x_ref[...].astype(F32), 0.0).astype(BF)
    pack_ref[0:rows] = x_live
    pack_ref[rows : 2 * rows] = jnp.where(keep, dy_ref[...].astype(F32), 0.0).astype(BF)
    map_scr[...] = jnp.full(map_scr.shape, rows + 2 * halo, jnp.int32)
    map_scr[0 : map_ref.shape[0]] = map_ref[...]
    slots = map_scr[...]
    pack_ref[2 * rows :] = jnp.where(slots > 256, 256 - slots, slots).astype(F32).astype(BF)
    iota = lax.broadcasted_iota(jnp.int32, (rows, halo), 0)
    for index_ref, picked_ref in ((up_ref, up_rows_ref), (down_ref, down_rows_ref)):
        chosen = (iota == index_ref[...]).astype(F32).astype(BF)
        picked_ref[...] = lax.dot_general(chosen, x_live, (((0,), (0,)), ((), ())), preferred_element_type=F32).astype(BF)


def prep(live, features, cotangent, kernel_map, send_up, send_down, map_rows):
    rows, width = features.shape
    halo = send_up.shape[1]
    return pl.pallas_call(
        prep_kernel,
        out_shape=(
            jax.ShapeDtypeStruct((2 * rows + map_rows, width), BF),
            jax.ShapeDtypeStruct((halo, width), BF),
            jax.ShapeDtypeStruct((halo, width), BF),
        ),
        in_specs=[SMEM] + [VMEM] * 5,
        out_specs=(VMEM,) * 3,
        scratch_shapes=[pltpu.VMEM((map_rows, rows), jnp.int32)],
        compiler_params=params(),
        name="prep",
    )(live, features, cotangent, kernel_map, send_up, send_down)


def own_kernel(live_ref, pack_ref, lower_ref, upper_ref, map_ref, w_ref, out_ref, own_ref, low_ref, high_ref, table, out_acc, grad_acc):
    step = pl.program_id(0)
    offsets = w_ref.shape[0]
    halo, width = lower_ref.shape
    rows = out_ref.shape[0]
    slots = table.shape[0]

    @pl.when(step == 0)
    def _():
        table[0:rows] = pack_ref[0:rows]
        table[rows : rows + halo] = lower_ref[...]
        table[rows + halo :] = upper_ref[...]
        out_acc[...] = jnp.zeros_like(out_acc)
        grad_acc[...] = jnp.zeros_like(grad_acc)

    dy = pack_ref[rows : 2 * rows]
    slot_down = lax.broadcasted_iota(jnp.int32, (slots, rows), 0)
    slot_along = lax.broadcasted_iota(jnp.int32, (rows, 128), 1)
    out_sum = out_acc[...]
    grad_sum = grad_acc[...]
    for i in range(offsets):
        row = map_ref[pl.ds(step * offsets + i, 1), :]
        scatter = (slot_down == row).astype(F32).astype(BF)
        column = jnp.transpose(jnp.broadcast_to(row, (128, rows)))
        gather = jnp.concatenate(
            [(slot_along + 128 * b == column).astype(F32).astype(BF) for b in range(slots // 128)], axis=1
        )
        weight = w_ref[i]
        out_sum = out_sum + dot(dot(gather, table[...]).astype(BF), weight)
        back = lax.dot_general(dy, weight, (((1,), (1,)), ((), ())), preferred_element_type=F32)
        for part in split(back, 2):
            grad_sum = grad_sum + dot(scatter, part)
    out_acc[...] = out_sum
    grad_acc[...] = grad_sum

    @pl.when(step == pl.num_programs(0) - 1)
    def _():
        keep = lax.broadcasted_iota(jnp.int32, (rows, width), 0) < live_ref[0]
        out_ref[...] = jnp.where(keep, out_acc[...], 0.0).astype(BF)
        own_ref[...] = grad_acc[0:rows]
        low_ref[...] = grad_acc[rows : rows + halo]
        high_ref[...] = grad_acc[rows + halo :]


def own(live, pack, lower, upper, kernel_map, weights):
    offsets, width, _ = weights.shape
    halo = lower.shape[0]
    rows = kernel_map.shape[1]
    slots = rows + 2 * halo
    per_step = 3 if offsets % 3 == 0 else 1
    whole = lambda shape: pl.BlockSpec(shape, lambda k: (0,) * len(shape))
    return pl.pallas_call(
        own_kernel,
        grid=(offsets // per_step,),
        out_shape=(
            jax.ShapeDtypeStruct((rows, width), BF),
            jax.ShapeDtypeStruct((rows, width), F32),
            jax.ShapeDtypeStruct((halo, width), F32),
            jax.ShapeDtypeStruct((halo, width), F32),
        ),
        in_specs=[
            SMEM,
            whole(pack.shape),
            whole(lower.shape),
            whole(upper.shape),
            whole(kernel_map.shape),
            pl.BlockSpec((per_step, width, width), lambda k: (k, 0, 0)),
        ],
        out_specs=(whole((rows, width)), whole((rows, width)), whole((halo, width)), whole((halo, width))),
        scratch_shapes=[pltpu.VMEM((slots, width), BF), pltpu.VMEM((rows, width), F32), pltpu.VMEM((slots, width), F32)],
        compiler_params=params(),
        cost_estimate=pl.CostEstimate(flops=12_000_000_000, bytes_accessed=4_500_000, transcendentals=0),
        name="own",
    )(live, pack, lower, upper, kernel_map, weights)


def wgrad_kernel(sources, place_ref, *refs):
    packs, lowers, uppers = refs[:sources], refs[sources : 2 * sources], refs[2 * sources : 3 * sources]
    keep_ref, send_ref, table_t, dys, maps, picked = refs[3 * sources :]
    count, half, width = keep_ref.shape
    halo = lowers[0].shape[0]
    rows = dys.shape[0] // sources
    slots = rows + 2 * halo
    for s in range(sources):
        table_t[:, s * slots : s * slots + rows] = jnp.transpose(packs[s][0:rows])
        table_t[:, s * slots + rows : (s + 1) * slots] = jnp.transpose(
            jnp.concatenate([lowers[s][...], uppers[s][...]], axis=0)
        )
        dys[s * rows : (s + 1) * rows] = packs[s][rows : 2 * rows]
        code = packs[s][2 * rows :].astype(F32).astype(jnp.int32)
        maps[s] = jnp.where(code < 0, 256 - code, code)
    first = place_ref[0] * count
    core = place_ref[1]
    slot_down = lax.broadcasted_iota(jnp.int32, (slots, rows), 0)

    def offset(j, carry):
        for s in range(sources):
            row = maps[s, pl.ds(first + j, 1), :]
            chosen = (slot_down == row).astype(F32).astype(BF)
            picked[:, s * rows : (s + 1) * rows] = dot(table_t[:, s * slots : (s + 1) * slots], chosen).astype(BF)
        send_ref[j] = dot(picked[pl.ds(pl.multiple_of((1 - core) * half, half), half), :], dys[...])
        keep_ref[j] = dot(picked[pl.ds(pl.multiple_of(core * half, half), half), :], dys[...])
        return carry

    lax.fori_loop(0, count, offset, 0)


def wgrad(place, packs, lowers, uppers, count, rows):
    sources = len(packs)
    width = packs[0].shape[1]
    halo = lowers[0].shape[0]
    slots = rows + 2 * halo
    shape = jax.ShapeDtypeStruct((count, width // 2, width), F32)
    return pl.pallas_call(
        functools.partial(wgrad_kernel, sources),
        out_shape=(shape, shape),
        in_specs=[SMEM] + [VMEM] * (3 * sources),
        out_specs=(VMEM, VMEM),
        scratch_shapes=[
            pltpu.VMEM((width, sources * slots), BF),
            pltpu.VMEM((sources * rows, width), BF),
            pltpu.VMEM((sources, packs[0].shape[0] - 2 * rows, rows), jnp.int32),
            pltpu.VMEM((width, sources * rows), BF),
        ],
        compiler_params=params(),
        cost_estimate=pl.CostEstimate(flops=4_000_000_000, bytes_accessed=4_500_000, transcendentals=0),
        name="wgrad",
    )(place, *packs, *lowers, *uppers)


def blocks_kernel(place_ref, keep_ref, got_ref, *block_refs):
    block = block_refs[0].shape[1]
    for m, block_ref in enumerate(block_refs):
        at = pl.ds(pl.multiple_of((place_ref[2] ^ m) * block, block), block)
        block_ref[...] = keep_ref[:, at, :] + got_ref[:, at, :]


def blocks(place, keep, got, parts):
    count, half, width = keep.shape
    shape = jax.ShapeDtypeStruct((count, half // parts, width), F32)
    return pl.pallas_call(
        blocks_kernel,
        out_shape=(shape,) * parts,
        in_specs=[SMEM, VMEM, VMEM],
        out_specs=(VMEM,) * parts,
        compiler_params=params(),
        name="blocks",
    )(place, keep, got)


def final_kernel(live_ref, own_ref, back_up_ref, back_down_ref, up_ref, down_ref, out_ref):
    rows, width = own_ref.shape
    halo = up_ref.shape[1]
    total = own_ref[...]
    iota = lax.broadcasted_iota(jnp.int32, (rows, halo), 0)
    for index_ref, back_ref in ((up_ref, back_up_ref), (down_ref, back_down_ref)):
        chosen = (iota == index_ref[...]).astype(F32).astype(BF)
        for part in split(back_ref[...], 3):
            total = total + dot(chosen, part)
    keep = lax.broadcasted_iota(jnp.int32, (rows, width), 0) < live_ref[0]
    out_ref[...] = jnp.where(keep, total, 0.0).astype(BF)


def final(live, own_grad, back_up, back_down, send_up, send_down):
    return pl.pallas_call(
        final_kernel,
        out_shape=jax.ShapeDtypeStruct(own_grad.shape, BF),
        in_specs=[SMEM] + [VMEM] * 5,
        out_specs=VMEM,
        compiler_params=params(),
        name="final",
    )(live, own_grad, back_up, back_down, send_up, send_down)


def assemble_kernel(groups, place_ref, *refs):
    sources, out_ref, sems = refs[: 2 * groups], refs[2 * groups], refs[2 * groups + 1]
    offsets = out_ref.shape[0]
    parts, count, block, _ = sources[0].shape
    short = offsets - (groups - 1) * count

    def copies(index, part):
        m, o = index // 2, index % 2
        group = place_ref[0] ^ m
        row = ((place_ref[1] ^ o) * parts + (place_ref[2] ^ part)) * block
        row = pl.ds(pl.multiple_of(row, block), block)
        source = sources[index].at[part]
        sem = sems.at[index, part]
        yield group == group, pltpu.make_async_copy(
            source.at[0:short], out_ref.at[pl.ds(group * count, short), row], sem.at[0]
        )
        if short < count:
            yield group < groups - 1, pltpu.make_async_copy(
                source.at[short:count], out_ref.at[pl.ds(group * count + short, count - short), row], sem.at[1]
            )

    for act in ("start", "wait"):
        for index in range(2 * groups):
            for part in range(parts):
                for n, (wanted, copy) in enumerate(copies(index, part)):
                    if n == 0:
                        getattr(copy, act)()
                    else:
                        pl.when(wanted)(getattr(copy, act))


def assemble(place, pieces, offsets, width):
    parts = pieces[0].shape[0]
    return pl.pallas_call(
        functools.partial(assemble_kernel, len(pieces) // 2),
        out_shape=jax.ShapeDtypeStruct((offsets, width, width), BF),
        in_specs=[SMEM] + [pl.BlockSpec(memory_space=pl.ANY)] * len(pieces),
        out_specs=pl.BlockSpec(memory_space=pl.ANY),
        scratch_shapes=[pltpu.SemaphoreType.DMA((len(pieces), parts, 2))],
        compiler_params=params(),
        name="assemble",
    )(place, *pieces)


def assemble_plain(place, pieces, offsets, width):
    parts, count, block, _ = pieces[0].shape
    groups = len(pieces) // 2
    whole = jnp.zeros((groups * count, width, width), BF)
    for index, piece in enumerate(pieces):
        for part in range(parts):
            row = ((place[1] ^ (index % 2)) * parts + (place[2] ^ part)) * block
            whole = lax.dynamic_update_slice(whole, piece[part], ((place[0] ^ (index // 2)) * count, row, 0))
    return whole[:offsets]


def swap(value, axis, mask):
    return lax.ppermute(value, axis, [(i, i ^ mask) for i in range(lax.axis_size(axis))])


def passed_along(value, axis, steps):
    count = lax.axis_size(axis)
    return lax.ppermute(value, axis, [(i, i + steps) for i in range(max(0, -steps), min(count, count - steps))])


def shards(features, weights, cotangent, kernel_map, live, send_up, send_down):
    rows, width = features.shape
    offsets = weights.shape[0]
    groups = lax.axis_size("dp") // 2
    parts = lax.axis_size("space")
    count = -(-offsets // groups)
    map_rows = -(-(groups * count) // 16) * 16
    dp, space = lax.axis_index("dp"), lax.axis_index("space")
    place = jnp.stack([dp // 2, dp % 2, space]).astype(jnp.int32)

    pack, up_rows, down_rows = prep(live, features, cotangent, kernel_map, send_up, send_down, map_rows)
    lower = passed_along(up_rows, "space", 1)
    upper = passed_along(down_rows, "space", -1)
    packs = [pack] + [swap(pack, "dp", 2 * m) for m in range(1, groups)]
    lowers = [lower] + [swap(lower, "dp", 2 * m) for m in range(1, groups)]
    uppers = [upper] + [swap(upper, "dp", 2 * m) for m in range(1, groups)]

    out_features, own_grad, low_grad, high_grad = own(live, pack, lower, upper, kernel_map, weights)
    back_up = passed_along(low_grad, "space", -1)
    back_down = passed_along(high_grad, "space", 1)
    grad_features = final(live, own_grad, back_up, back_down, send_up, send_down)

    keep, send = wgrad(place, packs, lowers, uppers, count, rows)
    mine = blocks(place, keep, swap(send, "dp", 1), parts)
    total = mine[0]
    for m in range(1, parts):
        total = total + swap(mine[m], "space", m)
    scale = 1.0 / math.sqrt(rows * lax.axis_size("dp") * parts)
    rounded = (total * scale).astype(BF)
    line = jnp.stack([rounded] + [swap(rounded, "space", m) for m in range(1, parts)])
    pieces = []
    for m in range(groups):
        piece = swap(line, "dp", 2 * m) if m else line
        pieces += [piece, swap(piece, "dp", 1)]
    put = assemble if rounded.shape[1] % 16 == 0 else assemble_plain
    grad_weights = put(place, pieces, offsets, width)
    return (out_features, grad_features, grad_weights)


def solution(mesh):
    placed = (
        P(("dp", "space"), None),
        P(),
        P(("dp", "space"), None),
        P(None, ("dp", "space")),
        P(("dp", "space")),
        P(("dp", "space"), None),
        P(("dp", "space"), None),
    )
    return jax.shard_map(
        shards,
        mesh=mesh,
        in_specs=placed,
        out_specs=(P(("dp", "space"), None), P(("dp", "space"), None), P()),
        check_vma=False,
    )
```

```python
import functools
import math

import jax
import jax.numpy as jnp
from jax import lax
from jax.experimental import pallas as pl
from jax.experimental.pallas import tpu as pltpu
from jax.sharding import PartitionSpec as P

BF = jnp.bfloat16
F32 = jnp.float32
VMEM_LIMIT = 48 * 1024 * 1024
VMEM = pl.BlockSpec(memory_space=pltpu.VMEM)
SMEM = pl.BlockSpec(memory_space=pltpu.SMEM)
ANY = pl.BlockSpec(memory_space=pl.ANY)
HBM = pl.BlockSpec(memory_space=pltpu.HBM)
TOKEN = jax.ShapeDtypeStruct((8, 128), F32)


def params():
    return pltpu.CompilerParams(vmem_limit_bytes=VMEM_LIMIT)


def dot(a, b):
    return jnp.dot(a, b, preferred_element_type=F32)


def split(value, terms):
    parts = []
    for _ in range(terms):
        part = value.astype(BF)
        parts.append(part)
        value = value - part.astype(F32)
    return parts


def prep_kernel(live_ref, x_hbm, dy_hbm, map_hbm, up_hbm, down_hbm, pack_ref, up_rows_ref, down_rows_ref, *scratch):
    x_ref, dy_ref, map_ref, up_ref, down_ref, map_scr, sems = scratch
    sources = (x_hbm, up_hbm, down_hbm, dy_hbm, map_hbm)
    targets = (x_ref, up_ref, down_ref, dy_ref, map_ref)
    copies = [pltpu.make_async_copy(a, b, sems.at[i]) for i, (a, b) in enumerate(zip(sources, targets))]
    for copy in copies:
        copy.start()
    rows, width = x_ref.shape
    halo = up_ref.shape[1]
    keep = lax.broadcasted_iota(jnp.int32, (rows, width), 0) < live_ref[0]
    iota = lax.broadcasted_iota(jnp.int32, (rows, halo), 0)
    for copy in copies[:3]:
        copy.wait()
    x_live = jnp.where(keep, x_ref[...].astype(F32), 0.0).astype(BF)
    pack_ref[0:rows] = x_live
    for index_ref, picked_ref in ((up_ref, up_rows_ref), (down_ref, down_rows_ref)):
        chosen = (iota == index_ref[...]).astype(F32).astype(BF)
        picked_ref[...] = lax.dot_general(chosen, x_live, (((0,), (0,)), ((), ())), preferred_element_type=F32).astype(BF)
    for copy in copies[3:]:
        copy.wait()
    pack_ref[rows : 2 * rows] = jnp.where(keep, dy_ref[...].astype(F32), 0.0).astype(BF)
    map_scr[...] = jnp.full(map_scr.shape, rows + 2 * halo, jnp.int32)
    map_scr[0 : map_ref.shape[0]] = map_ref[...]
    slots = map_scr[...]
    pack_ref[2 * rows :] = jnp.where(slots > 256, 256 - slots, slots).astype(F32).astype(BF)


def prep(live, features, cotangent, kernel_map, send_up, send_down, map_rows):
    rows, width = features.shape
    halo = send_up.shape[1]
    return pl.pallas_call(
        prep_kernel,
        out_shape=(
            jax.ShapeDtypeStruct((2 * rows + map_rows, width), BF),
            jax.ShapeDtypeStruct((halo, width), BF),
            jax.ShapeDtypeStruct((halo, width), BF),
        ),
        in_specs=[SMEM] + [HBM] * 5,
        out_specs=(VMEM,) * 3,
        scratch_shapes=[
            pltpu.VMEM((rows, width), BF),
            pltpu.VMEM((rows, width), BF),
            pltpu.VMEM(kernel_map.shape, jnp.int32),
            pltpu.VMEM(send_up.shape, jnp.int32),
            pltpu.VMEM(send_down.shape, jnp.int32),
            pltpu.VMEM((map_rows, rows), jnp.int32),
            pltpu.SemaphoreType.DMA((5,)),
        ],
        compiler_params=params(),
        name="prep",
    )(live, features, cotangent, kernel_map, send_up, send_down)


def decoded(code):
    code = code.astype(F32).astype(jnp.int32)
    return jnp.where(code < 0, 256 - code, code)


def backward_kernel(pack_ref, w_ref, after_ref, own_ref, low_ref, high_ref, token_ref, maps, grad_acc, chosen, terms):
    step = pl.program_id(0)
    offsets = w_ref.shape[0]
    rows, width = own_ref.shape
    halo = low_ref.shape[0]
    slots = grad_acc.shape[0]

    @pl.when(step == 0)
    def _():
        maps[...] = decoded(pack_ref[2 * rows :])
        grad_acc[...] = jnp.zeros_like(grad_acc)

    dy = pack_ref[rows : 2 * rows]
    slot_down = lax.broadcasted_iota(jnp.int32, (slots, rows), 0)
    for i in range(offsets):
        row = maps[pl.ds(step * offsets + i, 1), :]
        chosen[:, i * rows : (i + 1) * rows] = (slot_down == row).astype(F32).astype(BF)
        back = lax.dot_general(dy, w_ref[i], (((1,), (1,)), ((), ())), preferred_element_type=F32)
        for t, part in enumerate(split(back, 2)):
            terms[t, i * rows : (i + 1) * rows] = part
    grad_acc[...] += dot(chosen[...], terms[0]) + dot(chosen[...], terms[1])

    @pl.when(step == pl.num_programs(0) - 1)
    def _():
        own_ref[...] = grad_acc[0:rows]
        low_ref[...] = grad_acc[rows : rows + halo]
        high_ref[...] = grad_acc[rows + halo :]
        token_ref[...] = jnp.zeros_like(token_ref)


def whole(shape):
    return pl.BlockSpec(shape, lambda k: (0,) * len(shape))


def backward(pack, weights, rows, halo, after):
    offsets, width, _ = weights.shape
    slots = rows + 2 * halo
    per_step = 3 if offsets % 3 == 0 else 1
    return pl.pallas_call(
        backward_kernel,
        grid=(offsets // per_step,),
        out_shape=(
            jax.ShapeDtypeStruct((rows, width), F32),
            jax.ShapeDtypeStruct((halo, width), F32),
            jax.ShapeDtypeStruct((halo, width), F32),
            TOKEN,
        ),
        in_specs=[whole(pack.shape), pl.BlockSpec((per_step, width, width), lambda k: (k, 0, 0)), ANY],
        out_specs=(whole((rows, width)), whole((halo, width)), whole((halo, width)), whole(TOKEN.shape)),
        scratch_shapes=[
            pltpu.VMEM((pack.shape[0] - 2 * rows, rows), jnp.int32),
            pltpu.VMEM((slots, width), F32),
            pltpu.VMEM((slots, per_step * rows), BF),
            pltpu.VMEM((2, per_step * rows, width), BF),
        ],
        compiler_params=params(),
        cost_estimate=pl.CostEstimate(flops=8_000_000_000, bytes_accessed=4_500_000, transcendentals=0),
        name="backward",
    )(pack, weights, after)


def forward_kernel(live_ref, pack_ref, halo_ref, w_ref, after_ref, out_ref, token_ref, table, maps, out_acc, picked):
    step = pl.program_id(0)
    offsets = w_ref.shape[0]
    rows, width = out_ref.shape
    slots = table.shape[0]

    @pl.when(step == 0)
    def _():
        maps[...] = decoded(pack_ref[2 * rows :])
        table[0:rows] = pack_ref[0:rows]
        table[rows:] = halo_ref[...]
        out_acc[...] = jnp.zeros_like(out_acc)

    along = lax.broadcasted_iota(jnp.int32, (rows, 128), 1)
    for i in range(offsets):
        row = maps[pl.ds(step * offsets + i, 1), :]
        column = jnp.transpose(jnp.broadcast_to(row, (128, rows)))
        chosen = jnp.concatenate(
            [(along + 128 * b == column).astype(F32).astype(BF) for b in range(slots // 128)], axis=1
        )
        picked[:, i * width : (i + 1) * width] = dot(chosen, table[...]).astype(BF)
    out_acc[...] += dot(picked[...], w_ref[...].reshape(offsets * width, width))

    @pl.when(step == pl.num_programs(0) - 1)
    def _():
        keep = lax.broadcasted_iota(jnp.int32, (rows, width), 0) < live_ref[0]
        out_ref[...] = jnp.where(keep, out_acc[...], 0.0).astype(BF)
        token_ref[...] = jnp.zeros_like(token_ref)


def forward(live, pack, halo_rows, weights, rows, after):
    offsets, width, _ = weights.shape
    slots = rows + halo_rows.shape[0]
    per_step = 3 if offsets % 3 == 0 else 1
    return pl.pallas_call(
        forward_kernel,
        grid=(offsets // per_step,),
        out_shape=(jax.ShapeDtypeStruct((rows, width), BF), TOKEN),
        in_specs=[
            SMEM,
            whole(pack.shape),
            whole(halo_rows.shape),
            pl.BlockSpec((per_step, width, width), lambda k: (k, 0, 0)),
            ANY,
        ],
        out_specs=(whole((rows, width)), whole(TOKEN.shape)),
        scratch_shapes=[
            pltpu.VMEM((slots, width), BF),
            pltpu.VMEM((pack.shape[0] - 2 * rows, rows), jnp.int32),
            pltpu.VMEM((rows, width), F32),
            pltpu.VMEM((rows, per_step * width), BF),
        ],
        compiler_params=params(),
        cost_estimate=pl.CostEstimate(flops=5_000_000_000, bytes_accessed=4_500_000, transcendentals=0),
        name="forward",
    )(live, pack, halo_rows, weights, after)


def wgrad_kernel(sources, place_ref, *refs):
    packs, halos = refs[:sources], refs[sources : 2 * sources]
    keep_ref, send_ref, table_t, dys, maps, picked = refs[2 * sources :]
    count, half, width = keep_ref.shape
    rows = dys.shape[0] // sources
    slots = rows + halos[0].shape[0]
    for s in range(sources):
        table_t[:, s * slots : s * slots + rows] = jnp.transpose(packs[s][0:rows])
        table_t[:, s * slots + rows : (s + 1) * slots] = jnp.transpose(halos[s][...])
        dys[s * rows : (s + 1) * rows] = packs[s][rows : 2 * rows]
        maps[s] = decoded(packs[s][2 * rows :])
    first = place_ref[0] * count
    core = place_ref[1]
    slot_down = lax.broadcasted_iota(jnp.int32, (slots, rows), 0)

    def offset(j, carry):
        for s in range(sources):
            row = maps[s, pl.ds(first + j, 1), :]
            chosen = (slot_down == row).astype(F32).astype(BF)
            picked[:, s * rows : (s + 1) * rows] = dot(table_t[:, s * slots : (s + 1) * slots], chosen).astype(BF)
        send_ref[j] = dot(picked[pl.ds(pl.multiple_of((1 - core) * half, half), half), :], dys[...])
        keep_ref[j] = dot(picked[pl.ds(pl.multiple_of(core * half, half), half), :], dys[...])
        return carry

    lax.fori_loop(0, count, offset, 0)


def wgrad(place, packs, halos, count, rows):
    sources = len(packs)
    width = packs[0].shape[1]
    slots = rows + halos[0].shape[0]
    shape = jax.ShapeDtypeStruct((count, width // 2, width), F32)
    return pl.pallas_call(
        functools.partial(wgrad_kernel, sources),
        out_shape=(shape, shape),
        in_specs=[SMEM] + [VMEM] * (2 * sources),
        out_specs=(VMEM, VMEM),
        scratch_shapes=[
            pltpu.VMEM((width, sources * slots), BF),
            pltpu.VMEM((sources * rows, width), BF),
            pltpu.VMEM((sources, packs[0].shape[0] - 2 * rows, rows), jnp.int32),
            pltpu.VMEM((width, sources * rows), BF),
        ],
        compiler_params=params(),
        cost_estimate=pl.CostEstimate(flops=4_000_000_000, bytes_accessed=4_500_000, transcendentals=0),
        name="wgrad",
    )(place, *packs, *halos)


def blocks_kernel(place_ref, keep_ref, got_ref, *block_refs):
    block = block_refs[0].shape[1]
    for m, block_ref in enumerate(block_refs):
        at = pl.ds(pl.multiple_of((place_ref[2] ^ m) * block, block), block)
        block_ref[...] = keep_ref[:, at, :] + got_ref[:, at, :]


def blocks(place, keep, got, parts):
    count, half, width = keep.shape
    shape = jax.ShapeDtypeStruct((count, half // parts, width), F32)
    return pl.pallas_call(
        blocks_kernel,
        out_shape=(shape,) * parts,
        in_specs=[SMEM, VMEM, VMEM],
        out_specs=(VMEM,) * parts,
        compiler_params=params(),
        name="blocks",
    )(place, keep, got)


def total_kernel(scale, *refs):
    *terms, _, out_ref = refs
    total = terms[0][...]
    for term in terms[1:]:
        total = total + term[...]
    out_ref[...] = (total * scale).astype(BF)


def scaled_total(terms, scale, after):
    return pl.pallas_call(
        functools.partial(total_kernel, scale),
        out_shape=jax.ShapeDtypeStruct(terms[0].shape, BF),
        in_specs=[VMEM] * len(terms) + [ANY],
        out_specs=VMEM,
        compiler_params=params(),
        name="total",
    )(*terms, after)


def final_kernel(live_ref, own_ref, back_up_ref, back_down_ref, up_ref, down_ref, after_ref, out_ref, token_ref):
    rows, width = own_ref.shape
    halo = up_ref.shape[1]
    total = own_ref[...]
    iota = lax.broadcasted_iota(jnp.int32, (rows, halo), 0)
    for index_ref, back_ref in ((up_ref, back_up_ref), (down_ref, back_down_ref)):
        chosen = (iota == index_ref[...]).astype(F32).astype(BF)
        for part in split(back_ref[...], 3):
            total = total + dot(chosen, part)
    keep = lax.broadcasted_iota(jnp.int32, (rows, width), 0) < live_ref[0]
    out_ref[...] = jnp.where(keep, total, 0.0).astype(BF)
    token_ref[...] = jnp.zeros_like(token_ref)


def final(live, own_grad, back_up, back_down, send_up, send_down, after):
    return pl.pallas_call(
        final_kernel,
        out_shape=(jax.ShapeDtypeStruct(own_grad.shape, BF), TOKEN),
        in_specs=[SMEM] + [VMEM] * 5 + [ANY],
        out_specs=(VMEM, VMEM),
        compiler_params=params(),
        name="final",
    )(live, own_grad, back_up, back_down, send_up, send_down, after)


def assemble_kernel(groups, place_ref, *refs):
    sources, out_ref, sems = refs[: 2 * groups], refs[-2], refs[-1]
    offsets = out_ref.shape[0]
    parts, count, block, _ = sources[0].shape
    short = offsets - (groups - 1) * count

    def copies(index, part):
        m, o = index // 2, index % 2
        group = place_ref[0] ^ m
        row = ((place_ref[1] ^ o) * parts + (place_ref[2] ^ part)) * block
        row = pl.ds(pl.multiple_of(row, block), block)
        source = sources[index].at[part]
        sem = sems.at[index, part]
        yield group == group, pltpu.make_async_copy(
            source.at[0:short], out_ref.at[pl.ds(group * count, short), row], sem.at[0]
        )
        if short < count:
            yield group < groups - 1, pltpu.make_async_copy(
                source.at[short:count], out_ref.at[pl.ds(group * count + short, count - short), row], sem.at[1]
            )

    for act in ("start", "wait"):
        for index in range(2 * groups):
            for part in range(parts):
                for n, (wanted, copy) in enumerate(copies(index, part)):
                    if n == 0:
                        getattr(copy, act)()
                    else:
                        pl.when(wanted)(getattr(copy, act))


def assemble(place, pieces, offsets, width, after):
    parts = pieces[0].shape[0]
    return pl.pallas_call(
        functools.partial(assemble_kernel, len(pieces) // 2),
        out_shape=jax.ShapeDtypeStruct((offsets, width, width), BF),
        in_specs=[SMEM] + [ANY] * (len(pieces) + len(after)),
        out_specs=ANY,
        scratch_shapes=[pltpu.SemaphoreType.DMA((len(pieces), parts, 2))],
        compiler_params=params(),
        name="assemble",
    )(place, *pieces, *after)


def assemble_plain(place, pieces, offsets, width, after):
    parts, count, block, _ = pieces[0].shape
    groups = len(pieces) // 2
    whole = jnp.zeros((groups * count, width, width), BF)
    for index, piece in enumerate(pieces):
        for part in range(parts):
            row = ((place[1] ^ (index % 2)) * parts + (place[2] ^ part)) * block
            whole = lax.dynamic_update_slice(whole, piece[part], ((place[0] ^ (index // 2)) * count, row, 0))
    return whole[:offsets]


def swap(value, axis, mask):
    return lax.ppermute(value, axis, [(i, i ^ mask) for i in range(lax.axis_size(axis))])


def passed_along(value, axis, steps):
    count = lax.axis_size(axis)
    return lax.ppermute(value, axis, [(i, i + steps) for i in range(max(0, -steps), min(count, count - steps))])


def shards(features, weights, cotangent, kernel_map, live, send_up, send_down):
    rows, width = features.shape
    offsets = weights.shape[0]
    groups = lax.axis_size("dp") // 2
    parts = lax.axis_size("space")
    count = -(-offsets // groups)
    map_rows = -(-(groups * count) // 16) * 16
    dp, space = lax.axis_index("dp"), lax.axis_index("space")
    place = jnp.stack([dp // 2, dp % 2, space]).astype(jnp.int32)

    pack, up_rows, down_rows = prep(live, features, cotangent, kernel_map, send_up, send_down, map_rows)
    lower = passed_along(up_rows, "space", 1)
    upper = passed_along(down_rows, "space", -1)
    packs = [pack] + [swap(pack, "dp", 2 * m) for m in range(1, groups)]
    halo_rows = jnp.concatenate([lower, upper])
    halos = [halo_rows] + [swap(halo_rows, "dp", 2 * m) for m in range(1, groups)]

    keep, send = wgrad(place, packs, halos, count, rows)
    mine = blocks(place, keep, swap(send, "dp", 1), parts)
    got = [swap(mine[m], "space", m) for m in range(1, parts)]
    own_grad, low_grad, high_grad, token = backward(pack, weights, rows, send_up.shape[1], mine[0])
    back_up = passed_along(low_grad, "space", -1)
    back_down = passed_along(high_grad, "space", 1)
    scale = 1.0 / math.sqrt(rows * lax.axis_size("dp") * parts)
    rounded = scaled_total([mine[0], *got], scale, token)
    line = jnp.stack([rounded] + [swap(rounded, "space", m) for m in range(1, parts)])
    out_features, out_token = forward(live, pack, halo_rows, weights, rows, line)
    grad_features, grad_token = final(live, own_grad, back_up, back_down, send_up, send_down, line)
    pieces = []
    for m in range(groups):
        piece = swap(line, "dp", 2 * m) if m else line
        pieces += [piece, swap(piece, "dp", 1)]
    put = assemble if rounded.shape[1] % 16 == 0 else assemble_plain
    grad_weights = put(place, pieces, offsets, width, (out_token, grad_token))
    return (out_features, grad_features, grad_weights)


def solution(mesh):
    placed = (
        P(("dp", "space"), None),
        P(),
        P(("dp", "space"), None),
        P(None, ("dp", "space")),
        P(("dp", "space")),
        P(("dp", "space"), None),
        P(("dp", "space"), None),
    )
    return jax.shard_map(
        shards,
        mesh=mesh,
        in_specs=placed,
        out_specs=(P(("dp", "space"), None), P(("dp", "space"), None), P()),
        check_vma=False,
    )
```

```python
import functools
import math

import jax
import jax.numpy as jnp
from jax import lax
from jax.experimental import pallas as pl
from jax.experimental.pallas import tpu as pltpu
from jax.sharding import PartitionSpec as P

BF = jnp.bfloat16
F32 = jnp.float32
VMEM_LIMIT = 32 * 1024 * 1024
PREP_LIMIT = 60 * 1024 * 1024
VMEM = pl.BlockSpec(memory_space=pltpu.VMEM)
SMEM = pl.BlockSpec(memory_space=pltpu.SMEM)
ANY = pl.BlockSpec(memory_space=pl.ANY)
HBM = pl.BlockSpec(memory_space=pltpu.HBM)
TOKEN = jax.ShapeDtypeStruct((8, 128), F32)


def params(limit=VMEM_LIMIT):
    return pltpu.CompilerParams(vmem_limit_bytes=limit)


def cost():
    return pl.CostEstimate(flops=100_000_000, bytes_accessed=100_000, transcendentals=0)


def dot(a, b):
    return jnp.dot(a, b, preferred_element_type=F32)


def split(value, terms):
    parts = []
    for _ in range(terms):
        part = value.astype(BF)
        parts.append(part)
        value = value - part.astype(F32)
    return parts


def prep_kernel(live_ref, x_hbm, dy_hbm, map_hbm, up_hbm, down_hbm, pack_ref, *scratch):
    x_ref, dy_ref, map_ref, up_ref, down_ref, map_scr, sems = scratch
    sources = (x_hbm, dy_hbm, map_hbm, up_hbm, down_hbm)
    targets = (x_ref, dy_ref, map_ref, up_ref, down_ref)
    copies = [pltpu.make_async_copy(a, b, sems.at[i]) for i, (a, b) in enumerate(zip(sources, targets))]
    for copy in copies:
        copy.start()
    rows, width = x_ref.shape
    offsets = map_ref.shape[0]
    halo = up_ref.shape[1]
    keep = lax.broadcasted_iota(jnp.int32, (rows, width), 0) < live_ref[0]
    map_scr[...] = jnp.full(map_scr.shape, rows + 2 * halo, jnp.int32)
    for copy in copies:
        copy.wait()
    pack_ref[0:rows] = jnp.where(keep, x_ref[...].astype(F32), 0.0).astype(BF)
    pack_ref[rows : 2 * rows] = jnp.where(keep, dy_ref[...].astype(F32), 0.0).astype(BF)
    map_scr[0:offsets] = map_ref[...]
    map_scr[map_scr.shape[0] - 1 :, 0:halo] = up_ref[...]
    map_scr[map_scr.shape[0] - 1 :, halo : 2 * halo] = down_ref[...]
    slots = map_scr[...]
    pack_ref[2 * rows :] = jnp.where(slots > 256, 256 - slots, slots).astype(F32).astype(BF)


def prep(live, features, cotangent, kernel_map, send_up, send_down, map_rows):
    rows, width = features.shape
    return pl.pallas_call(
        prep_kernel,
        out_shape=jax.ShapeDtypeStruct((2 * rows + map_rows, width), BF),
        in_specs=[SMEM] + [HBM] * 5,
        out_specs=VMEM,
        scratch_shapes=[
            pltpu.VMEM((rows, width), BF),
            pltpu.VMEM((rows, width), BF),
            pltpu.VMEM(kernel_map.shape, jnp.int32),
            pltpu.VMEM(send_up.shape, jnp.int32),
            pltpu.VMEM(send_down.shape, jnp.int32),
            pltpu.VMEM((map_rows, rows), jnp.int32),
            pltpu.SemaphoreType.DMA((5,)),
        ],
        compiler_params=params(PREP_LIMIT),
        name="prep",
    )(live, features, cotangent, kernel_map, send_up, send_down)


def pick_kernel(rows, *refs):
    *packs, up_ref, down_ref = refs
    halo = up_ref.shape[0] // len(packs)
    iota = lax.broadcasted_iota(jnp.int32, (rows, 2 * halo), 0)
    for s, pack in enumerate(packs):
        sent = pack[2 * rows :].astype(F32).astype(jnp.int32)[-1:, 0 : 2 * halo]
        chosen = (iota == sent).astype(F32).astype(BF)
        picked = lax.dot_general(chosen, pack[0:rows], (((0,), (0,)), ((), ())), preferred_element_type=F32)
        up_ref[s * halo : (s + 1) * halo] = picked[0:halo].astype(BF)
        down_ref[s * halo : (s + 1) * halo] = picked[halo:].astype(BF)


def pick(packs, rows, halo, after):
    shape = jax.ShapeDtypeStruct((len(packs) * halo, packs[0].shape[1]), BF)
    return pl.pallas_call(
        functools.partial(pick_kernel_after, rows),
        out_shape=(shape, shape),
        in_specs=[VMEM] * len(packs) + [ANY],
        out_specs=(VMEM, VMEM),
        compiler_params=params(),
        cost_estimate=cost(),
        name="pick",
    )(*packs, after)


def pick_kernel_after(rows, *refs):
    pick_kernel(rows, *refs[:-3], *refs[-2:])


def decoded(code):
    code = code.astype(F32).astype(jnp.int32)
    return jnp.where(code < 0, 256 - code, code)


def backward_kernel(start, end, pack_ref, w_ref, before_ref, *refs):
    outs, (maps, grad_acc, chosen, terms) = refs[:-4], refs[-4:]
    step = pl.program_id(0)
    offsets, width, _ = w_ref.shape
    slots = grad_acc.shape[0]
    rows = chosen.shape[1] // offsets

    @pl.when(step == 0)
    def _():
        maps[...] = decoded(pack_ref[2 * rows :])
        grad_acc[...] = before_ref[...] if start else jnp.zeros_like(grad_acc)

    dy = pack_ref[rows : 2 * rows]
    slot_down = lax.broadcasted_iota(jnp.int32, (slots, rows), 0)
    for i in range(offsets):
        row = maps[pl.ds((start + step) * offsets + i, 1), :]
        chosen[:, i * rows : (i + 1) * rows] = (slot_down == row).astype(F32).astype(BF)
        back = lax.dot_general(dy, w_ref[i], (((1,), (1,)), ((), ())), preferred_element_type=F32)
        for t, part in enumerate(split(back, 2)):
            terms[t, i * rows : (i + 1) * rows] = part
    grad_acc[...] += dot(chosen[...], terms[0]) + dot(chosen[...], terms[1])

    @pl.when(step == end - start - 1)
    def _():
        at = 0
        for out in outs:
            out[...] = grad_acc[at : at + out.shape[0]]
            at += out.shape[0]


def whole(shape):
    return pl.BlockSpec(shape, lambda k: (0,) * len(shape))


def backward(pack, weights, rows, halo, start, end, per_step, before):
    offsets, width, _ = weights.shape
    slots = rows + 2 * halo
    sizes = (rows, halo, halo) if end * per_step == offsets else (slots,)
    return pl.pallas_call(
        functools.partial(backward_kernel, start, end),
        grid=(end - start,),
        out_shape=tuple(jax.ShapeDtypeStruct((n, width), F32) for n in sizes),
        in_specs=[
            whole(pack.shape),
            pl.BlockSpec((per_step, width, width), lambda k: (start + k, 0, 0)),
            whole(before.shape) if start else ANY,
        ],
        out_specs=tuple(whole((n, width)) for n in sizes),
        scratch_shapes=[
            pltpu.VMEM((pack.shape[0] - 2 * rows, rows), jnp.int32),
            pltpu.VMEM((slots, width), F32),
            pltpu.VMEM((slots, per_step * rows), BF),
            pltpu.VMEM((2, per_step * rows, width), BF),
        ],
        compiler_params=params(),
        cost_estimate=cost(),
        name="backward",
    )(pack, weights, before)


def forward_kernel(live_ref, pack_ref, lower_ref, upper_ref, w_ref, after_ref, out_ref, token_ref, table, maps, out_acc, picked):
    step = pl.program_id(0)
    offsets = w_ref.shape[0]
    rows, width = out_ref.shape
    slots = table.shape[0]

    @pl.when(step == 0)
    def _():
        maps[...] = decoded(pack_ref[2 * rows :])
        table[0:rows] = pack_ref[0:rows]
        halo = (slots - rows) // 2
        table[rows : rows + halo] = lower_ref[0:halo]
        table[rows + halo :] = upper_ref[0:halo]
        out_acc[...] = jnp.zeros_like(out_acc)

    along = lax.broadcasted_iota(jnp.int32, (rows, 128), 1)
    for i in range(offsets):
        row = maps[pl.ds(step * offsets + i, 1), :]
        column = jnp.transpose(jnp.broadcast_to(row, (128, rows)))
        chosen = jnp.concatenate(
            [(along + 128 * b == column).astype(F32).astype(BF) for b in range(slots // 128)], axis=1
        )
        picked[:, i * width : (i + 1) * width] = dot(chosen, table[...]).astype(BF)
    out_acc[...] += dot(picked[...], w_ref[...].reshape(offsets * width, width))

    @pl.when(step == pl.num_programs(0) - 1)
    def _():
        keep = lax.broadcasted_iota(jnp.int32, (rows, width), 0) < live_ref[0]
        out_ref[...] = jnp.where(keep, out_acc[...], 0.0).astype(BF)
        token_ref[...] = jnp.zeros_like(token_ref)


def forward(live, pack, lower, upper, weights, rows, halo, after):
    offsets, width, _ = weights.shape
    slots = rows + 2 * halo
    per_step = 3 if offsets % 3 == 0 else 1
    return pl.pallas_call(
        forward_kernel,
        grid=(offsets // per_step,),
        out_shape=(jax.ShapeDtypeStruct((rows, width), BF), TOKEN),
        in_specs=[
            SMEM,
            whole(pack.shape),
            whole(lower.shape),
            whole(upper.shape),
            pl.BlockSpec((per_step, width, width), lambda k: (k, 0, 0)),
            ANY,
        ],
        out_specs=(whole((rows, width)), whole(TOKEN.shape)),
        scratch_shapes=[
            pltpu.VMEM((slots, width), BF),
            pltpu.VMEM((pack.shape[0] - 2 * rows, rows), jnp.int32),
            pltpu.VMEM((rows, width), F32),
            pltpu.VMEM((rows, per_step * width), BF),
        ],
        compiler_params=params(),
        cost_estimate=cost(),
        name="forward",
    )(live, pack, lower, upper, weights, after)


def chosen_slots(maps, s, at, low, high, rows):
    iota = lax.broadcasted_iota(jnp.int32, (high - low, rows), 0) + low
    return (iota == maps[s, pl.ds(at, 1), :]).astype(F32).astype(BF)


def wgrad_own_kernel(sources, place_ref, *refs):
    packs = refs[:sources]
    picked_ref, dys, maps, tables = refs[sources + 1 :]
    count, width, _ = picked_ref.shape
    rows = dys.shape[0] // sources
    for s in range(sources):
        tables[:, s * rows : (s + 1) * rows] = jnp.transpose(packs[s][0:rows])
        dys[s * rows : (s + 1) * rows] = packs[s][rows : 2 * rows]
        maps[s] = decoded(packs[s][2 * rows :])

    def offset(j, carry):
        for s in range(sources):
            chosen = chosen_slots(maps, s, place_ref[0] * count + j, 0, rows, rows)
            picked_ref[j, :, s * rows : (s + 1) * rows] = dot(tables[:, s * rows : (s + 1) * rows], chosen).astype(BF)
        return carry

    lax.fori_loop(0, count, offset, 0)


def wgrad_own(place, packs, count, rows, after):
    sources, width = len(packs), packs[0].shape[1]
    return pl.pallas_call(
        functools.partial(wgrad_own_kernel, sources),
        out_shape=(
            jax.ShapeDtypeStruct((count, width, sources * rows), BF),
            jax.ShapeDtypeStruct((sources * rows, width), BF),
            jax.ShapeDtypeStruct((sources, packs[0].shape[0] - 2 * rows, rows), jnp.int32),
        ),
        in_specs=[SMEM] + [VMEM] * sources + [ANY],
        out_specs=(VMEM, VMEM, VMEM),
        scratch_shapes=[pltpu.VMEM((width, sources * rows), BF)],
        compiler_params=params(),
        cost_estimate=cost(),
        name="wgrad_own",
    )(place, *packs, after)


def wgrad_kernel(place_ref, picked_ref, dys, maps, lower_ref, upper_ref, keep_ref, send_ref, tables, picked):
    count, half, width = keep_ref.shape
    sources, _, rows = maps.shape
    halo = lower_ref.shape[0] // sources
    core = place_ref[1]
    for s in range(sources):
        both = jnp.concatenate([ref[s * halo : (s + 1) * halo].astype(F32) for ref in (lower_ref, upper_ref)], axis=0)
        tables[:, s * 2 * halo : (s + 1) * 2 * halo] = jnp.transpose(both).astype(BF)

    def offset(j, carry):
        for s in range(sources):
            chosen = chosen_slots(maps, s, place_ref[0] * count + j, rows, rows + 2 * halo, rows)
            far = dot(tables[:, s * 2 * halo : (s + 1) * 2 * halo], chosen)
            near = picked_ref[j, :, s * rows : (s + 1) * rows].astype(F32)
            picked[:, s * rows : (s + 1) * rows] = (far + near).astype(BF)
        send_ref[j] = dot(picked[pl.ds(pl.multiple_of((1 - core) * half, half), half), :], dys[...])
        keep_ref[j] = dot(picked[pl.ds(pl.multiple_of(core * half, half), half), :], dys[...])
        return carry

    lax.fori_loop(0, count, offset, 0)


def wgrad(place, picked, dys, maps, lower, upper):
    count, width, columns = picked.shape
    sources = maps.shape[0]
    shape = jax.ShapeDtypeStruct((count, width // 2, width), F32)
    return pl.pallas_call(
        wgrad_kernel,
        out_shape=(shape, shape),
        in_specs=[SMEM] + [VMEM] * 5,
        out_specs=(VMEM, VMEM),
        scratch_shapes=[
            pltpu.VMEM((width, 2 * lower.shape[0]), BF),
            pltpu.VMEM((width, columns), BF),
        ],
        compiler_params=params(),
        cost_estimate=cost(),
        name="wgrad",
    )(place, picked, dys, maps, lower, upper)


def power(exponent):
    value = jnp.ones(exponent.shape, F32)
    size = jnp.abs(exponent)
    for bit in range(7):
        factor = jnp.where(exponent < 0, 0.5 ** (1 << bit), 2.0 ** (1 << bit))
        value = value * jnp.where((size >> bit) & 1 == 1, factor, 1.0)
    return value


def blocks_kernel(place_ref, keep_ref, got_ref, mine_ref, *refs):
    coded_refs, exponents = refs[:-1], refs[-1]
    count, block, width = mine_ref.shape
    for m in range(len(coded_refs) + 1):
        at = pl.ds(pl.multiple_of((place_ref[2] ^ m) * block, block), block)
        if m == 0:
            mine_ref[...] = keep_ref[:, at, :] + got_ref[:, at, :]
            continue
        exponents[...] = jnp.zeros_like(exponents)
        for j in range(count):
            value = keep_ref[j, at, :] + got_ref[j, at, :]
            largest = jnp.max(jnp.abs(value), axis=0, keepdims=True)
            exponent = jnp.ceil(jnp.log(jnp.maximum(largest, 2.0**-100)) * (1.0 / math.log(2.0)))
            exponent = jnp.clip(exponent, -100.0, 100.0).astype(jnp.int32) - 15
            exponents[j : j + 1, :] = exponent
            scaled = jnp.round(jnp.clip(value * power(-exponent), -32767.0, 32767.0))
            coded_refs[m - 1][j * block : (j + 1) * block] = scaled.astype(jnp.int32).astype(jnp.int16)
        coded_refs[m - 1][count * block :] = exponents[...].astype(jnp.int16)


def blocks(place, keep, got, parts):
    count, half, width = keep.shape
    block = half // parts
    extra = -(-count // 16) * 16
    return pl.pallas_call(
        blocks_kernel,
        out_shape=(
            jax.ShapeDtypeStruct((count, block, width), F32),
            *(jax.ShapeDtypeStruct((count * block + extra, width), jnp.int16),) * (parts - 1),
        ),
        in_specs=[SMEM, VMEM, VMEM],
        out_specs=(VMEM,) * parts,
        scratch_shapes=[pltpu.VMEM((extra, width), jnp.int32)],
        compiler_params=params(),
        cost_estimate=cost(),
        name="blocks",
    )(place, keep, got)


def total_kernel(scale, mine_ref, *refs):
    *coded_refs, _, _, out_ref = refs
    count, block, width = mine_ref.shape
    powers = [power(ref[count * block :].astype(jnp.int32)) for ref in coded_refs]
    for j in range(count):
        total = mine_ref[j]
        for ref, factor in zip(coded_refs, powers):
            value = ref[j * block : (j + 1) * block].astype(jnp.int32).astype(F32)
            total = total + value * factor[j : j + 1, :]
        out_ref[j] = (total * scale).astype(BF)


def scaled_total(mine, coded, scale, after):
    return pl.pallas_call(
        functools.partial(total_kernel, scale),
        out_shape=jax.ShapeDtypeStruct(mine.shape, BF),
        in_specs=[VMEM] * (len(coded) + 1) + [ANY] * 2,
        out_specs=VMEM,
        compiler_params=params(),
        cost_estimate=cost(),
        name="total",
    )(mine, *coded, *after)


def final_kernel(live_ref, own_ref, back_up_ref, back_down_ref, up_ref, down_ref, after_ref, out_ref, token_ref):
    rows, width = own_ref.shape
    halo = up_ref.shape[1]
    total = own_ref[...]
    iota = lax.broadcasted_iota(jnp.int32, (rows, halo), 0)
    for index_ref, back_ref in ((up_ref, back_up_ref), (down_ref, back_down_ref)):
        chosen = (iota == index_ref[...]).astype(F32).astype(BF)
        for part in split(back_ref[...], 3):
            total = total + dot(chosen, part)
    keep = lax.broadcasted_iota(jnp.int32, (rows, width), 0) < live_ref[0]
    out_ref[...] = jnp.where(keep, total, 0.0).astype(BF)
    token_ref[...] = jnp.zeros_like(token_ref)


def final(live, own_grad, back_up, back_down, send_up, send_down, after):
    return pl.pallas_call(
        final_kernel,
        out_shape=(jax.ShapeDtypeStruct(own_grad.shape, BF), TOKEN),
        in_specs=[SMEM] + [VMEM] * 5 + [ANY],
        out_specs=(VMEM, VMEM),
        compiler_params=params(),
        name="final",
    )(live, own_grad, back_up, back_down, send_up, send_down, after)


def line_kernel(count, *refs):
    for m in range(count):
        refs[-1][m] = refs[m][...]


def line(blocks, after):
    if len(blocks) == 1:
        return blocks[0][None]
    return pl.pallas_call(
        functools.partial(line_kernel, len(blocks)),
        out_shape=jax.ShapeDtypeStruct((len(blocks), *blocks[0].shape), BF),
        in_specs=[VMEM] * len(blocks) + [ANY] * len(after),
        out_specs=VMEM,
        compiler_params=params(),
        cost_estimate=cost(),
        name="line",
    )(*blocks, *after)


def assemble_kernel(marks, parts, groups, place_ref, *refs):
    out_ref, sems = refs[-2:]
    offsets = out_ref.shape[0]
    _, count, block, _ = refs[0].shape
    short = offsets - (groups - 1) * count

    def each(act):
        for index, (m, o, masks) in enumerate(marks):
            group = place_ref[0] ^ m
            for part, mask in enumerate(masks):
                row = pl.multiple_of(((place_ref[1] ^ o) * parts + (place_ref[2] ^ mask)) * block, block)
                source = refs[index].at[part]

                def copy(lo, hi, sem):
                    target = out_ref.at[pl.ds(group * count + lo, hi - lo), pl.ds(row, block)]
                    return pltpu.make_async_copy(source.at[lo:hi], target, sems.at[index, part, sem])

                getattr(copy(0, short, 0), act)()
                if short < count:
                    pl.when(group < groups - 1)(getattr(copy(short, count, 1), act))

    each("start")
    each("wait")


def assemble(place, pieces, marks, parts, groups, offsets, width):
    return pl.pallas_call(
        functools.partial(assemble_kernel, marks, parts, groups),
        out_shape=jax.ShapeDtypeStruct((offsets, width, width), BF),
        in_specs=[SMEM] + [ANY] * len(pieces),
        out_specs=ANY,
        scratch_shapes=[pltpu.SemaphoreType.DMA((len(pieces), parts, 2))],
        compiler_params=params(),
        name="assemble",
    )(place, *pieces)


def assemble_plain(place, pieces, marks, parts, groups, offsets, width):
    _, count, block, _ = pieces[0].shape
    total = jnp.zeros((groups * count, width, width), BF)
    for piece, (m, o, masks) in zip(pieces, marks):
        for part, mask in enumerate(masks):
            row = ((place[1] ^ o) * parts + (place[2] ^ mask)) * block
            total = lax.dynamic_update_slice(total, piece[part], ((place[0] ^ m) * count, row, 0))
    return total[:offsets]


def swap(value, axis, mask):
    return lax.ppermute(value, axis, [(i, i ^ mask) for i in range(lax.axis_size(axis))])


def passed_along(value, axis, steps):
    count = lax.axis_size(axis)
    return lax.ppermute(value, axis, [(i, i + steps) for i in range(max(0, -steps), min(count, count - steps))])


def SPLITS(parts):
    return [(0,), tuple(range(1, parts))]


def shards(features, weights, cotangent, kernel_map, live, send_up, send_down):
    rows, width = features.shape
    offsets, halo = weights.shape[0], send_up.shape[1]
    groups = lax.axis_size("dp") // 2
    parts = lax.axis_size("space")
    count = -(-offsets // groups)
    map_rows = -(-(groups * count + 1) // 16) * 16
    dp, space = lax.axis_index("dp"), lax.axis_index("space")
    place = jnp.stack([dp // 2, dp % 2, space]).astype(jnp.int32)

    pack = prep(live, features, cotangent, kernel_map, send_up, send_down, map_rows)
    packs = [pack] + [swap(pack, "dp", 2 * m) for m in range(1, groups)]
    per_step = 3 if offsets % 3 == 0 else 1
    own_grad, low_grad, high_grad = backward(pack, weights, rows, halo, 0, offsets // per_step, per_step, pack)
    back_up = passed_along(low_grad, "space", -1)
    back_down = passed_along(high_grad, "space", 1)

    up_rows, down_rows = pick(packs, rows, halo, low_grad)
    lower = passed_along(up_rows, "space", 1)
    upper = passed_along(down_rows, "space", -1)
    picked, dys, maps = wgrad_own(place, packs, count, rows, up_rows)
    keep, send = wgrad(place, picked, dys, maps, lower, upper)
    mine, *coded = blocks(place, keep, swap(send, "dp", 1), parts)
    out_features, token = forward(live, pack, lower, upper, weights, rows, halo, mine)
    grad_features, grad_token = final(live, own_grad, back_up, back_down, send_up, send_down, token)
    scale = 1.0 / math.sqrt(rows * lax.axis_size("dp") * parts)
    rounded = scaled_total(mine, [swap(block, "space", m + 1) for m, block in enumerate(coded)], scale, (token, grad_token))

    in_line = [rounded] + [swap(rounded, "space", m) for m in range(1, parts)]
    pieces, marks = [], []
    for masks in SPLITS(parts):
        lines = line([in_line[m] for m in masks], pieces[2::2][-groups:])
        for m in range(groups):
            piece = swap(lines, "dp", 2 * m) if m else lines
            pieces += [piece, swap(piece, "dp", 1)]
            marks += [(m, 0, masks), (m, 1, masks)]
    dense = rounded.shape[1] % 16 == 0 and groups * count - offsets < count
    put = assemble if dense else assemble_plain
    grad_weights = put(place, pieces, marks, parts, groups, offsets, width)
    return (out_features, grad_features, grad_weights)


def solution(mesh):
    placed = (
        P(("dp", "space"), None),
        P(),
        P(("dp", "space"), None),
        P(None, ("dp", "space")),
        P(("dp", "space")),
        P(("dp", "space"), None),
        P(("dp", "space"), None),
    )
    return jax.shard_map(
        shards,
        mesh=mesh,
        in_specs=placed,
        out_specs=(P(("dp", "space"), None), P(("dp", "space"), None), P()),
        check_vma=False,
    )
```

```python
import functools
import math

import jax
import jax.numpy as jnp
from jax import lax
from jax.experimental import pallas as pl
from jax.experimental.pallas import tpu as pltpu
from jax.sharding import PartitionSpec as P

BF = jnp.bfloat16
F32 = jnp.float32
VMEM_LIMIT = 32 * 1024 * 1024
PREP_LIMIT = 60 * 1024 * 1024
VMEM = pl.BlockSpec(memory_space=pltpu.VMEM)
SMEM = pl.BlockSpec(memory_space=pltpu.SMEM)
ANY = pl.BlockSpec(memory_space=pl.ANY)
HBM = pl.BlockSpec(memory_space=pltpu.HBM)
TOKEN = jax.ShapeDtypeStruct((8, 128), F32)


def params(limit=VMEM_LIMIT):
    return pltpu.CompilerParams(vmem_limit_bytes=limit)


def cost():
    return pl.CostEstimate(flops=100_000_000, bytes_accessed=100_000, transcendentals=0)


def dot(a, b):
    return jnp.dot(a, b, preferred_element_type=F32)


def split(value, terms):
    parts = []
    for _ in range(terms):
        part = value.astype(BF)
        parts.append(part)
        value = value - part.astype(F32)
    return parts


def prep_kernel(live_ref, x_hbm, dy_hbm, map_hbm, up_hbm, down_hbm, pack_ref, up_rows_ref, down_rows_ref, *scratch):
    x_ref, dy_ref, map_ref, up_ref, down_ref, map_scr, sems = scratch
    sources = (x_hbm, dy_hbm, map_hbm, up_hbm, down_hbm)
    targets = (x_ref, dy_ref, map_ref, up_ref, down_ref)
    copies = [pltpu.make_async_copy(a, b, sems.at[i]) for i, (a, b) in enumerate(zip(sources, targets))]
    for copy in copies:
        copy.start()
    rows, width = x_ref.shape
    offsets = map_ref.shape[0]
    halo = up_ref.shape[1]
    keep = lax.broadcasted_iota(jnp.int32, (rows, width), 0) < live_ref[0]
    map_scr[...] = jnp.full(map_scr.shape, rows + 2 * halo, jnp.int32)
    for copy in copies:
        copy.wait()
    x_live = jnp.where(keep, x_ref[...].astype(F32), 0.0).astype(BF)
    pack_ref[0:rows] = x_live
    iota = lax.broadcasted_iota(jnp.int32, (rows, halo), 0)
    for index_ref, picked_ref in ((up_ref, up_rows_ref), (down_ref, down_rows_ref)):
        chosen = (iota == index_ref[...]).astype(F32).astype(BF)
        picked_ref[...] = lax.dot_general(chosen, x_live, (((0,), (0,)), ((), ())), preferred_element_type=F32).astype(BF)
    pack_ref[rows : 2 * rows] = jnp.where(keep, dy_ref[...].astype(F32), 0.0).astype(BF)
    map_scr[0:offsets] = map_ref[...]
    slots = map_scr[...]
    pack_ref[2 * rows :] = jnp.where(slots > 256, 256 - slots, slots).astype(F32).astype(BF)


def prep(live, features, cotangent, kernel_map, send_up, send_down, map_rows):
    rows, width = features.shape
    return pl.pallas_call(
        prep_kernel,
        out_shape=(
            jax.ShapeDtypeStruct((2 * rows + map_rows, width), BF),
            jax.ShapeDtypeStruct((send_up.shape[1], width), BF),
            jax.ShapeDtypeStruct((send_up.shape[1], width), BF),
        ),
        in_specs=[SMEM] + [HBM] * 5,
        out_specs=(VMEM,) * 3,
        scratch_shapes=[
            pltpu.VMEM((rows, width), BF),
            pltpu.VMEM((rows, width), BF),
            pltpu.VMEM(kernel_map.shape, jnp.int32),
            pltpu.VMEM(send_up.shape, jnp.int32),
            pltpu.VMEM(send_down.shape, jnp.int32),
            pltpu.VMEM((map_rows, rows), jnp.int32),
            pltpu.SemaphoreType.DMA((5,)),
        ],
        compiler_params=params(PREP_LIMIT),
        name="prep",
    )(live, features, cotangent, kernel_map, send_up, send_down)


def decoded(code):
    code = code.astype(F32).astype(jnp.int32)
    return jnp.where(code < 0, 256 - code, code)


def backward_kernel(pack_ref, w_ref, after_ref, own_ref, low_ref, high_ref, token_ref, *refs):
    maps, grad_acc, chosen, terms = refs
    step = pl.program_id(0)
    offsets, width, _ = w_ref.shape
    slots = grad_acc.shape[0]
    rows = chosen.shape[1] // offsets

    @pl.when(step == 0)
    def _():
        maps[...] = decoded(pack_ref[2 * rows :])
        grad_acc[...] = jnp.zeros_like(grad_acc)

    dy = pack_ref[rows : 2 * rows]
    slot_down = lax.broadcasted_iota(jnp.int32, (slots, rows), 0)
    for i in range(offsets):
        row = maps[pl.ds(step * offsets + i, 1), :]
        chosen[:, i * rows : (i + 1) * rows] = (slot_down == row).astype(F32).astype(BF)
        back = lax.dot_general(dy, w_ref[i], (((1,), (1,)), ((), ())), preferred_element_type=F32)
        for t, part in enumerate(split(back, 2)):
            terms[t, i * rows : (i + 1) * rows] = part
    grad_acc[...] += dot(chosen[...], terms[0]) + dot(chosen[...], terms[1])

    @pl.when(step == pl.num_programs(0) - 1)
    def _():
        token_ref[...] = jnp.zeros_like(token_ref)
        at = 0
        for out in (own_ref, low_ref, high_ref):
            out[...] = grad_acc[at : at + out.shape[0]]
            at += out.shape[0]


def whole(shape):
    return pl.BlockSpec(shape, lambda k: (0,) * len(shape))


def backward(pack, weights, rows, halo, after):
    offsets, width, _ = weights.shape
    slots = rows + 2 * halo
    per_step = 3 if offsets % 3 == 0 else 1
    shapes = [jax.ShapeDtypeStruct((n, width), F32) for n in (rows, halo, halo)] + [TOKEN]
    return pl.pallas_call(
        backward_kernel,
        grid=(offsets // per_step,),
        out_shape=tuple(shapes),
        in_specs=[whole(pack.shape), pl.BlockSpec((per_step, width, width), lambda k: (k, 0, 0)), ANY],
        out_specs=tuple(whole(shape.shape) for shape in shapes),
        scratch_shapes=[
            pltpu.VMEM((pack.shape[0] - 2 * rows, rows), jnp.int32),
            pltpu.VMEM((slots, width), F32),
            pltpu.VMEM((slots, per_step * rows), BF),
            pltpu.VMEM((2, per_step * rows, width), BF),
        ],
        compiler_params=params(),
        cost_estimate=cost(),
        name="backward",
    )(pack, weights, after)


def forward_kernel(live_ref, pack_ref, halo_ref, w_ref, after_ref, out_ref, token_ref, table, maps, out_acc, picked):
    step = pl.program_id(0)
    offsets = w_ref.shape[0]
    rows, width = out_ref.shape
    slots = table.shape[0]

    @pl.when(step == 0)
    def _():
        maps[...] = decoded(pack_ref[2 * rows :])
        table[0:rows] = pack_ref[0:rows]
        table[rows:] = halo_ref[...]
        out_acc[...] = jnp.zeros_like(out_acc)

    along = lax.broadcasted_iota(jnp.int32, (rows, 128), 1)
    for i in range(offsets):
        row = maps[pl.ds(step * offsets + i, 1), :]
        column = jnp.transpose(jnp.broadcast_to(row, (128, rows)))
        chosen = jnp.concatenate(
            [(along + 128 * b == column).astype(F32).astype(BF) for b in range(slots // 128)], axis=1
        )
        picked[:, i * width : (i + 1) * width] = dot(chosen, table[...]).astype(BF)
    out_acc[...] += dot(picked[...], w_ref[...].reshape(offsets * width, width))

    @pl.when(step == pl.num_programs(0) - 1)
    def _():
        keep = lax.broadcasted_iota(jnp.int32, (rows, width), 0) < live_ref[0]
        out_ref[...] = jnp.where(keep, out_acc[...], 0.0).astype(BF)
        token_ref[...] = jnp.zeros_like(token_ref)


def forward(live, pack, halo_rows, weights, rows, after):
    offsets, width, _ = weights.shape
    slots = rows + halo_rows.shape[0]
    per_step = 3 if offsets % 3 == 0 else 1
    return pl.pallas_call(
        forward_kernel,
        grid=(offsets // per_step,),
        out_shape=(jax.ShapeDtypeStruct((rows, width), BF), TOKEN),
        in_specs=[
            SMEM,
            whole(pack.shape),
            whole(halo_rows.shape),
            pl.BlockSpec((per_step, width, width), lambda k: (k, 0, 0)),
            ANY,
        ],
        out_specs=(whole((rows, width)), whole(TOKEN.shape)),
        scratch_shapes=[
            pltpu.VMEM((slots, width), BF),
            pltpu.VMEM((pack.shape[0] - 2 * rows, rows), jnp.int32),
            pltpu.VMEM((rows, width), F32),
            pltpu.VMEM((rows, per_step * width), BF),
        ],
        compiler_params=params(),
        cost_estimate=cost(),
        name="forward",
    )(live, pack, halo_rows, weights, after)


def chosen_slots(maps, s, at, low, high, rows):
    iota = lax.broadcasted_iota(jnp.int32, (high - low, rows), 0) + low
    return (iota == maps[s, pl.ds(at, 1), :]).astype(F32).astype(BF)


def wgrad_own_kernel(sources, place_ref, *refs):
    packs = refs[:sources]
    picked_ref, dys, maps, tables = refs[sources:]
    count, width, _ = picked_ref.shape
    rows = dys.shape[0] // sources
    for s in range(sources):
        tables[:, s * rows : (s + 1) * rows] = jnp.transpose(packs[s][0:rows])
        dys[s * rows : (s + 1) * rows] = packs[s][rows : 2 * rows]
        maps[s] = decoded(packs[s][2 * rows :])

    def offset(j, carry):
        for s in range(sources):
            chosen = chosen_slots(maps, s, place_ref[0] * count + j, 0, rows, rows)
            picked_ref[j, :, s * rows : (s + 1) * rows] = dot(tables[:, s * rows : (s + 1) * rows], chosen).astype(BF)
        return carry

    lax.fori_loop(0, count, offset, 0)


def wgrad_own(place, packs, count, rows):
    sources, width = len(packs), packs[0].shape[1]
    return pl.pallas_call(
        functools.partial(wgrad_own_kernel, sources),
        out_shape=(
            jax.ShapeDtypeStruct((count, width, sources * rows), BF),
            jax.ShapeDtypeStruct((sources * rows, width), BF),
            jax.ShapeDtypeStruct((sources, packs[0].shape[0] - 2 * rows, rows), jnp.int32),
        ),
        in_specs=[SMEM] + [VMEM] * sources,
        out_specs=(VMEM, VMEM, VMEM),
        scratch_shapes=[pltpu.VMEM((width, sources * rows), BF)],
        compiler_params=params(),
        cost_estimate=cost(),
        name="wgrad_own",
    )(place, *packs)


def wgrad_kernel(sources, first, place_ref, picked_ref, dys, maps, *refs):
    halos, (after_ref, keep_ref, send_ref, tables, picked) = refs[:sources], refs[sources:]
    count, half, width = keep_ref.shape
    rows = maps.shape[2]
    far = halos[0].shape[0]
    core = place_ref[1]
    for s in range(sources):
        tables[:, s * far : (s + 1) * far] = jnp.transpose(halos[s][...])
    for j in range(count):
        for s in range(sources):
            chosen = chosen_slots(maps, s, place_ref[0] * picked_ref.shape[0] + first + j, rows, rows + far, rows)
            near = picked_ref[first + j, :, s * rows : (s + 1) * rows].astype(F32)
            picked[j, :, s * rows : (s + 1) * rows] = (dot(tables[:, s * far : (s + 1) * far], chosen) + near).astype(BF)
        send_ref[j] = dot(picked[j, pl.ds(pl.multiple_of((1 - core) * half, half), half), :], dys[...])
        keep_ref[j] = dot(picked[j, pl.ds(pl.multiple_of(core * half, half), half), :], dys[...])


def wgrad(place, picked, dys, maps, halos, first, count, after):
    _, width, columns = picked.shape
    sources = maps.shape[0]
    shape = jax.ShapeDtypeStruct((count, width // 2, width), F32)
    return pl.pallas_call(
        functools.partial(wgrad_kernel, sources, first),
        out_shape=(shape, shape),
        in_specs=[SMEM] + [VMEM] * (3 + sources) + [ANY],
        out_specs=(VMEM, VMEM),
        scratch_shapes=[
            pltpu.VMEM((width, sources * halos[0].shape[0]), BF),
            pltpu.VMEM((count, width, columns), BF),
        ],
        compiler_params=params(),
        cost_estimate=cost(),
        name="wgrad",
    )(place, picked, dys, maps, *halos, after)


def power(exponent):
    value = jnp.ones(exponent.shape, F32)
    size = jnp.abs(exponent)
    for bit in range(7):
        factor = jnp.where(exponent < 0, 0.5 ** (1 << bit), 2.0 ** (1 << bit))
        value = value * jnp.where((size >> bit) & 1 == 1, factor, 1.0)
    return value


def blocks_kernel(place_ref, keep_ref, got_ref, mine_ref, *refs):
    coded_refs, exponents = refs[:-1], refs[-1]
    count, block, width = mine_ref.shape
    for m in range(len(coded_refs) + 1):
        at = pl.ds(pl.multiple_of((place_ref[2] ^ m) * block, block), block)
        if m == 0:
            mine_ref[...] = keep_ref[:, at, :] + got_ref[:, at, :]
            continue
        exponents[...] = jnp.zeros_like(exponents)
        for j in range(count):
            value = keep_ref[j, at, :] + got_ref[j, at, :]
            largest = jnp.max(jnp.abs(value), axis=0, keepdims=True)
            exponent = jnp.ceil(jnp.log(jnp.maximum(largest, 2.0**-100)) * (1.0 / math.log(2.0)))
            exponent = jnp.clip(exponent, -100.0, 100.0).astype(jnp.int32) - 15
            exponents[j : j + 1, :] = exponent
            scaled = jnp.round(jnp.clip(value * power(-exponent), -32767.0, 32767.0))
            coded_refs[m - 1][j * block : (j + 1) * block] = scaled.astype(jnp.int32).astype(jnp.int16)
        coded_refs[m - 1][count * block :] = exponents[...].astype(jnp.int16)


def blocks(place, keep, got, parts):
    count, half, width = keep.shape
    block = half // parts
    extra = -(-count // 16) * 16
    return pl.pallas_call(
        blocks_kernel,
        out_shape=(
            jax.ShapeDtypeStruct((count, block, width), F32),
            *(jax.ShapeDtypeStruct((count * block + extra, width), jnp.int16),) * (parts - 1),
        ),
        in_specs=[SMEM, VMEM, VMEM],
        out_specs=(VMEM,) * parts,
        scratch_shapes=[pltpu.VMEM((extra, width), jnp.int32)],
        compiler_params=params(),
        cost_estimate=cost(),
        name="blocks",
    )(place, keep, got)


def total_kernel(scale, mine_ref, *refs):
    *coded_refs, _, _, out_ref = refs
    count, block, width = mine_ref.shape
    powers = [power(ref[count * block :].astype(jnp.int32)) for ref in coded_refs]
    for j in range(count):
        total = mine_ref[j]
        for ref, factor in zip(coded_refs, powers):
            value = ref[j * block : (j + 1) * block].astype(jnp.int32).astype(F32)
            total = total + value * factor[j : j + 1, :]
        out_ref[j] = (total * scale).astype(BF)


def scaled_total(mine, coded, scale, after):
    return pl.pallas_call(
        functools.partial(total_kernel, scale),
        out_shape=jax.ShapeDtypeStruct(mine.shape, BF),
        in_specs=[VMEM] * (len(coded) + 1) + [ANY] * 2,
        out_specs=VMEM,
        compiler_params=params(),
        cost_estimate=cost(),
        name="total",
    )(mine, *coded, *after)


def final_kernel(live_ref, own_ref, back_up_ref, back_down_ref, up_ref, down_ref, after_ref, out_ref, token_ref):
    rows, width = own_ref.shape
    halo = up_ref.shape[1]
    total = own_ref[...]
    iota = lax.broadcasted_iota(jnp.int32, (rows, halo), 0)
    for index_ref, back_ref in ((up_ref, back_up_ref), (down_ref, back_down_ref)):
        chosen = (iota == index_ref[...]).astype(F32).astype(BF)
        for part in split(back_ref[...], 3):
            total = total + dot(chosen, part)
    keep = lax.broadcasted_iota(jnp.int32, (rows, width), 0) < live_ref[0]
    out_ref[...] = jnp.where(keep, total, 0.0).astype(BF)
    token_ref[...] = jnp.zeros_like(token_ref)


def final(live, own_grad, back_up, back_down, send_up, send_down, after):
    return pl.pallas_call(
        final_kernel,
        out_shape=(jax.ShapeDtypeStruct(own_grad.shape, BF), TOKEN),
        in_specs=[SMEM] + [VMEM] * 5 + [ANY],
        out_specs=(VMEM, VMEM),
        compiler_params=params(),
        name="final",
    )(live, own_grad, back_up, back_down, send_up, send_down, after)


def line_kernel(count, *refs):
    for m in range(count):
        refs[-1][m] = refs[m][...]


def line(blocks, after):
    if len(blocks) == 1:
        return blocks[0][None]
    return pl.pallas_call(
        functools.partial(line_kernel, len(blocks)),
        out_shape=jax.ShapeDtypeStruct((len(blocks), *blocks[0].shape), BF),
        in_specs=[VMEM] * len(blocks) + [ANY] * len(after),
        out_specs=VMEM,
        compiler_params=params(),
        cost_estimate=cost(),
        name="line",
    )(*blocks, *after)


def assemble_kernel(marks, parts, groups, place_ref, *refs):
    out_ref, sems = refs[-2:]
    offsets = out_ref.shape[0]
    _, count, block, _ = refs[0].shape
    short = offsets - (groups - 1) * count

    def each(act):
        for index, (m, o, masks) in enumerate(marks):
            group = place_ref[0] ^ m
            for part, mask in enumerate(masks):
                row = pl.multiple_of(((place_ref[1] ^ o) * parts + (place_ref[2] ^ mask)) * block, block)
                source = refs[index].at[part]

                def copy(lo, hi, sem):
                    target = out_ref.at[pl.ds(group * count + lo, hi - lo), pl.ds(row, block)]
                    return pltpu.make_async_copy(source.at[lo:hi], target, sems.at[index, part, sem])

                getattr(copy(0, short, 0), act)()
                if short < count:
                    pl.when(group < groups - 1)(getattr(copy(short, count, 1), act))

    each("start")
    each("wait")


def assemble(place, pieces, marks, parts, groups, offsets, width, after):
    return pl.pallas_call(
        functools.partial(assemble_kernel, marks, parts, groups),
        out_shape=jax.ShapeDtypeStruct((offsets, width, width), BF),
        in_specs=[SMEM] + [ANY] * (len(pieces) + 1),
        out_specs=ANY,
        scratch_shapes=[pltpu.SemaphoreType.DMA((len(pieces), parts, 2))],
        compiler_params=params(),
        name="assemble",
    )(place, *pieces, after)


def assemble_plain(place, pieces, marks, parts, groups, offsets, width, after):
    _, count, block, _ = pieces[0].shape
    total = jnp.zeros((groups * count, width, width), BF)
    for piece, (m, o, masks) in zip(pieces, marks):
        for part, mask in enumerate(masks):
            row = ((place[1] ^ o) * parts + (place[2] ^ mask)) * block
            total = lax.dynamic_update_slice(total, piece[part], ((place[0] ^ m) * count, row, 0))
    return total[:offsets]


def swap(value, axis, mask):
    return lax.ppermute(value, axis, [(i, i ^ mask) for i in range(lax.axis_size(axis))])


def passed_along(value, axis, steps):
    count = lax.axis_size(axis)
    return lax.ppermute(value, axis, [(i, i + steps) for i in range(max(0, -steps), min(count, count - steps))])


def SPLITS(parts):
    return [(0,), tuple(range(1, parts))]


def shards(features, weights, cotangent, kernel_map, live, send_up, send_down):
    rows, width = features.shape
    offsets, halo = weights.shape[0], send_up.shape[1]
    groups = lax.axis_size("dp") // 2
    parts = lax.axis_size("space")
    count = -(-offsets // groups)
    map_rows = -(-(groups * count) // 16) * 16
    dp, space = lax.axis_index("dp"), lax.axis_index("space")
    place = jnp.stack([dp // 2, dp % 2, space]).astype(jnp.int32)

    pack, up_rows, down_rows = prep(live, features, cotangent, kernel_map, send_up, send_down, map_rows)
    packs = [pack] + [swap(pack, "dp", 2 * m) for m in range(1, groups)]
    lower = passed_along(up_rows, "space", 1)
    upper = passed_along(down_rows, "space", -1)
    halo_rows = jnp.concatenate([lower, upper])
    halos = [halo_rows] + [swap(halo_rows, "dp", 2 * m) for m in range(1, groups)]
    picked, dys, maps = wgrad_own(place, packs, count, rows)
    keep, send = wgrad(place, picked, dys, maps, halos, 0, count, dys)
    mine, *coded = blocks(place, keep, swap(send, "dp", 1), parts)
    own_grad, low_grad, high_grad, token = backward(pack, weights, rows, halo, mine)
    back_up = passed_along(low_grad, "space", -1)
    back_down = passed_along(high_grad, "space", 1)
    scale = 1.0 / math.sqrt(rows * lax.axis_size("dp") * parts)
    rounded = scaled_total(mine, [swap(block, "space", m + 1) for m, block in enumerate(coded)], scale, (token, token))
    out_features, token = forward(live, pack, halo_rows, weights, rows, rounded)

    in_line = [rounded] + [swap(rounded, "space", m) for m in range(1, parts)]
    pieces, marks = [], []
    for masks in SPLITS(parts):
        lines = line([in_line[m] for m in masks], pieces[2::2][-groups:] + [token])
        for m in range(groups):
            piece = swap(lines, "dp", 2 * m) if m else lines
            pieces += [piece, swap(piece, "dp", 1)]
            marks += [(m, 0, masks), (m, 1, masks)]
    grad_features, token = final(live, own_grad, back_up, back_down, send_up, send_down, lines)
    dense = rounded.shape[1] % 16 == 0 and groups * count - offsets < count
    put = assemble if dense else assemble_plain
    grad_weights = put(place, pieces, marks, parts, groups, offsets, width, token)
    return (out_features, grad_features, grad_weights)


def solution(mesh):
    placed = (
        P(("dp", "space"), None),
        P(),
        P(("dp", "space"), None),
        P(None, ("dp", "space")),
        P(("dp", "space")),
        P(("dp", "space"), None),
        P(("dp", "space"), None),
    )
    return jax.shard_map(
        shards,
        mesh=mesh,
        in_specs=placed,
        out_specs=(P(("dp", "space"), None), P(("dp", "space"), None), P()),
        check_vma=False,
    )
```

```python
import functools
import math

import jax
import jax.numpy as jnp
from jax import lax
from jax.experimental import pallas as pl
from jax.experimental.pallas import tpu as pltpu
from jax.sharding import PartitionSpec as P

BF = jnp.bfloat16
F32 = jnp.float32
VMEM_LIMIT = 32 * 1024 * 1024
PREP_LIMIT = 60 * 1024 * 1024
VMEM = pl.BlockSpec(memory_space=pltpu.VMEM)
SMEM = pl.BlockSpec(memory_space=pltpu.SMEM)
ANY = pl.BlockSpec(memory_space=pl.ANY)
HBM = pl.BlockSpec(memory_space=pltpu.HBM)
TOKEN = jax.ShapeDtypeStruct((8, 128), F32)


def params(limit=VMEM_LIMIT):
    return pltpu.CompilerParams(vmem_limit_bytes=limit)


def cost():
    return pl.CostEstimate(flops=100_000_000, bytes_accessed=100_000, transcendentals=0)


def dot(a, b):
    return jnp.dot(a, b, preferred_element_type=F32)


def split(value, terms):
    parts = []
    for _ in range(terms):
        part = value.astype(BF)
        parts.append(part)
        value = value - part.astype(F32)
    return parts


def prep_kernel(live_ref, x_hbm, dy_hbm, map_hbm, up_hbm, down_hbm, pack_ref, up_rows_ref, down_rows_ref, *scratch):
    x_ref, dy_ref, map_ref, up_ref, down_ref, map_scr, sems = scratch
    sources = (x_hbm, dy_hbm, map_hbm, up_hbm, down_hbm)
    targets = (x_ref, dy_ref, map_ref, up_ref, down_ref)
    copies = [pltpu.make_async_copy(a, b, sems.at[i]) for i, (a, b) in enumerate(zip(sources, targets))]
    for copy in copies:
        copy.start()
    rows, width = x_ref.shape
    offsets = map_ref.shape[0]
    halo = up_ref.shape[1]
    keep = lax.broadcasted_iota(jnp.int32, (rows, width), 0) < live_ref[0]
    map_scr[...] = jnp.full(map_scr.shape, rows + 2 * halo, jnp.int32)
    for copy in copies:
        copy.wait()
    x_live = jnp.where(keep, x_ref[...].astype(F32), 0.0).astype(BF)
    pack_ref[0:rows] = x_live
    iota = lax.broadcasted_iota(jnp.int32, (rows, halo), 0)
    for index_ref, picked_ref in ((up_ref, up_rows_ref), (down_ref, down_rows_ref)):
        chosen = (iota == index_ref[...]).astype(F32).astype(BF)
        picked_ref[...] = lax.dot_general(chosen, x_live, (((0,), (0,)), ((), ())), preferred_element_type=F32).astype(BF)
    pack_ref[rows : 2 * rows] = jnp.where(keep, dy_ref[...].astype(F32), 0.0).astype(BF)
    map_scr[0:offsets] = map_ref[...]
    slots = map_scr[...]
    pack_ref[2 * rows :] = jnp.where(slots > 256, 256 - slots, slots).astype(F32).astype(BF)


def prep(live, features, cotangent, kernel_map, send_up, send_down, map_rows):
    rows, width = features.shape
    return pl.pallas_call(
        prep_kernel,
        out_shape=(
            jax.ShapeDtypeStruct((2 * rows + map_rows, width), BF),
            jax.ShapeDtypeStruct((send_up.shape[1], width), BF),
            jax.ShapeDtypeStruct((send_up.shape[1], width), BF),
        ),
        in_specs=[SMEM] + [HBM] * 5,
        out_specs=(VMEM,) * 3,
        scratch_shapes=[
            pltpu.VMEM((rows, width), BF),
            pltpu.VMEM((rows, width), BF),
            pltpu.VMEM(kernel_map.shape, jnp.int32),
            pltpu.VMEM(send_up.shape, jnp.int32),
            pltpu.VMEM(send_down.shape, jnp.int32),
            pltpu.VMEM((map_rows, rows), jnp.int32),
            pltpu.SemaphoreType.DMA((5,)),
        ],
        compiler_params=params(PREP_LIMIT),
        name="prep",
    )(live, features, cotangent, kernel_map, send_up, send_down)


def decoded(code):
    code = code.astype(F32).astype(jnp.int32)
    return jnp.where(code < 0, 256 - code, code)


def backward_kernel(group, pack_ref, w_ref, after_ref, own_ref, low_ref, high_ref, token_ref, maps, chosen, terms):
    offsets, width, _ = w_ref.shape
    rows = own_ref.shape[0]
    slots = chosen.shape[1]
    maps[...] = decoded(pack_ref[2 * rows :])
    dy = pack_ref[rows : 2 * rows]
    slot_down = lax.broadcasted_iota(jnp.int32, (slots, rows), 0)
    for k in range(offsets):
        at = slice(k % group * rows, (k % group + 1) * rows)
        chosen[k // group, :, at] = (slot_down == maps[k : k + 1, :]).astype(F32).astype(BF)
        back = lax.dot_general(dy, w_ref[k], (((1,), (1,)), ((), ())), preferred_element_type=F32)
        for t, part in enumerate(split(back, 2)):
            terms[k // group, t, at] = part
    for g in range(offsets // group):
        at = 0
        for out in (own_ref, low_ref, high_ref):
            some = chosen[g, at : at + out.shape[0]]
            value = dot(some, terms[g, 0]) + dot(some, terms[g, 1])
            out[...] = value if g == 0 else out[...] + value
            at += out.shape[0]
    token_ref[...] = jnp.zeros_like(token_ref)


def backward(pack, weights, rows, halo, after):
    offsets, width, _ = weights.shape
    slots = rows + 2 * halo
    group = 3 if offsets % 3 == 0 else 1
    return pl.pallas_call(
        functools.partial(backward_kernel, group),
        out_shape=tuple(jax.ShapeDtypeStruct((n, width), F32) for n in (rows, halo, halo)) + (TOKEN,),
        in_specs=[VMEM, VMEM, ANY],
        out_specs=(VMEM,) * 4,
        scratch_shapes=[
            pltpu.VMEM((pack.shape[0] - 2 * rows, rows), jnp.int32),
            pltpu.VMEM((offsets // group, slots, group * rows), BF),
            pltpu.VMEM((offsets // group, 2, group * rows, width), BF),
        ],
        compiler_params=params(),
        cost_estimate=cost(),
        name="backward",
    )(pack, weights, after)


def forward_kernel(group, live_ref, pack_ref, halo_ref, w_ref, after_ref, out_ref, token_ref, table, maps, out_acc, picked):
    offsets, width, _ = w_ref.shape
    rows = out_ref.shape[0]
    slots = table.shape[0]
    table[0:rows] = pack_ref[0:rows]
    table[rows:] = halo_ref[...]
    codes = decoded(pack_ref[2 * rows :])
    maps[...] = jnp.transpose(jnp.concatenate([codes] * (maps.shape[1] // codes.shape[0]), axis=0))
    along = lax.broadcasted_iota(jnp.int32, (rows, 128), 1)
    for k in range(offsets):
        column = jnp.broadcast_to(maps[:, k : k + 1], (rows, 128))
        chosen = jnp.concatenate(
            [(along + 128 * b == column).astype(F32).astype(BF) for b in range(slots // 128)], axis=1
        )
        picked[k // group, :, k % group * width : (k % group + 1) * width] = dot(chosen, table[...]).astype(BF)
    for g in range(offsets // group):
        value = dot(picked[g], w_ref[g * group : (g + 1) * group].reshape(group * width, width))
        out_acc[...] = value if g == 0 else out_acc[...] + value
    keep = lax.broadcasted_iota(jnp.int32, (rows, width), 0) < live_ref[0]
    out_ref[...] = jnp.where(keep, out_acc[...], 0.0).astype(BF)
    token_ref[...] = jnp.zeros_like(token_ref)


def forward(live, pack, halo_rows, weights, rows, after):
    offsets, width, _ = weights.shape
    slots = rows + halo_rows.shape[0]
    group = 3 if offsets % 3 == 0 else 1
    return pl.pallas_call(
        functools.partial(forward_kernel, group),
        out_shape=(jax.ShapeDtypeStruct((rows, width), BF), TOKEN),
        in_specs=[SMEM, VMEM, VMEM, VMEM, ANY],
        out_specs=(VMEM, VMEM),
        scratch_shapes=[
            pltpu.VMEM((slots, width), BF),
            pltpu.VMEM((rows, 128), jnp.int32),
            pltpu.VMEM((rows, width), F32),
            pltpu.VMEM((offsets // group, rows, group * width), BF),
        ],
        compiler_params=params(),
        cost_estimate=cost(),
        name="forward",
    )(live, pack, halo_rows, weights, after)


def chosen_slots(maps, s, at, low, high, rows):
    iota = lax.broadcasted_iota(jnp.int32, (high - low, rows), 0) + low
    return (iota == maps[s, pl.ds(at, 1), :]).astype(F32).astype(BF)


def wgrad_own_kernel(sources, place_ref, *refs):
    packs = refs[:sources]
    picked_ref, dys, maps, tables = refs[sources:]
    count, width, _ = picked_ref.shape
    rows = dys.shape[0] // sources
    for s in range(sources):
        tables[:, s * rows : (s + 1) * rows] = jnp.transpose(packs[s][0:rows])
        dys[s * rows : (s + 1) * rows] = packs[s][rows : 2 * rows]
        maps[s] = decoded(packs[s][2 * rows :])

    for j in range(count):
        for s in range(sources):
            chosen = chosen_slots(maps, s, place_ref[0] * count + j, 0, rows, rows)
            picked_ref[j, :, s * rows : (s + 1) * rows] = dot(tables[:, s * rows : (s + 1) * rows], chosen).astype(BF)


def wgrad_own(place, packs, count, rows):
    sources, width = len(packs), packs[0].shape[1]
    return pl.pallas_call(
        functools.partial(wgrad_own_kernel, sources),
        out_shape=(
            jax.ShapeDtypeStruct((count, width, sources * rows), BF),
            jax.ShapeDtypeStruct((sources * rows, width), BF),
            jax.ShapeDtypeStruct((sources, packs[0].shape[0] - 2 * rows, rows), jnp.int32),
        ),
        in_specs=[SMEM] + [VMEM] * sources,
        out_specs=(VMEM, VMEM, VMEM),
        scratch_shapes=[pltpu.VMEM((width, sources * rows), BF)],
        compiler_params=params(),
        cost_estimate=cost(),
        name="wgrad_own",
    )(place, *packs)


def wgrad_kernel(sources, first, place_ref, picked_ref, dys, maps, *refs):
    halos, (after_ref, keep_ref, send_ref, tables, picked) = refs[:sources], refs[sources:]
    count, half, width = keep_ref.shape
    rows = maps.shape[2]
    far = halos[0].shape[0]
    core = place_ref[1]
    for s in range(sources):
        tables[:, s * far : (s + 1) * far] = jnp.transpose(halos[s][...])
    for j in range(count):
        for s in range(sources):
            chosen = chosen_slots(maps, s, place_ref[0] * picked_ref.shape[0] + first + j, rows, rows + far, rows)
            near = picked_ref[first + j, :, s * rows : (s + 1) * rows].astype(F32)
            picked[j, :, s * rows : (s + 1) * rows] = (dot(tables[:, s * far : (s + 1) * far], chosen) + near).astype(BF)
    for j in range(count):
        send_ref[j] = dot(picked[j, pl.ds(pl.multiple_of((1 - core) * half, half), half), :], dys[...])
        keep_ref[j] = dot(picked[j, pl.ds(pl.multiple_of(core * half, half), half), :], dys[...])


def wgrad(place, picked, dys, maps, halos, first, count, after):
    _, width, columns = picked.shape
    sources = maps.shape[0]
    shape = jax.ShapeDtypeStruct((count, width // 2, width), F32)
    return pl.pallas_call(
        functools.partial(wgrad_kernel, sources, first),
        out_shape=(shape, shape),
        in_specs=[SMEM] + [VMEM] * (3 + sources) + [ANY],
        out_specs=(VMEM, VMEM),
        scratch_shapes=[
            pltpu.VMEM((width, sources * halos[0].shape[0]), BF),
            pltpu.VMEM((count, width, columns), BF),
        ],
        compiler_params=params(),
        cost_estimate=cost(),
        name="wgrad",
    )(place, picked, dys, maps, *halos, after)


def power(exponent):
    value = jnp.ones(exponent.shape, F32)
    size = jnp.abs(exponent)
    for bit in range(7):
        factor = jnp.where(exponent < 0, 0.5 ** (1 << bit), 2.0 ** (1 << bit))
        value = value * jnp.where((size >> bit) & 1 == 1, factor, 1.0)
    return value


def blocks_kernel(place_ref, keep_ref, got_ref, mine_ref, *refs):
    coded_refs, exponents = refs[:-1], refs[-1]
    count, block, width = mine_ref.shape
    for m in range(len(coded_refs) + 1):
        at = pl.ds(pl.multiple_of((place_ref[2] ^ m) * block, block), block)
        if m == 0:
            mine_ref[...] = keep_ref[:, at, :] + got_ref[:, at, :]
            continue
        exponents[...] = jnp.zeros_like(exponents)
        for j in range(count):
            value = keep_ref[j, at, :] + got_ref[j, at, :]
            largest = jnp.max(jnp.abs(value), axis=0, keepdims=True)
            exponent = jnp.ceil(jnp.log(jnp.maximum(largest, 2.0**-100)) * (1.0 / math.log(2.0)))
            exponent = jnp.clip(exponent, -100.0, 100.0).astype(jnp.int32) - 15
            exponents[j : j + 1, :] = exponent
            scaled = jnp.round(jnp.clip(value * power(-exponent), -32767.0, 32767.0))
            coded_refs[m - 1][j * block : (j + 1) * block] = scaled.astype(jnp.int32).astype(jnp.int16)
        coded_refs[m - 1][count * block :] = exponents[...].astype(jnp.int16)


def blocks(place, keep, got, parts):
    count, half, width = keep.shape
    block = half // parts
    extra = -(-count // 16) * 16
    return pl.pallas_call(
        blocks_kernel,
        out_shape=(
            jax.ShapeDtypeStruct((count, block, width), F32),
            *(jax.ShapeDtypeStruct((count * block + extra, width), jnp.int16),) * (parts - 1),
        ),
        in_specs=[SMEM, VMEM, VMEM],
        out_specs=(VMEM,) * parts,
        scratch_shapes=[pltpu.VMEM((extra, width), jnp.int32)],
        compiler_params=params(),
        cost_estimate=cost(),
        name="blocks",
    )(place, keep, got)


def total_kernel(scale, mine_ref, *refs):
    *coded_refs, _, _, out_ref = refs
    count, block, width = mine_ref.shape
    powers = [power(ref[count * block :].astype(jnp.int32)) for ref in coded_refs]
    for j in range(count):
        total = mine_ref[j]
        for ref, factor in zip(coded_refs, powers):
            value = ref[j * block : (j + 1) * block].astype(jnp.int32).astype(F32)
            total = total + value * factor[j : j + 1, :]
        out_ref[j] = (total * scale).astype(BF)


def scaled_total(mine, coded, scale, after):
    return pl.pallas_call(
        functools.partial(total_kernel, scale),
        out_shape=jax.ShapeDtypeStruct(mine.shape, BF),
        in_specs=[VMEM] * (len(coded) + 1) + [ANY] * 2,
        out_specs=VMEM,
        compiler_params=params(),
        cost_estimate=cost(),
        name="total",
    )(mine, *coded, *after)


def final_kernel(live_ref, own_ref, back_up_ref, back_down_ref, up_ref, down_ref, after_ref, out_ref, token_ref):
    rows, width = own_ref.shape
    halo = up_ref.shape[1]
    total = own_ref[...]
    iota = lax.broadcasted_iota(jnp.int32, (rows, halo), 0)
    for index_ref, back_ref in ((up_ref, back_up_ref), (down_ref, back_down_ref)):
        chosen = (iota == index_ref[...]).astype(F32).astype(BF)
        for part in split(back_ref[...], 3):
            total = total + dot(chosen, part)
    keep = lax.broadcasted_iota(jnp.int32, (rows, width), 0) < live_ref[0]
    out_ref[...] = jnp.where(keep, total, 0.0).astype(BF)
    token_ref[...] = jnp.zeros_like(token_ref)


def final(live, own_grad, back_up, back_down, send_up, send_down, after):
    return pl.pallas_call(
        final_kernel,
        out_shape=(jax.ShapeDtypeStruct(own_grad.shape, BF), TOKEN),
        in_specs=[SMEM] + [VMEM] * 5 + [ANY],
        out_specs=(VMEM, VMEM),
        compiler_params=params(),
        name="final",
    )(live, own_grad, back_up, back_down, send_up, send_down, after)


def line_kernel(count, *refs):
    for m in range(count):
        refs[-1][m] = refs[m][...]


def line(blocks, after):
    if len(blocks) == 1:
        return blocks[0][None]
    return pl.pallas_call(
        functools.partial(line_kernel, len(blocks)),
        out_shape=jax.ShapeDtypeStruct((len(blocks), *blocks[0].shape), BF),
        in_specs=[VMEM] * len(blocks) + [ANY] * len(after),
        out_specs=VMEM,
        compiler_params=params(),
        cost_estimate=cost(),
        name="line",
    )(*blocks, *after)


def assemble_kernel(marks, parts, groups, place_ref, *refs):
    out_ref, sems = refs[-2:]
    offsets = out_ref.shape[0]
    _, count, block, _ = refs[0].shape
    short = offsets - (groups - 1) * count

    def each(act):
        for index, (m, o, masks) in enumerate(marks):
            group = place_ref[0] ^ m
            for part, mask in enumerate(masks):
                row = pl.multiple_of(((place_ref[1] ^ o) * parts + (place_ref[2] ^ mask)) * block, block)
                source = refs[index].at[part]

                def copy(lo, hi, sem):
                    target = out_ref.at[pl.ds(group * count + lo, hi - lo), pl.ds(row, block)]
                    return pltpu.make_async_copy(source.at[lo:hi], target, sems.at[index, part, sem])

                getattr(copy(0, short, 0), act)()
                if short < count:
                    pl.when(group < groups - 1)(getattr(copy(short, count, 1), act))

    each("start")
    each("wait")


def assemble(place, pieces, marks, parts, groups, offsets, width, after):
    return pl.pallas_call(
        functools.partial(assemble_kernel, marks, parts, groups),
        out_shape=jax.ShapeDtypeStruct((offsets, width, width), BF),
        in_specs=[SMEM] + [ANY] * (len(pieces) + 1),
        out_specs=ANY,
        scratch_shapes=[pltpu.SemaphoreType.DMA((len(pieces), parts, 2))],
        compiler_params=params(),
        name="assemble",
    )(place, *pieces, after)


def assemble_plain(place, pieces, marks, parts, groups, offsets, width, after):
    _, count, block, _ = pieces[0].shape
    total = jnp.zeros((groups * count, width, width), BF)
    for piece, (m, o, masks) in zip(pieces, marks):
        for part, mask in enumerate(masks):
            row = ((place[1] ^ o) * parts + (place[2] ^ mask)) * block
            total = lax.dynamic_update_slice(total, piece[part], ((place[0] ^ m) * count, row, 0))
    return total[:offsets]


def swap(value, axis, mask):
    return lax.ppermute(value, axis, [(i, i ^ mask) for i in range(lax.axis_size(axis))])


def passed_along(value, axis, steps):
    count = lax.axis_size(axis)
    return lax.ppermute(value, axis, [(i, i + steps) for i in range(max(0, -steps), min(count, count - steps))])


def SPLITS(parts):
    return [(0,), tuple(range(1, parts))]


def shards(features, weights, cotangent, kernel_map, live, send_up, send_down):
    rows, width = features.shape
    offsets, halo = weights.shape[0], send_up.shape[1]
    groups = lax.axis_size("dp") // 2
    parts = lax.axis_size("space")
    count = -(-offsets // groups)
    map_rows = -(-(groups * count) // 16) * 16
    dp, space = lax.axis_index("dp"), lax.axis_index("space")
    place = jnp.stack([dp // 2, dp % 2, space]).astype(jnp.int32)

    pack, up_rows, down_rows = prep(live, features, cotangent, kernel_map, send_up, send_down, map_rows)
    packs = [pack] + [swap(pack, "dp", 2 * m) for m in range(1, groups)]
    lower = passed_along(up_rows, "space", 1)
    upper = passed_along(down_rows, "space", -1)
    halo_rows = jnp.concatenate([lower, upper])
    halos = [halo_rows] + [swap(halo_rows, "dp", 2 * m) for m in range(1, groups)]
    picked, dys, maps = wgrad_own(place, packs, count, rows)
    keep, send = wgrad(place, picked, dys, maps, halos, 0, count, dys)
    mine, *coded = blocks(place, keep, swap(send, "dp", 1), parts)
    own_grad, low_grad, high_grad, token = backward(pack, weights, rows, halo, mine)
    back_up = passed_along(low_grad, "space", -1)
    back_down = passed_along(high_grad, "space", 1)
    scale = 1.0 / math.sqrt(rows * lax.axis_size("dp") * parts)
    rounded = scaled_total(mine, [swap(block, "space", m + 1) for m, block in enumerate(coded)], scale, (token, token))
    out_features, token = forward(live, pack, halo_rows, weights, rows, rounded)

    in_line = [rounded] + [swap(rounded, "space", m) for m in range(1, parts)]
    pieces, marks = [], []
    for masks in SPLITS(parts):
        lines = line([in_line[m] for m in masks], pieces[2::2][-groups:] + [token])
        for m in range(groups):
            piece = swap(lines, "dp", 2 * m) if m else lines
            pieces += [piece, swap(piece, "dp", 1)]
            marks += [(m, 0, masks), (m, 1, masks)]
    grad_features, token = final(live, own_grad, back_up, back_down, send_up, send_down, lines)
    dense = rounded.shape[1] % 16 == 0 and groups * count - offsets < count
    put = assemble if dense else assemble_plain
    grad_weights = put(place, pieces, marks, parts, groups, offsets, width, token)
    return (out_features, grad_features, grad_weights)


def solution(mesh):
    placed = (
        P(("dp", "space"), None),
        P(),
        P(("dp", "space"), None),
        P(None, ("dp", "space")),
        P(("dp", "space")),
        P(("dp", "space"), None),
        P(("dp", "space"), None),
    )
    return jax.shard_map(
        shards,
        mesh=mesh,
        in_specs=placed,
        out_specs=(P(("dp", "space"), None), P(("dp", "space"), None), P()),
        check_vma=False,
    )
```

```python
import functools
import math

import jax
import jax.numpy as jnp
from jax import lax
from jax.experimental import pallas as pl
from jax.experimental.pallas import tpu as pltpu
from jax.sharding import PartitionSpec as P

BF = jnp.bfloat16
F32 = jnp.float32
VMEM_LIMIT = 32 * 1024 * 1024
PREP_LIMIT = 60 * 1024 * 1024
VMEM = pl.BlockSpec(memory_space=pltpu.VMEM)
SMEM = pl.BlockSpec(memory_space=pltpu.SMEM)
ANY = pl.BlockSpec(memory_space=pl.ANY)
HBM = pl.BlockSpec(memory_space=pltpu.HBM)
TOKEN = jax.ShapeDtypeStruct((8, 128), F32)


def params(limit=VMEM_LIMIT):
    return pltpu.CompilerParams(vmem_limit_bytes=limit)


def cost():
    return pl.CostEstimate(flops=100_000_000, bytes_accessed=100_000, transcendentals=0)


def dot(a, b):
    return jnp.dot(a, b, preferred_element_type=F32)


def split(value, terms):
    parts = []
    for _ in range(terms):
        part = value.astype(BF)
        parts.append(part)
        value = value - part.astype(F32)
    return parts


def place():
    dp = lax.axis_index("dp")
    return dp // 2, lax.rem(dp, 2), lax.axis_index("space")


def turns(up, down):
    even = lax.rem(place()[2], 2) == 0
    return jnp.where(even, up, down), jnp.where(even, down, up)


def prep_kernel(live_ref, x_hbm, dy_hbm, map_hbm, up_hbm, down_hbm, pack_ref, first_ref, second_ref, *scratch):
    x_ref, dy_ref, map_ref, up_ref, down_ref, map_scr, sems = scratch
    sources = (x_hbm, dy_hbm, map_hbm, up_hbm, down_hbm)
    targets = (x_ref, dy_ref, map_ref, up_ref, down_ref)
    copies = [pltpu.make_async_copy(a, b, sems.at[i]) for i, (a, b) in enumerate(zip(sources, targets))]
    for copy in copies:
        copy.start()
    rows, width = x_ref.shape
    offsets = map_ref.shape[0]
    halo = up_ref.shape[1]
    keep = lax.broadcasted_iota(jnp.int32, (rows, width), 0) < live_ref[0]
    map_scr[...] = jnp.full(map_scr.shape, rows + 2 * halo, jnp.int32)
    for copy in copies:
        copy.wait()
    x_live = jnp.where(keep, x_ref[...].astype(F32), 0.0).astype(BF)
    pack_ref[0:rows] = x_live
    iota = lax.broadcasted_iota(jnp.int32, (rows, halo), 0)
    for index, picked_ref in zip(turns(up_ref[...], down_ref[...]), (first_ref, second_ref)):
        chosen = (iota == index).astype(F32).astype(BF)
        picked_ref[...] = lax.dot_general(chosen, x_live, (((0,), (0,)), ((), ())), preferred_element_type=F32).astype(BF)
    pack_ref[rows : 2 * rows] = jnp.where(keep, dy_ref[...].astype(F32), 0.0).astype(BF)
    map_scr[0:offsets] = map_ref[...]
    slots = map_scr[...]
    pack_ref[2 * rows :] = jnp.where(slots > 256, 256 - slots, slots).astype(F32).astype(BF)


def prep(live, features, cotangent, kernel_map, send_up, send_down, map_rows):
    rows, width = features.shape
    return pl.pallas_call(
        prep_kernel,
        out_shape=(
            jax.ShapeDtypeStruct((2 * rows + map_rows, width), BF),
            jax.ShapeDtypeStruct((send_up.shape[1], width), BF),
            jax.ShapeDtypeStruct((send_up.shape[1], width), BF),
        ),
        in_specs=[SMEM] + [HBM] * 5,
        out_specs=(VMEM,) * 3,
        scratch_shapes=[
            pltpu.VMEM((rows, width), BF),
            pltpu.VMEM((rows, width), BF),
            pltpu.VMEM(kernel_map.shape, jnp.int32),
            pltpu.VMEM(send_up.shape, jnp.int32),
            pltpu.VMEM(send_down.shape, jnp.int32),
            pltpu.VMEM((map_rows, rows), jnp.int32),
            pltpu.SemaphoreType.DMA((5,)),
        ],
        compiler_params=params(PREP_LIMIT),
        name="prep",
    )(live, features, cotangent, kernel_map, send_up, send_down)


def decoded(code):
    code = code.astype(F32).astype(jnp.int32)
    return jnp.where(code < 0, 256 - code, code)


def backward_kernel(group, pack_ref, w_ref, after_ref, own_ref, first_ref, second_ref, token_ref, *scratch):
    maps, chosen, terms, low_ref, high_ref = scratch
    offsets, width, _ = w_ref.shape
    rows = own_ref.shape[0]
    slots = chosen.shape[1]
    maps[...] = decoded(pack_ref[2 * rows :])
    dy = pack_ref[rows : 2 * rows]
    slot_down = lax.broadcasted_iota(jnp.int32, (slots, rows), 0)
    for k in range(offsets):
        at = slice(k % group * rows, (k % group + 1) * rows)
        chosen[k // group, :, at] = (slot_down == maps[k : k + 1, :]).astype(F32).astype(BF)
        back = lax.dot_general(dy, w_ref[k], (((1,), (1,)), ((), ())), preferred_element_type=F32)
        for t, part in enumerate(split(back, 2)):
            terms[k // group, t, at] = part
    for g in range(offsets // group):
        at = 0
        for out in (own_ref, low_ref, high_ref):
            some = chosen[g, at : at + out.shape[0]]
            value = dot(some, terms[g, 0]) + dot(some, terms[g, 1])
            out[...] = value if g == 0 else out[...] + value
            at += out.shape[0]
    first_ref[...], second_ref[...] = turns(high_ref[...], low_ref[...])
    token_ref[...] = jnp.zeros_like(token_ref)


def backward(pack, weights, rows, halo, after):
    offsets, width, _ = weights.shape
    slots = rows + 2 * halo
    group = 3 if offsets % 3 == 0 else 1
    return pl.pallas_call(
        functools.partial(backward_kernel, group),
        out_shape=tuple(jax.ShapeDtypeStruct((n, width), F32) for n in (rows, halo, halo)) + (TOKEN,),
        in_specs=[VMEM, VMEM, ANY],
        out_specs=(VMEM,) * 4,
        scratch_shapes=[
            pltpu.VMEM((pack.shape[0] - 2 * rows, rows), jnp.int32),
            pltpu.VMEM((offsets // group, slots, group * rows), BF),
            pltpu.VMEM((offsets // group, 2, group * rows, width), BF),
            pltpu.VMEM((halo, width), F32),
            pltpu.VMEM((halo, width), F32),
        ],
        compiler_params=params(),
        cost_estimate=cost(),
        name="backward",
    )(pack, weights, after)


def forward_kernel(group, live_ref, pack_ref, halo_ref, w_ref, after_ref, out_ref, token_ref, table, maps, out_acc, picked):
    offsets, width, _ = w_ref.shape
    rows = out_ref.shape[0]
    slots = table.shape[0]
    table[0:rows] = pack_ref[0:rows]
    table[rows:] = halo_ref[...]
    codes = decoded(pack_ref[2 * rows :])
    maps[...] = jnp.transpose(jnp.concatenate([codes] * (maps.shape[1] // codes.shape[0]), axis=0))
    along = lax.broadcasted_iota(jnp.int32, (rows, 128), 1)
    for k in range(offsets):
        column = jnp.broadcast_to(maps[:, k : k + 1], (rows, 128))
        chosen = jnp.concatenate(
            [(along + 128 * b == column).astype(F32).astype(BF) for b in range(slots // 128)], axis=1
        )
        picked[k // group, :, k % group * width : (k % group + 1) * width] = dot(chosen, table[...]).astype(BF)
    for g in range(offsets // group):
        value = dot(picked[g], w_ref[g * group : (g + 1) * group].reshape(group * width, width))
        out_acc[...] = value if g == 0 else out_acc[...] + value
    keep = lax.broadcasted_iota(jnp.int32, (rows, width), 0) < live_ref[0]
    out_ref[...] = jnp.where(keep, out_acc[...], 0.0).astype(BF)
    token_ref[...] = jnp.zeros_like(token_ref)


def forward(live, pack, halo_rows, weights, rows, after):
    offsets, width, _ = weights.shape
    slots = rows + halo_rows.shape[0]
    group = 3 if offsets % 3 == 0 else 1
    return pl.pallas_call(
        functools.partial(forward_kernel, group),
        out_shape=(jax.ShapeDtypeStruct((rows, width), BF), TOKEN),
        in_specs=[SMEM, VMEM, VMEM, VMEM, ANY],
        out_specs=(VMEM, VMEM),
        scratch_shapes=[
            pltpu.VMEM((slots, width), BF),
            pltpu.VMEM((rows, 128), jnp.int32),
            pltpu.VMEM((rows, width), F32),
            pltpu.VMEM((offsets // group, rows, group * width), BF),
        ],
        compiler_params=params(),
        cost_estimate=cost(),
        name="forward",
    )(live, pack, halo_rows, weights, after)


def chosen_slots(maps, s, at, low, high, rows):
    iota = lax.broadcasted_iota(jnp.int32, (high - low, rows), 0) + low
    return (iota == maps[s, pl.ds(at, 1), :]).astype(F32).astype(BF)


def wgrad_own_kernel(sources, *refs):
    packs = refs[:sources]
    picked_ref, dys, maps, tables = refs[sources:]
    count, width, _ = picked_ref.shape
    rows = dys.shape[0] // sources
    for s in range(sources):
        tables[:, s * rows : (s + 1) * rows] = jnp.transpose(packs[s][0:rows])
        dys[s * rows : (s + 1) * rows] = packs[s][rows : 2 * rows]
        maps[s] = decoded(packs[s][2 * rows :])

    for j in range(count):
        for s in range(sources):
            chosen = chosen_slots(maps, s, place()[0] * count + j, 0, rows, rows)
            picked_ref[j, :, s * rows : (s + 1) * rows] = dot(tables[:, s * rows : (s + 1) * rows], chosen).astype(BF)


def wgrad_own(packs, count, rows):
    sources, width = len(packs), packs[0].shape[1]
    return pl.pallas_call(
        functools.partial(wgrad_own_kernel, sources),
        out_shape=(
            jax.ShapeDtypeStruct((count, width, sources * rows), BF),
            jax.ShapeDtypeStruct((sources * rows, width), BF),
            jax.ShapeDtypeStruct((sources, packs[0].shape[0] - 2 * rows, rows), jnp.int32),
        ),
        in_specs=[VMEM] * sources,
        out_specs=(VMEM, VMEM, VMEM),
        scratch_shapes=[pltpu.VMEM((width, sources * rows), BF)],
        compiler_params=params(),
        cost_estimate=cost(),
        name="wgrad_own",
    )(*packs)


def wgrad_kernel(sources, first, picked_ref, dys, maps, *refs):
    halos, (after_ref, keep_ref, send_ref, tables, picked) = refs[:sources], refs[sources:]
    count, half, width = keep_ref.shape
    rows = maps.shape[2]
    far = halos[0].shape[0]
    core = place()[1]
    for s in range(sources):
        tables[:, s * far : (s + 1) * far] = jnp.transpose(halos[s][...])
    for j in range(count):
        for s in range(sources):
            chosen = chosen_slots(maps, s, place()[0] * picked_ref.shape[0] + first + j, rows, rows + far, rows)
            near = picked_ref[first + j, :, s * rows : (s + 1) * rows].astype(F32)
            picked[j, :, s * rows : (s + 1) * rows] = (dot(tables[:, s * far : (s + 1) * far], chosen) + near).astype(BF)
    for j in range(count):
        send_ref[j] = dot(picked[j, pl.ds(pl.multiple_of((1 - core) * half, half), half), :], dys[...])
        keep_ref[j] = dot(picked[j, pl.ds(pl.multiple_of(core * half, half), half), :], dys[...])


def wgrad(picked, dys, maps, halos, first, count, after):
    _, width, columns = picked.shape
    sources = maps.shape[0]
    shape = jax.ShapeDtypeStruct((count, width // 2, width), F32)
    return pl.pallas_call(
        functools.partial(wgrad_kernel, sources, first),
        out_shape=(shape, shape),
        in_specs=[VMEM] * (3 + sources) + [ANY],
        out_specs=(VMEM, VMEM),
        scratch_shapes=[
            pltpu.VMEM((width, sources * halos[0].shape[0]), BF),
            pltpu.VMEM((count, width, columns), BF),
        ],
        compiler_params=params(),
        cost_estimate=cost(),
        name="wgrad",
    )(picked, dys, maps, *halos, after)


def power(exponent):
    value = jnp.ones(exponent.shape, F32)
    size = jnp.abs(exponent)
    for bit in range(7):
        factor = jnp.where(exponent < 0, 0.5 ** (1 << bit), 2.0 ** (1 << bit))
        value = value * jnp.where((size >> bit) & 1 == 1, factor, 1.0)
    return value


def joined_kernel(first_ref, second_ref, pack_ref, out_ref, copy_ref):
    halo = first_ref.shape[0]
    second, first = turns(0, halo)
    out_ref[pl.ds(pl.multiple_of(first, halo), halo)] = first_ref[...]
    out_ref[pl.ds(pl.multiple_of(second, halo), halo)] = second_ref[...]
    copy_ref[...] = pack_ref[...]


def joined(first, second, pack):
    return pl.pallas_call(
        joined_kernel,
        out_shape=(
            jax.ShapeDtypeStruct((2 * first.shape[0], first.shape[1]), BF),
            jax.ShapeDtypeStruct(pack.shape, BF),
        ),
        in_specs=[VMEM] * 3,
        out_specs=(VMEM, VMEM),
        compiler_params=params(),
        cost_estimate=cost(),
        name="joined",
    )(first, second, pack)


def blocks_kernel(keep_ref, got_ref, mine_ref, *refs):
    coded_refs, exponents = refs[:-1], refs[-1]
    count, block, width = mine_ref.shape
    for m in range(len(coded_refs) + 1):
        at = pl.ds(pl.multiple_of((place()[2] ^ m) * block, block), block)
        if m == 0:
            mine_ref[...] = keep_ref[:, at, :] + got_ref[:, at, :]
            continue
        exponents[...] = jnp.zeros_like(exponents)
        for j in range(count):
            value = keep_ref[j, at, :] + got_ref[j, at, :]
            largest = jnp.max(jnp.abs(value), axis=0, keepdims=True)
            exponent = jnp.ceil(jnp.log(jnp.maximum(largest, 2.0**-100)) * (1.0 / math.log(2.0)))
            exponent = jnp.clip(exponent, -100.0, 100.0).astype(jnp.int32) - 15
            exponents[j : j + 1, :] = exponent
            scaled = jnp.round(jnp.clip(value * power(-exponent), -32767.0, 32767.0))
            coded_refs[m - 1][j * block : (j + 1) * block] = scaled.astype(jnp.int32).astype(jnp.int16)
        coded_refs[m - 1][count * block :] = exponents[...].astype(jnp.int16)


def blocks(keep, got, parts):
    count, half, width = keep.shape
    block = half // parts
    extra = -(-count // 16) * 16
    return pl.pallas_call(
        blocks_kernel,
        out_shape=(
            jax.ShapeDtypeStruct((count, block, width), F32),
            *(jax.ShapeDtypeStruct((count * block + extra, width), jnp.int16),) * (parts - 1),
        ),
        in_specs=[VMEM, VMEM],
        out_specs=(VMEM,) * parts,
        scratch_shapes=[pltpu.VMEM((extra, width), jnp.int32)],
        compiler_params=params(),
        cost_estimate=cost(),
        name="blocks",
    )(keep, got)


def total_kernel(scale, mine_ref, *refs):
    *coded_refs, _, _, out_ref = refs
    count, block, width = mine_ref.shape
    powers = [power(ref[count * block :].astype(jnp.int32)) for ref in coded_refs]
    for j in range(count):
        total = mine_ref[j]
        for ref, factor in zip(coded_refs, powers):
            value = ref[j * block : (j + 1) * block].astype(jnp.int32).astype(F32)
            total = total + value * factor[j : j + 1, :]
        out_ref[j] = (total * scale).astype(BF)


def scaled_total(mine, coded, scale, after):
    return pl.pallas_call(
        functools.partial(total_kernel, scale),
        out_shape=jax.ShapeDtypeStruct(mine.shape, BF),
        in_specs=[VMEM] * (len(coded) + 1) + [ANY] * 2,
        out_specs=VMEM,
        compiler_params=params(),
        cost_estimate=cost(),
        name="total",
    )(mine, *coded, *after)


def final_kernel(live_ref, own_ref, first_ref, second_ref, up_ref, down_ref, after_ref, out_ref, token_ref):
    rows, width = own_ref.shape
    halo = up_ref.shape[1]
    total = own_ref[...]
    iota = lax.broadcasted_iota(jnp.int32, (rows, halo), 0)
    chosen = [(iota == index).astype(F32) for index in turns(up_ref[...], down_ref[...])]
    chosen = jnp.concatenate(chosen, axis=1).astype(BF)
    for part in split(jnp.concatenate([first_ref[...], second_ref[...]], axis=0), 3):
        total = total + dot(chosen, part)
    keep = lax.broadcasted_iota(jnp.int32, (rows, width), 0) < live_ref[0]
    out_ref[...] = jnp.where(keep, total, 0.0).astype(BF)
    token_ref[...] = jnp.zeros_like(token_ref)


def final(live, own_grad, first_back, second_back, send_up, send_down, after):
    return pl.pallas_call(
        final_kernel,
        out_shape=(jax.ShapeDtypeStruct(own_grad.shape, BF), TOKEN),
        in_specs=[SMEM] + [VMEM] * 5 + [ANY],
        out_specs=(VMEM, VMEM),
        compiler_params=params(),
        name="final",
    )(live, own_grad, first_back, second_back, send_up, send_down, after)


def stack_kernel(count, *refs):
    at = 0
    for ref in refs[:count]:
        for m in range(ref.shape[0] if len(ref.shape) == 4 else 1):
            refs[-1][at] = ref[m] if len(ref.shape) == 4 else ref[...]
            at += 1


def stack(arrays, after):
    blocks = sum(array.shape[0] if array.ndim == 4 else 1 for array in arrays)
    return pl.pallas_call(
        functools.partial(stack_kernel, len(arrays)),
        out_shape=jax.ShapeDtypeStruct((blocks, *arrays[0].shape[-3:]), BF),
        in_specs=[VMEM] * len(arrays) + [ANY] * len(after),
        out_specs=VMEM,
        compiler_params=params(),
        cost_estimate=cost(),
        name="stack",
    )(*arrays, *after)


def gate_kernel(*refs):
    pass


def gate(value, after):
    return pl.pallas_call(
        gate_kernel,
        out_shape=jax.ShapeDtypeStruct(value.shape, value.dtype),
        in_specs=[ANY] * (1 + len(after)),
        out_specs=ANY,
        input_output_aliases={0: 0},
        compiler_params=params(),
        cost_estimate=cost(),
        name="gate",
    )(value, *after)


def assemble_kernel(marks, parts, groups, *refs):
    out_ref, sems = refs[-2:]
    offsets = out_ref.shape[0]
    _, count, block, _ = refs[0].shape
    short = offsets - (groups - 1) * count

    def each(act):
        for index, (o, sources) in enumerate(marks):
            for part, (m, mask) in enumerate(sources):
                group = place()[0] ^ m
                row = pl.multiple_of(((place()[1] ^ o) * parts + (place()[2] ^ mask)) * block, block)
                source = refs[index].at[part]

                def copy(lo, hi, sem):
                    target = out_ref.at[pl.ds(group * count + lo, hi - lo), pl.ds(row, block)]
                    return pltpu.make_async_copy(source.at[lo:hi], target, sems.at[index, part, sem])

                getattr(copy(0, short, 0), act)()
                if short < count:
                    pl.when(group < groups - 1)(getattr(copy(short, count, 1), act))

    each("start")
    each("wait")


def assemble(pieces, marks, parts, groups, offsets, width, after, base=()):
    most = max(piece.shape[0] for piece in pieces)
    return pl.pallas_call(
        functools.partial(assemble_kernel, marks, parts, groups),
        out_shape=jax.ShapeDtypeStruct((offsets, width, width), BF),
        in_specs=[ANY] * (len(pieces) + len(after) + len(base)),
        out_specs=ANY,
        scratch_shapes=[pltpu.SemaphoreType.DMA((len(pieces), most, 2))],
        input_output_aliases={len(pieces) + len(after): 0} if base else {},
        compiler_params=params(),
        cost_estimate=cost(),
        name="assemble",
    )(*pieces, *after, *base)


def assemble_plain(pieces, marks, parts, groups, offsets, width):
    _, count, block, _ = pieces[0].shape
    total = jnp.zeros((groups * count, width, width), BF)
    for piece, (o, sources) in zip(pieces, marks):
        for part, (m, mask) in enumerate(sources):
            row = ((place()[1] ^ o) * parts + (place()[2] ^ mask)) * block
            total = lax.dynamic_update_slice(total, piece[part], ((place()[0] ^ m) * count, row, 0))
    return total[:offsets]


def swap(value, axis, mask):
    return lax.ppermute(value, axis, [(i, i ^ mask) for i in range(lax.axis_size(axis))])


def met(value, turn):
    count = lax.axis_size("space")
    starts = range(turn, count - 1, 2)
    return lax.ppermute(value, "space", [(i, i + 1) for i in starts] + [(i + 1, i) for i in starts])


def shards(features, weights, cotangent, kernel_map, live, send_up, send_down):
    rows, width = features.shape
    offsets, halo = weights.shape[0], send_up.shape[1]
    groups = lax.axis_size("dp") // 2
    parts = lax.axis_size("space")
    count = -(-offsets // groups)
    map_rows = -(-(groups * count) // 16) * 16

    pack, first_rows, second_rows = prep(live, features, cotangent, kernel_map, send_up, send_down, map_rows)
    packs = [pack] + [swap(pack, "dp", 2 * m) for m in range(1, groups)]
    halo_rows, pack = joined(met(first_rows, 0), met(second_rows, 1), pack)
    packs[0] = pack
    halos = [halo_rows] + [swap(halo_rows, "dp", 2 * m) for m in range(1, groups)]
    picked, dys, maps = wgrad_own(packs, count, rows)
    keep, send = wgrad(picked, dys, maps, halos, 0, count, dys)
    mine, *coded = blocks(keep, swap(send, "dp", 1), parts)
    own_grad, first_grad, second_grad, token = backward(pack, weights, rows, halo, mine)
    first_back, second_back = met(first_grad, 0), met(second_grad, 1)
    scale = 1.0 / math.sqrt(rows * lax.axis_size("dp") * parts)
    rounded = scaled_total(mine, [swap(block, "space", m + 1) for m, block in enumerate(coded)], scale, (token, token))
    out_features, token = forward(live, pack, halo_rows, weights, rows, rounded)

    along = [swap(rounded, "space", m) for m in range(1, parts)]
    across = {m: swap(rounded, "dp", 2 * m) for m in reversed(range(1, groups))}
    lines = gate(stack(along, [token]), list(across.values()))
    far = {m: swap(lines, "dp", 2 * m) for m in reversed(range(1, groups))}
    line_masks = range(1, parts)
    near = stack([rounded, lines], [])
    sides = stack([across[m] for m in range(1, groups)], [])
    near_marks = [(0, mask) for mask in range(parts)]
    side_marks = [(m, 0) for m in range(1, groups)]
    pieces = [near, swap(near, "dp", 1), sides, swap(sides, "dp", 1)]
    marks = [(0, near_marks), (1, near_marks), (0, side_marks), (1, side_marks)]
    grad_features, token = final(live, own_grad, first_back, second_back, send_up, send_down, lines)
    dense = rounded.shape[1] % 16 == 0 and groups * count - offsets < count
    sizes = (parts, groups, offsets, width)
    first = ()
    for m in range(1, groups):
        pieces += [far[m], swap(far[m], "dp", 1)]
        marks += [(o, [(m, mask) for mask in line_masks]) for o in range(2)]
    if dense:
        grad_weights = assemble(pieces, marks, *sizes, (token,), first)
    else:
        grad_weights = assemble_plain(pieces, marks, *sizes)
    return (out_features, grad_features, grad_weights)


def solution(mesh):
    placed = (
        P(("dp", "space"), None),
        P(),
        P(("dp", "space"), None),
        P(None, ("dp", "space")),
        P(("dp", "space")),
        P(("dp", "space"), None),
        P(("dp", "space"), None),
    )
    return jax.shard_map(
        shards,
        mesh=mesh,
        in_specs=placed,
        out_specs=(P(("dp", "space"), None), P(("dp", "space"), None), P()),
        check_vma=False,
    )
```

```python
import functools
import math

import jax
import jax.numpy as jnp
from jax import lax
from jax.experimental import pallas as pl
from jax.experimental.pallas import tpu as pltpu
from jax.sharding import PartitionSpec as P

BF = jnp.bfloat16
F32 = jnp.float32
VMEM_LIMIT = 32 * 1024 * 1024
PREP_LIMIT = 60 * 1024 * 1024
VMEM = pl.BlockSpec(memory_space=pltpu.VMEM)
SMEM = pl.BlockSpec(memory_space=pltpu.SMEM)
ANY = pl.BlockSpec(memory_space=pl.ANY)
HBM = pl.BlockSpec(memory_space=pltpu.HBM)
TOKEN = jax.ShapeDtypeStruct((8, 128), F32)


def params(limit=VMEM_LIMIT):
    return pltpu.CompilerParams(vmem_limit_bytes=limit)


def cost():
    return pl.CostEstimate(flops=100_000_000, bytes_accessed=100_000, transcendentals=0)


def dot(a, b):
    return jnp.dot(a, b, preferred_element_type=F32)


def split(value, terms):
    parts = []
    for _ in range(terms):
        part = value.astype(BF)
        parts.append(part)
        value = value - part.astype(F32)
    return parts


def place():
    dp = lax.axis_index("dp")
    return dp // 2, lax.rem(dp, 2), lax.axis_index("space")


def turns(up, down):
    even = lax.rem(place()[2], 2) == 0
    return jnp.where(even, up, down), jnp.where(even, down, up)


def prep_kernel(live_ref, x_hbm, dy_hbm, map_hbm, up_hbm, down_hbm, pack_ref, first_ref, second_ref, *scratch):
    x_ref, dy_ref, map_ref, up_ref, down_ref, map_scr, sems = scratch
    sources = (x_hbm, dy_hbm, map_hbm, up_hbm, down_hbm)
    targets = (x_ref, dy_ref, map_ref, up_ref, down_ref)
    copies = [pltpu.make_async_copy(a, b, sems.at[i]) for i, (a, b) in enumerate(zip(sources, targets))]
    for copy in copies:
        copy.start()
    rows, width = x_ref.shape
    offsets = map_ref.shape[0]
    halo = up_ref.shape[1]
    keep = lax.broadcasted_iota(jnp.int32, (rows, width), 0) < live_ref[0]
    map_scr[...] = jnp.full(map_scr.shape, rows + 2 * halo, jnp.int32)
    for copy in copies:
        copy.wait()
    x_live = jnp.where(keep, x_ref[...].astype(F32), 0.0).astype(BF)
    pack_ref[0:rows] = x_live
    iota = lax.broadcasted_iota(jnp.int32, (rows, halo), 0)
    for index, picked_ref in zip(turns(up_ref[...], down_ref[...]), (first_ref, second_ref)):
        chosen = (iota == index).astype(F32).astype(BF)
        picked_ref[...] = lax.dot_general(chosen, x_live, (((0,), (0,)), ((), ())), preferred_element_type=F32).astype(BF)
    pack_ref[rows : 2 * rows] = jnp.where(keep, dy_ref[...].astype(F32), 0.0).astype(BF)
    map_scr[0:offsets] = map_ref[...]
    slots = map_scr[...]
    pack_ref[2 * rows :] = jnp.where(slots > 256, 256 - slots, slots).astype(F32).astype(BF)


def prep(live, features, cotangent, kernel_map, send_up, send_down, map_rows):
    rows, width = features.shape
    return pl.pallas_call(
        prep_kernel,
        out_shape=(
            jax.ShapeDtypeStruct((2 * rows + map_rows, width), BF),
            jax.ShapeDtypeStruct((send_up.shape[1], width), BF),
            jax.ShapeDtypeStruct((send_up.shape[1], width), BF),
        ),
        in_specs=[SMEM] + [HBM] * 5,
        out_specs=(VMEM,) * 3,
        scratch_shapes=[
            pltpu.VMEM((rows, width), BF),
            pltpu.VMEM((rows, width), BF),
            pltpu.VMEM(kernel_map.shape, jnp.int32),
            pltpu.VMEM(send_up.shape, jnp.int32),
            pltpu.VMEM(send_down.shape, jnp.int32),
            pltpu.VMEM((map_rows, rows), jnp.int32),
            pltpu.SemaphoreType.DMA((5,)),
        ],
        compiler_params=params(PREP_LIMIT),
        name="prep",
    )(live, features, cotangent, kernel_map, send_up, send_down)


def decoded(code):
    code = code.astype(F32).astype(jnp.int32)
    return jnp.where(code < 0, 256 - code, code)


def backward_kernel(group, pack_ref, w_ref, after_ref, own_ref, first_ref, second_ref, token_ref, *scratch):
    maps, chosen, terms, low_ref, high_ref = scratch
    offsets, width, _ = w_ref.shape
    rows = own_ref.shape[0]
    slots = chosen.shape[1]
    maps[...] = decoded(pack_ref[2 * rows :])
    dy = pack_ref[rows : 2 * rows]
    slot_down = lax.broadcasted_iota(jnp.int32, (slots, rows), 0)
    for k in range(offsets):
        at = slice(k % group * rows, (k % group + 1) * rows)
        chosen[k // group, :, at] = (slot_down == maps[k : k + 1, :]).astype(F32).astype(BF)
        back = lax.dot_general(dy, w_ref[k], (((1,), (1,)), ((), ())), preferred_element_type=F32)
        for t, part in enumerate(split(back, 2)):
            terms[k // group, t, at] = part
    for g in range(offsets // group):
        at = 0
        for out in (own_ref, low_ref, high_ref):
            some = chosen[g, at : at + out.shape[0]]
            value = dot(some, terms[g, 0]) + dot(some, terms[g, 1])
            out[...] = value if g == 0 else out[...] + value
            at += out.shape[0]
    first_ref[...], second_ref[...] = turns(high_ref[...], low_ref[...])
    token_ref[...] = jnp.zeros_like(token_ref)


def backward(pack, weights, rows, halo, after):
    offsets, width, _ = weights.shape
    slots = rows + 2 * halo
    group = 3 if offsets % 3 == 0 else 1
    return pl.pallas_call(
        functools.partial(backward_kernel, group),
        out_shape=tuple(jax.ShapeDtypeStruct((n, width), F32) for n in (rows, halo, halo)) + (TOKEN,),
        in_specs=[VMEM, VMEM, ANY],
        out_specs=(VMEM,) * 4,
        scratch_shapes=[
            pltpu.VMEM((pack.shape[0] - 2 * rows, rows), jnp.int32),
            pltpu.VMEM((offsets // group, slots, group * rows), BF),
            pltpu.VMEM((offsets // group, 2, group * rows, width), BF),
            pltpu.VMEM((halo, width), F32),
            pltpu.VMEM((halo, width), F32),
        ],
        compiler_params=params(),
        cost_estimate=cost(),
        name="backward",
    )(pack, weights, after)


def forward_kernel(group, live_ref, pack_ref, halo_ref, w_ref, after_ref, out_ref, token_ref, table, maps, out_acc, picked):
    offsets, width, _ = w_ref.shape
    rows = out_ref.shape[0]
    slots = table.shape[0]
    table[0:rows] = pack_ref[0:rows]
    table[rows:] = halo_ref[...]
    codes = decoded(pack_ref[2 * rows :])
    maps[...] = jnp.transpose(jnp.concatenate([codes] * (maps.shape[1] // codes.shape[0]), axis=0))
    along = lax.broadcasted_iota(jnp.int32, (rows, 128), 1)
    for k in range(offsets):
        column = jnp.broadcast_to(maps[:, k : k + 1], (rows, 128))
        chosen = jnp.concatenate(
            [(along + 128 * b == column).astype(F32).astype(BF) for b in range(slots // 128)], axis=1
        )
        picked[k // group, :, k % group * width : (k % group + 1) * width] = dot(chosen, table[...]).astype(BF)
    for g in range(offsets // group):
        value = dot(picked[g], w_ref[g * group : (g + 1) * group].reshape(group * width, width))
        out_acc[...] = value if g == 0 else out_acc[...] + value
    keep = lax.broadcasted_iota(jnp.int32, (rows, width), 0) < live_ref[0]
    out_ref[...] = jnp.where(keep, out_acc[...], 0.0).astype(BF)
    token_ref[...] = jnp.zeros_like(token_ref)


def forward(live, pack, halo_rows, weights, rows, after):
    offsets, width, _ = weights.shape
    slots = rows + halo_rows.shape[0]
    group = 3 if offsets % 3 == 0 else 1
    return pl.pallas_call(
        functools.partial(forward_kernel, group),
        out_shape=(jax.ShapeDtypeStruct((rows, width), BF), TOKEN),
        in_specs=[SMEM, VMEM, VMEM, VMEM, ANY],
        out_specs=(VMEM, VMEM),
        scratch_shapes=[
            pltpu.VMEM((slots, width), BF),
            pltpu.VMEM((rows, 128), jnp.int32),
            pltpu.VMEM((rows, width), F32),
            pltpu.VMEM((offsets // group, rows, group * width), BF),
        ],
        compiler_params=params(),
        cost_estimate=cost(),
        name="forward",
    )(live, pack, halo_rows, weights, after)


def chosen_slots(maps, s, at, low, high, rows):
    iota = lax.broadcasted_iota(jnp.int32, (high - low, rows), 0) + low
    return (iota == maps[s, pl.ds(at, 1), :]).astype(F32).astype(BF)


def wgrad_own_kernel(sources, *refs):
    packs = refs[:sources]
    picked_ref, dys, maps, tables = refs[sources:]
    count, width, _ = picked_ref.shape
    rows = dys.shape[0] // sources
    for s in range(sources):
        tables[:, s * rows : (s + 1) * rows] = jnp.transpose(packs[s][0:rows])
        dys[s * rows : (s + 1) * rows] = packs[s][rows : 2 * rows]
        maps[s] = decoded(packs[s][2 * rows :])

    for j in range(count):
        for s in range(sources):
            chosen = chosen_slots(maps, s, place()[0] * count + j, 0, rows, rows)
            picked_ref[j, :, s * rows : (s + 1) * rows] = dot(tables[:, s * rows : (s + 1) * rows], chosen).astype(BF)


def wgrad_own(packs, count, rows):
    sources, width = len(packs), packs[0].shape[1]
    return pl.pallas_call(
        functools.partial(wgrad_own_kernel, sources),
        out_shape=(
            jax.ShapeDtypeStruct((count, width, sources * rows), BF),
            jax.ShapeDtypeStruct((sources * rows, width), BF),
            jax.ShapeDtypeStruct((sources, packs[0].shape[0] - 2 * rows, rows), jnp.int32),
        ),
        in_specs=[VMEM] * sources,
        out_specs=(VMEM, VMEM, VMEM),
        scratch_shapes=[pltpu.VMEM((width, sources * rows), BF)],
        compiler_params=params(),
        cost_estimate=cost(),
        name="wgrad_own",
    )(*packs)


def wgrad_kernel(sources, first, picked_ref, dys, maps, *refs):
    halos, (after_ref, keep_ref, send_ref, tables, picked) = refs[:sources], refs[sources:]
    count, half, width = keep_ref.shape
    rows = maps.shape[2]
    far = halos[0].shape[0]
    core = place()[1]
    for s in range(sources):
        tables[:, s * far : (s + 1) * far] = jnp.transpose(halos[s][...])
    for j in range(count):
        for s in range(sources):
            chosen = chosen_slots(maps, s, place()[0] * picked_ref.shape[0] + first + j, rows, rows + far, rows)
            near = picked_ref[first + j, :, s * rows : (s + 1) * rows].astype(F32)
            picked[j, :, s * rows : (s + 1) * rows] = (dot(tables[:, s * far : (s + 1) * far], chosen) + near).astype(BF)
    for j in range(count):
        send_ref[j] = dot(picked[j, pl.ds(pl.multiple_of((1 - core) * half, half), half), :], dys[...])
        keep_ref[j] = dot(picked[j, pl.ds(pl.multiple_of(core * half, half), half), :], dys[...])


def wgrad(picked, dys, maps, halos, first, count, after):
    _, width, columns = picked.shape
    sources = maps.shape[0]
    shape = jax.ShapeDtypeStruct((count, width // 2, width), F32)
    return pl.pallas_call(
        functools.partial(wgrad_kernel, sources, first),
        out_shape=(shape, shape),
        in_specs=[VMEM] * (3 + sources) + [ANY],
        out_specs=(VMEM, VMEM),
        scratch_shapes=[
            pltpu.VMEM((width, sources * halos[0].shape[0]), BF),
            pltpu.VMEM((count, width, columns), BF),
        ],
        compiler_params=params(),
        cost_estimate=cost(),
        name="wgrad",
    )(picked, dys, maps, *halos, after)


def power(exponent):
    value = jnp.ones(exponent.shape, F32)
    size = jnp.abs(exponent)
    for bit in range(7):
        factor = jnp.where(exponent < 0, 0.5 ** (1 << bit), 2.0 ** (1 << bit))
        value = value * jnp.where((size >> bit) & 1 == 1, factor, 1.0)
    return value


def joined_kernel(first_ref, second_ref, pack_ref, out_ref, copy_ref):
    halo = first_ref.shape[0]
    second, first = turns(0, halo)
    out_ref[pl.ds(pl.multiple_of(first, halo), halo)] = first_ref[...]
    out_ref[pl.ds(pl.multiple_of(second, halo), halo)] = second_ref[...]
    copy_ref[...] = pack_ref[...]


def joined(first, second, pack):
    return pl.pallas_call(
        joined_kernel,
        out_shape=(
            jax.ShapeDtypeStruct((2 * first.shape[0], first.shape[1]), BF),
            jax.ShapeDtypeStruct(pack.shape, BF),
        ),
        in_specs=[VMEM] * 3,
        out_specs=(VMEM, VMEM),
        compiler_params=params(),
        cost_estimate=cost(),
        name="joined",
    )(first, second, pack)


def blocks_kernel(keep_ref, got_ref, mine_ref, *refs):
    coded_refs, exponents = refs[:-1], refs[-1]
    count, block, width = mine_ref.shape
    for m in range(len(coded_refs) + 1):
        at = pl.ds(pl.multiple_of((place()[2] ^ m) * block, block), block)
        if m == 0:
            mine_ref[...] = keep_ref[:, at, :] + got_ref[:, at, :]
            continue
        exponents[...] = jnp.zeros_like(exponents)
        for j in range(count):
            value = keep_ref[j, at, :] + got_ref[j, at, :]
            largest = jnp.max(jnp.abs(value), axis=0, keepdims=True)
            exponent = jnp.ceil(jnp.log(jnp.maximum(largest, 2.0**-100)) * (1.0 / math.log(2.0)))
            exponent = jnp.clip(exponent, -100.0, 100.0).astype(jnp.int32) - 15
            exponents[j : j + 1, :] = exponent
            scaled = jnp.round(jnp.clip(value * power(-exponent), -32767.0, 32767.0))
            coded_refs[m - 1][j * block : (j + 1) * block] = scaled.astype(jnp.int32).astype(jnp.int16)
        coded_refs[m - 1][count * block :] = exponents[...].astype(jnp.int16)


def blocks(keep, got, parts):
    count, half, width = keep.shape
    block = half // parts
    extra = -(-count // 16) * 16
    return pl.pallas_call(
        blocks_kernel,
        out_shape=(
            jax.ShapeDtypeStruct((count, block, width), F32),
            *(jax.ShapeDtypeStruct((count * block + extra, width), jnp.int16),) * (parts - 1),
        ),
        in_specs=[VMEM, VMEM],
        out_specs=(VMEM,) * parts,
        scratch_shapes=[pltpu.VMEM((extra, width), jnp.int32)],
        compiler_params=params(),
        cost_estimate=cost(),
        name="blocks",
    )(keep, got)


def total_kernel(scale, mine_ref, *refs):
    *coded_refs, _, _, out_ref = refs
    count, block, width = mine_ref.shape
    powers = [power(ref[count * block :].astype(jnp.int32)) for ref in coded_refs]
    for j in range(count):
        total = mine_ref[j]
        for ref, factor in zip(coded_refs, powers):
            value = ref[j * block : (j + 1) * block].astype(jnp.int32).astype(F32)
            total = total + value * factor[j : j + 1, :]
        out_ref[j] = (total * scale).astype(BF)


def scaled_total(mine, coded, scale, after):
    return pl.pallas_call(
        functools.partial(total_kernel, scale),
        out_shape=jax.ShapeDtypeStruct(mine.shape, BF),
        in_specs=[VMEM] * (len(coded) + 1) + [ANY] * 2,
        out_specs=VMEM,
        compiler_params=params(),
        cost_estimate=cost(),
        name="total",
    )(mine, *coded, *after)


def final_kernel(live_ref, own_ref, first_ref, second_ref, up_ref, down_ref, after_ref, out_ref, token_ref):
    rows, width = own_ref.shape
    halo = up_ref.shape[1]
    total = own_ref[...]
    iota = lax.broadcasted_iota(jnp.int32, (rows, halo), 0)
    chosen = [(iota == index).astype(F32) for index in turns(up_ref[...], down_ref[...])]
    chosen = jnp.concatenate(chosen, axis=1).astype(BF)
    for part in split(jnp.concatenate([first_ref[...], second_ref[...]], axis=0), 3):
        total = total + dot(chosen, part)
    keep = lax.broadcasted_iota(jnp.int32, (rows, width), 0) < live_ref[0]
    out_ref[...] = jnp.where(keep, total, 0.0).astype(BF)
    token_ref[...] = jnp.zeros_like(token_ref)


def final(live, own_grad, first_back, second_back, send_up, send_down, after):
    return pl.pallas_call(
        final_kernel,
        out_shape=(jax.ShapeDtypeStruct(own_grad.shape, BF), TOKEN),
        in_specs=[SMEM] + [VMEM] * 5 + [ANY],
        out_specs=(VMEM, VMEM),
        compiler_params=params(),
        name="final",
    )(live, own_grad, first_back, second_back, send_up, send_down, after)


def stack_kernel(count, *refs):
    at = 0
    for ref in refs[:count]:
        for m in range(ref.shape[0] if len(ref.shape) == 4 else 1):
            refs[-1][at] = ref[m] if len(ref.shape) == 4 else ref[...]
            at += 1


def stack(arrays, after):
    blocks = sum(array.shape[0] if array.ndim == 4 else 1 for array in arrays)
    return pl.pallas_call(
        functools.partial(stack_kernel, len(arrays)),
        out_shape=jax.ShapeDtypeStruct((blocks, *arrays[0].shape[-3:]), BF),
        in_specs=[VMEM] * len(arrays) + [ANY] * len(after),
        out_specs=VMEM,
        compiler_params=params(),
        cost_estimate=cost(),
        name="stack",
    )(*arrays, *after)


def gate_kernel(*refs):
    pass


def gate(value, after):
    return pl.pallas_call(
        gate_kernel,
        out_shape=jax.ShapeDtypeStruct(value.shape, value.dtype),
        in_specs=[ANY] * (1 + len(after)),
        out_specs=ANY,
        input_output_aliases={0: 0},
        compiler_params=params(),
        cost_estimate=cost(),
        name="gate",
    )(value, *after)


def assemble_kernel(marks, parts, groups, *refs):
    out_ref, sems = refs[-2:]
    offsets = out_ref.shape[0]
    _, count, block, _ = refs[0].shape
    short = offsets - (groups - 1) * count

    def each(act):
        for index, (o, sources) in enumerate(marks):
            for part, (m, mask) in enumerate(sources):
                group = place()[0] ^ m
                row = pl.multiple_of(((place()[1] ^ o) * parts + (place()[2] ^ mask)) * block, block)
                source = refs[index].at[part]

                def copy(lo, hi, sem):
                    target = out_ref.at[pl.ds(group * count + lo, hi - lo), pl.ds(row, block)]
                    return pltpu.make_async_copy(source.at[lo:hi], target, sems.at[index, part, sem])

                getattr(copy(0, short, 0), act)()
                if short < count:
                    pl.when(group < groups - 1)(getattr(copy(short, count, 1), act))

    each("start")
    each("wait")


def assemble(pieces, marks, parts, groups, offsets, width, after, base=()):
    most = max(piece.shape[0] for piece in pieces)
    return pl.pallas_call(
        functools.partial(assemble_kernel, marks, parts, groups),
        out_shape=jax.ShapeDtypeStruct((offsets, width, width), BF),
        in_specs=[ANY] * (len(pieces) + len(after)) + [HBM] * len(base),
        out_specs=HBM,
        scratch_shapes=[pltpu.SemaphoreType.DMA((len(pieces), most, 2))],
        input_output_aliases={len(pieces) + len(after): 0} if base else {},
        compiler_params=params(),
        cost_estimate=cost(),
        name="assemble",
    )(*pieces, *after, *base)


def assemble_plain(pieces, marks, parts, groups, offsets, width):
    _, count, block, _ = pieces[0].shape
    total = jnp.zeros((groups * count, width, width), BF)
    for piece, (o, sources) in zip(pieces, marks):
        for part, (m, mask) in enumerate(sources):
            row = ((place()[1] ^ o) * parts + (place()[2] ^ mask)) * block
            total = lax.dynamic_update_slice(total, piece[part], ((place()[0] ^ m) * count, row, 0))
    return total[:offsets]


def swap(value, axis, mask):
    return lax.ppermute(value, axis, [(i, i ^ mask) for i in range(lax.axis_size(axis))])


def met(value, turn):
    count = lax.axis_size("space")
    starts = range(turn, count - 1, 2)
    return lax.ppermute(value, "space", [(i, i + 1) for i in starts] + [(i + 1, i) for i in starts])


def shards(features, weights, cotangent, kernel_map, live, send_up, send_down):
    rows, width = features.shape
    offsets, halo = weights.shape[0], send_up.shape[1]
    groups = lax.axis_size("dp") // 2
    parts = lax.axis_size("space")
    count = -(-offsets // groups)
    map_rows = -(-(groups * count) // 16) * 16

    pack, first_rows, second_rows = prep(live, features, cotangent, kernel_map, send_up, send_down, map_rows)
    packs = [pack] + [swap(pack, "dp", 2 * m) for m in range(1, groups)]
    halo_rows, pack = joined(met(first_rows, 0), met(second_rows, 1), pack)
    packs[0] = pack
    halos = [halo_rows] + [swap(halo_rows, "dp", 2 * m) for m in range(1, groups)]
    picked, dys, maps = wgrad_own(packs, count, rows)
    keep, send = wgrad(picked, dys, maps, halos, 0, count, dys)
    mine, *coded = blocks(keep, swap(send, "dp", 1), parts)
    own_grad, first_grad, second_grad, token = backward(pack, weights, rows, halo, mine)
    first_back, second_back = met(first_grad, 0), met(second_grad, 1)
    scale = 1.0 / math.sqrt(rows * lax.axis_size("dp") * parts)
    rounded = scaled_total(mine, [swap(block, "space", m + 1) for m, block in enumerate(coded)], scale, (token, token))
    out_features, token = forward(live, pack, halo_rows, weights, rows, rounded)

    along = [swap(rounded, "space", m) for m in range(1, parts)]
    across = {m: swap(rounded, "dp", 2 * m) for m in range(1, groups)}
    lines = gate(stack(along, [token]), list(across.values()))
    far = {m: swap(lines, "dp", 2 * m) for m in range(1, groups)}
    line_masks = range(1, parts)
    grad_features, token = final(live, own_grad, first_back, second_back, send_up, send_down, lines)
    near = stack([rounded, lines], [token])
    sides = stack([across[m] for m in range(1, groups)], [])
    near_marks = [(0, mask) for mask in range(parts)]
    side_marks = [(m, 0) for m in range(1, groups)]
    pieces = [near, swap(near, "dp", 1), sides, swap(sides, "dp", 1)]
    marks = [(0, near_marks), (1, near_marks), (0, side_marks), (1, side_marks)]
    dense = rounded.shape[1] % 16 == 0 and groups * count - offsets < count
    sizes = (parts, groups, offsets, width)
    first = ()
    if dense:
        first = (assemble(pieces, marks, *sizes, ()),)
        pieces, marks = [], []
        pass
    for m in range(1, groups):
        pieces += [far[m], swap(far[m], "dp", 1)]
        marks += [(o, [(m, mask) for mask in line_masks]) for o in range(2)]
    if dense:
        grad_weights = assemble(pieces, marks, *sizes, (token,), first)
    else:
        grad_weights = assemble_plain(pieces, marks, *sizes)
    return (out_features, grad_features, grad_weights)


def solution(mesh):
    placed = (
        P(("dp", "space"), None),
        P(),
        P(("dp", "space"), None),
        P(None, ("dp", "space")),
        P(("dp", "space")),
        P(("dp", "space"), None),
        P(("dp", "space"), None),
    )
    return jax.shard_map(
        shards,
        mesh=mesh,
        in_specs=placed,
        out_specs=(P(("dp", "space"), None), P(("dp", "space"), None), P()),
        check_vma=False,
    )
```

```python
import functools
import math

import jax
import jax.numpy as jnp
from jax import lax
from jax.experimental import pallas as pl
from jax.experimental.pallas import tpu as pltpu
from jax.sharding import PartitionSpec as P

BF = jnp.bfloat16
F32 = jnp.float32
VMEM_LIMIT = 32 * 1024 * 1024
PREP_LIMIT = 60 * 1024 * 1024
VMEM = pl.BlockSpec(memory_space=pltpu.VMEM)
ANY = pl.BlockSpec(memory_space=pl.ANY)
HBM = pl.BlockSpec(memory_space=pltpu.HBM)
TOKEN = jax.ShapeDtypeStruct((8, 128), F32)


def params(limit=VMEM_LIMIT):
    return pltpu.CompilerParams(vmem_limit_bytes=limit)


def cost():
    return pl.CostEstimate(flops=100_000_000, bytes_accessed=100_000, transcendentals=0)


def dot(a, b):
    return jnp.dot(a, b, preferred_element_type=F32)


def split(value, terms):
    parts = []
    for _ in range(terms):
        part = value.astype(BF)
        parts.append(part)
        value = value - part.astype(F32)
    return parts


def place():
    dp = lax.axis_index("dp")
    return dp // 2, lax.rem(dp, 2), lax.axis_index("space")


def turns(up, down):
    even = lax.rem(place()[2], 2) == 0
    return jnp.where(even, up, down), jnp.where(even, down, up)


def live_rows(maps, offsets, width, zero_slot):
    rows = maps.shape[1]
    centre = jnp.transpose(jnp.broadcast_to(maps[offsets // 2 : offsets // 2 + 1, :], (128, rows)))
    return jnp.concatenate([centre] * (width // 128), axis=1) != zero_slot


def prep_kernel(x_hbm, dy_hbm, map_hbm, up_hbm, down_hbm, pack_ref, first_ref, second_ref, *refs):
    part_refs, (x_ref, dy_ref, map_ref, up_ref, down_ref, map_scr, turned, sems) = refs[:-8], refs[-8:]
    sources = (x_hbm, dy_hbm, map_hbm, up_hbm, down_hbm)
    targets = (x_ref, dy_ref, map_ref, up_ref, down_ref)
    copies = [pltpu.make_async_copy(a, b, sems.at[i]) for i, (a, b) in enumerate(zip(sources, targets))]
    for copy in copies:
        copy.start()
    rows, width = x_ref.shape
    offsets = map_ref.shape[0]
    halo = up_ref.shape[1]
    zero_slot = rows + 2 * halo
    map_scr[...] = jnp.full(map_scr.shape, zero_slot, jnp.int32)
    for copy in copies:
        copy.wait()
    keep = live_rows(map_ref[...], offsets, width, zero_slot)
    x_live = jnp.where(keep, x_ref[...].astype(F32), 0.0).astype(BF)
    pack_ref[0:rows] = x_live
    iota = lax.broadcasted_iota(jnp.int32, (rows, halo), 0)
    for index, picked_ref in zip(turns(up_ref[...], down_ref[...]), (first_ref, second_ref)):
        chosen = (iota == index).astype(F32).astype(BF)
        picked_ref[...] = lax.dot_general(chosen, x_live, (((0,), (0,)), ((), ())), preferred_element_type=F32).astype(BF)
    pack_ref[rows : 2 * rows] = jnp.where(keep, dy_ref[...].astype(F32), 0.0).astype(BF)
    map_scr[0:offsets] = map_ref[...]
    slots = map_scr[...]
    pack_ref[2 * rows :] = jnp.where(slots > 256, 256 - slots, slots).astype(F32).astype(BF)
    turned[...] = jnp.transpose(x_live)
    for m, part_ref in enumerate(part_refs):
        slab = part_ref.shape[0] - (pack_ref.shape[0] - rows)
        part_ref[0:slab] = turned[pl.ds(pl.multiple_of((place()[0] ^ (m + 1)) * slab, slab), slab), :]
        part_ref[slab:] = pack_ref[rows:]


def prep(features, cotangent, kernel_map, send_up, send_down, map_rows, groups):
    rows, width = features.shape
    return pl.pallas_call(
        prep_kernel,
        out_shape=(
            jax.ShapeDtypeStruct((2 * rows + map_rows, width), BF),
            jax.ShapeDtypeStruct((send_up.shape[1], width), BF),
            jax.ShapeDtypeStruct((send_up.shape[1], width), BF),
            *(jax.ShapeDtypeStruct((width // groups + rows + map_rows, rows), BF),) * (groups - 1),
        ),
        in_specs=[HBM] * 5,
        out_specs=(VMEM,) * (2 + groups),
        scratch_shapes=[
            pltpu.VMEM((rows, width), BF),
            pltpu.VMEM((rows, width), BF),
            pltpu.VMEM(kernel_map.shape, jnp.int32),
            pltpu.VMEM(send_up.shape, jnp.int32),
            pltpu.VMEM(send_down.shape, jnp.int32),
            pltpu.VMEM((map_rows, rows), jnp.int32),
            pltpu.VMEM((width, rows), BF),
            pltpu.SemaphoreType.DMA((5,)),
        ],
        compiler_params=params(PREP_LIMIT),
        name="prep",
    )(features, cotangent, kernel_map, send_up, send_down)


def decoded(code):
    code = code.astype(F32).astype(jnp.int32)
    return jnp.where(code < 0, 256 - code, code)


def backward_kernel(group, pack_ref, w_ref, after_ref, own_ref, first_ref, second_ref, token_ref, *scratch):
    maps, chosen, terms, low_ref, high_ref = scratch
    offsets, width, _ = w_ref.shape
    rows = own_ref.shape[0]
    slots = chosen.shape[1]
    maps[...] = decoded(pack_ref[2 * rows :])
    dy = pack_ref[rows : 2 * rows]
    slot_down = lax.broadcasted_iota(jnp.int32, (slots, rows), 0)
    for k in range(offsets):
        at = slice(k % group * rows, (k % group + 1) * rows)
        chosen[k // group, :, at] = (slot_down == maps[k : k + 1, :]).astype(F32).astype(BF)
        back = lax.dot_general(dy, w_ref[k], (((1,), (1,)), ((), ())), preferred_element_type=F32)
        for t, part in enumerate(split(back, 2)):
            terms[k // group, t, at] = part
    for g in range(offsets // group):
        at = 0
        for out in (own_ref, low_ref, high_ref):
            some = chosen[g, at : at + out.shape[0]]
            value = dot(some, terms[g, 0]) + dot(some, terms[g, 1])
            out[...] = value if g == 0 else out[...] + value
            at += out.shape[0]
    first_ref[...], second_ref[...] = turns(high_ref[...], low_ref[...])
    token_ref[...] = jnp.zeros_like(token_ref)


def backward(pack, weights, rows, halo, after):
    offsets, width, _ = weights.shape
    slots = rows + 2 * halo
    group = 3 if offsets % 3 == 0 else 1
    return pl.pallas_call(
        functools.partial(backward_kernel, group),
        out_shape=tuple(jax.ShapeDtypeStruct((n, width), F32) for n in (rows, halo, halo)) + (TOKEN,),
        in_specs=[VMEM, VMEM, ANY],
        out_specs=(VMEM,) * 4,
        scratch_shapes=[
            pltpu.VMEM((pack.shape[0] - 2 * rows, rows), jnp.int32),
            pltpu.VMEM((offsets // group, slots, group * rows), BF),
            pltpu.VMEM((offsets // group, 2, group * rows, width), BF),
            pltpu.VMEM((halo, width), F32),
            pltpu.VMEM((halo, width), F32),
        ],
        compiler_params=params(),
        cost_estimate=cost(),
        name="backward",
    )(pack, weights, after)


def forward_kernel(group, pack_ref, halo_ref, w_ref, after_ref, out_ref, token_ref, table, maps, out_acc, picked):
    offsets, width, _ = w_ref.shape
    rows = out_ref.shape[0]
    slots = table.shape[0]
    table[0:rows] = pack_ref[0:rows]
    table[rows:] = halo_ref[...]
    codes = decoded(pack_ref[2 * rows :])
    maps[...] = jnp.transpose(jnp.concatenate([codes] * (maps.shape[1] // codes.shape[0]), axis=0))
    along = lax.broadcasted_iota(jnp.int32, (rows, 128), 1)
    for k in range(offsets):
        column = jnp.broadcast_to(maps[:, k : k + 1], (rows, 128))
        chosen = jnp.concatenate(
            [(along + 128 * b == column).astype(F32).astype(BF) for b in range(slots // 128)], axis=1
        )
        picked[k // group, :, k % group * width : (k % group + 1) * width] = dot(chosen, table[...]).astype(BF)
    for g in range(offsets // group):
        value = dot(picked[g], w_ref[g * group : (g + 1) * group].reshape(group * width, width))
        out_acc[...] = value if g == 0 else out_acc[...] + value
    keep = jnp.broadcast_to(maps[:, offsets // 2 : offsets // 2 + 1], (rows, width)) != slots
    out_ref[...] = jnp.where(keep, out_acc[...], 0.0).astype(BF)
    token_ref[...] = jnp.zeros_like(token_ref)


def forward(pack, halo_rows, weights, rows, after):
    offsets, width, _ = weights.shape
    slots = rows + halo_rows.shape[0]
    group = 3 if offsets % 3 == 0 else 1
    return pl.pallas_call(
        functools.partial(forward_kernel, group),
        out_shape=(jax.ShapeDtypeStruct((rows, width), BF), TOKEN),
        in_specs=[VMEM, VMEM, VMEM, ANY],
        out_specs=(VMEM, VMEM),
        scratch_shapes=[
            pltpu.VMEM((slots, width), BF),
            pltpu.VMEM((rows, 128), jnp.int32),
            pltpu.VMEM((rows, width), F32),
            pltpu.VMEM((offsets // group, rows, group * width), BF),
        ],
        compiler_params=params(),
        cost_estimate=cost(),
        name="forward",
    )(pack, halo_rows, weights, after)


def chosen_slots(maps, s, at, low, high, rows):
    slot = (lax.broadcasted_iota(jnp.int32, (high - low, rows), 0) + low).astype(jnp.int16)
    wanted = jnp.broadcast_to(maps[s, at : at + 1, :].astype(jnp.int16), (high - low, rows))
    return jnp.where(slot == wanted, jnp.ones((), BF), jnp.zeros((), BF))


def wgrad_own_kernel(offsets, *refs):
    packs, (picked_ref, dys, maps) = refs[:-3], refs[-3:]
    sources, _, rows = maps.shape
    slab = picked_ref.shape[1]
    for s in range(sources):
        dys[s * rows : (s + 1) * rows] = packs[s][slab : slab + rows]
        maps[s] = decoded(packs[s][slab + rows :])
    for j in range(offsets):
        for s in range(sources):
            chosen = chosen_slots(maps, s, j, 0, rows, rows)
            picked_ref[j, :, s * rows : (s + 1) * rows] = dot(packs[s][0:slab], chosen).astype(BF)


def wgrad_own(packs, offsets, slab, rows):
    sources, width = len(packs), packs[0].shape[1]
    return pl.pallas_call(
        functools.partial(wgrad_own_kernel, offsets),
        out_shape=(
            jax.ShapeDtypeStruct((offsets, slab, sources * rows), BF),
            jax.ShapeDtypeStruct((sources * rows, width), BF),
            jax.ShapeDtypeStruct((sources, packs[0].shape[0] - slab - rows, rows), jnp.int32),
        ),
        in_specs=[VMEM] * sources,
        out_specs=(VMEM, VMEM, VMEM),
        compiler_params=params(),
        cost_estimate=cost(),
        name="wgrad_own",
    )(*packs)


def wgrad_kernel(sizes, *refs):
    sets = [refs[3 * n : 3 * n + 3] for n in range(len(sizes))]
    halos, (keep_ref, send_ref, picked) = refs[3 * len(sizes) : -3], refs[-3:]
    count, half, width = keep_ref.shape
    far = halos[0].shape[1]
    offsets = sets[0][0].shape[0]
    rows = sets[0][2].shape[2]
    core = place()[1]
    for j in range(offsets):
        s = 0
        for (picked_ref, _, maps), size in zip(sets, sizes):
            for i in range(size):
                chosen = chosen_slots(maps, i, j, rows, rows + far, rows)
                near = picked_ref[j, :, i * rows : (i + 1) * rows].astype(F32)
                value = (dot(halos[s][...], chosen) + near).astype(BF)
                for h in range(2):
                    picked[h, j * half : (j + 1) * half, s * rows : (s + 1) * rows] = value[h * half : (h + 1) * half]
                s += 1
    picked[:, offsets * half :] = jnp.zeros((2, (count - offsets) * half, picked.shape[2]), BF)
    for out_ref, h in ((send_ref, 1 - core), (keep_ref, core)):
        total, s = 0.0, 0
        for (_, dys, _), size in zip(sets, sizes):
            total = total + dot(picked[h, :, s * rows : (s + size) * rows], dys[...])
            s += size
        out_ref[...] = total.reshape(out_ref.shape)


def wgrad(sets, halos, count):
    sizes = [maps.shape[0] for _, _, maps in sets]
    _, slab, _ = sets[0][0].shape
    columns = sum(picked.shape[2] for picked, _, _ in sets)
    shape = jax.ShapeDtypeStruct((count, slab // 2, sets[0][1].shape[1]), F32)
    return pl.pallas_call(
        functools.partial(wgrad_kernel, sizes),
        out_shape=(shape, shape),
        in_specs=[VMEM] * (3 * len(sizes) + len(halos)),
        out_specs=(VMEM, VMEM),
        scratch_shapes=[pltpu.VMEM((2, count * slab // 2, columns), BF)],
        compiler_params=params(),
        cost_estimate=cost(),
        name="wgrad",
    )(*[array for one in sets for array in one], *halos)


def power(exponent):
    value = jnp.ones(exponent.shape, F32)
    size = jnp.abs(exponent)
    for bit in range(7):
        factor = jnp.where(exponent < 0, 0.5 ** (1 << bit), 2.0 ** (1 << bit))
        value = value * jnp.where((size >> bit) & 1 == 1, factor, 1.0)
    return value


def near_kernel(pack_ref, copy_ref, own_ref, turned):
    slab = own_ref.shape[0] - (pack_ref.shape[0] - turned.shape[1])
    rows = turned.shape[1]
    copy_ref[...] = pack_ref[...]
    turned[...] = jnp.transpose(pack_ref[0:rows])
    own_ref[0:slab] = turned[pl.ds(pl.multiple_of(place()[0] * slab, slab), slab), :]
    own_ref[slab:] = pack_ref[rows:]


def near_pack(pack, rows, slab):
    width = pack.shape[1]
    return pl.pallas_call(
        near_kernel,
        out_shape=(
            jax.ShapeDtypeStruct(pack.shape, BF),
            jax.ShapeDtypeStruct((slab + pack.shape[0] - rows, width), BF),
        ),
        in_specs=[VMEM],
        out_specs=(VMEM, VMEM),
        scratch_shapes=[pltpu.VMEM((width, rows), BF)],
        compiler_params=params(),
        cost_estimate=cost(),
        name="near_pack",
    )(pack)


def joined_kernel(first_ref, second_ref, after_ref, out_ref, *refs):
    turned, halo_refs = refs[-1], refs[:-1]
    halo = first_ref.shape[0]
    slab = halo_refs[0].shape[0]
    second, first = turns(0, halo)
    out_ref[pl.ds(pl.multiple_of(first, halo), halo)] = first_ref[...]
    out_ref[pl.ds(pl.multiple_of(second, halo), halo)] = second_ref[...]
    turned[...] = jnp.transpose(out_ref[...])
    for m, halo_ref in enumerate(halo_refs):
        halo_ref[...] = turned[pl.ds(pl.multiple_of((place()[0] ^ m) * slab, slab), slab), :]


def joined(first, second, groups, after):
    halo, width = first.shape
    slab = width // groups
    return pl.pallas_call(
        joined_kernel,
        out_shape=(
            jax.ShapeDtypeStruct((2 * halo, width), BF),
            *(jax.ShapeDtypeStruct((slab, 2 * halo), BF),) * groups,
        ),
        in_specs=[VMEM] * 2 + [ANY],
        out_specs=(VMEM,) * (1 + groups),
        scratch_shapes=[pltpu.VMEM((width, 2 * halo), BF)],
        compiler_params=params(),
        cost_estimate=cost(),
        name="joined",
    )(first, second, after)


def blocks_kernel(keep_ref, got_ref, mine_ref, *refs):
    coded_refs, exponents = refs[:-1], refs[-1]
    count, block, width = mine_ref.shape
    for m in range(len(coded_refs) + 1):
        at = (place()[2] ^ m) * count
        if m == 0:
            mine_ref[...] = keep_ref[pl.ds(at, count)] + got_ref[pl.ds(at, count)]
            continue
        exponents[...] = jnp.zeros_like(exponents)
        for j in range(count):
            value = keep_ref[at + j] + got_ref[at + j]
            largest = jnp.max(jnp.abs(value), axis=0, keepdims=True)
            exponent = jnp.ceil(jnp.log(jnp.maximum(largest, 2.0**-100)) * (1.0 / math.log(2.0)))
            exponent = jnp.clip(exponent, -100.0, 100.0).astype(jnp.int32) - 15
            exponents[j : j + 1, :] = exponent
            scaled = jnp.round(jnp.clip(value * power(-exponent), -32767.0, 32767.0))
            coded_refs[m - 1][j * block : (j + 1) * block] = scaled.astype(jnp.int32).astype(jnp.int16)
        coded_refs[m - 1][count * block :] = exponents[...].astype(jnp.int16)


def blocks(keep, got, parts):
    total, block, width = keep.shape
    count = total // parts
    extra = -(-count // 16) * 16
    return pl.pallas_call(
        blocks_kernel,
        out_shape=(
            jax.ShapeDtypeStruct((count, block, width), F32),
            *(jax.ShapeDtypeStruct((count * block + extra, width), jnp.int16),) * (parts - 1),
        ),
        in_specs=[VMEM, VMEM],
        out_specs=(VMEM,) * parts,
        scratch_shapes=[pltpu.VMEM((extra, width), jnp.int32)],
        compiler_params=params(),
        cost_estimate=cost(),
        name="blocks",
    )(keep, got)


def total_kernel(scale, mine_ref, *refs):
    *coded_refs, _, _, out_ref = refs
    count, block, width = mine_ref.shape
    powers = [power(ref[count * block :].astype(jnp.int32)) for ref in coded_refs]
    for j in range(count):
        total = mine_ref[j]
        for ref, factor in zip(coded_refs, powers):
            value = ref[j * block : (j + 1) * block].astype(jnp.int32).astype(F32)
            total = total + value * factor[j : j + 1, :]
        out_ref[j] = (total * scale).astype(BF)


def scaled_total(mine, coded, scale, after):
    return pl.pallas_call(
        functools.partial(total_kernel, scale),
        out_shape=jax.ShapeDtypeStruct(mine.shape, BF),
        in_specs=[VMEM] * (len(coded) + 1) + [ANY] * 2,
        out_specs=VMEM,
        compiler_params=params(),
        cost_estimate=cost(),
        name="total",
    )(mine, *coded, *after)


def final_kernel(offsets, pack_ref, own_ref, first_ref, second_ref, up_ref, down_ref, after_ref, out_ref, token_ref):
    rows, width = own_ref.shape
    halo = up_ref.shape[1]
    total = own_ref[...]
    iota = lax.broadcasted_iota(jnp.int32, (rows, halo), 0)
    chosen = [(iota == index).astype(F32) for index in turns(up_ref[...], down_ref[...])]
    chosen = jnp.concatenate(chosen, axis=1).astype(BF)
    for part in split(jnp.concatenate([first_ref[...], second_ref[...]], axis=0), 3):
        total = total + dot(chosen, part)
    keep = live_rows(decoded(pack_ref[2 * rows :]), offsets, width, rows + 2 * halo)
    out_ref[...] = jnp.where(keep, total, 0.0).astype(BF)
    token_ref[...] = jnp.zeros_like(token_ref)


def final(offsets, pack, own_grad, first_back, second_back, send_up, send_down, after):
    return pl.pallas_call(
        functools.partial(final_kernel, offsets),
        out_shape=(jax.ShapeDtypeStruct(own_grad.shape, BF), TOKEN),
        in_specs=[VMEM] * 6 + [ANY],
        out_specs=(VMEM, VMEM),
        compiler_params=params(),
        name="final",
    )(pack, own_grad, first_back, second_back, send_up, send_down, after)


def stack_kernel(count, *refs):
    at = 0
    for ref in refs[:count]:
        for m in range(ref.shape[0] if len(ref.shape) == 4 else 1):
            refs[-1][at] = ref[m] if len(ref.shape) == 4 else ref[...]
            at += 1


def stack(arrays, after):
    blocks = sum(array.shape[0] if array.ndim == 4 else 1 for array in arrays)
    return pl.pallas_call(
        functools.partial(stack_kernel, len(arrays)),
        out_shape=jax.ShapeDtypeStruct((blocks, *arrays[0].shape[-3:]), BF),
        in_specs=[VMEM] * len(arrays) + [ANY] * len(after),
        out_specs=VMEM,
        compiler_params=params(),
        cost_estimate=cost(),
        name="stack",
    )(*arrays, *after)


def gate_kernel(*refs):
    pass


def gate(value, after):
    return pl.pallas_call(
        gate_kernel,
        out_shape=jax.ShapeDtypeStruct(value.shape, value.dtype),
        in_specs=[ANY] * (1 + len(after)),
        out_specs=ANY,
        input_output_aliases={0: 0},
        compiler_params=params(),
        cost_estimate=cost(),
        name="gate",
    )(value, *after)


def assemble_kernel(marks, parts, groups, *refs):
    out_ref, sems = refs[-2:]
    _, count, block, _ = refs[0].shape
    short = out_ref.shape[0] - (parts - 1) * count

    def each(act):
        for index, (o, sources) in enumerate(marks):
            for part, (m, mask) in enumerate(sources):
                group, core, space = place()
                at = (space ^ mask) * count
                row = pl.multiple_of(((group ^ m) * 2 + (core ^ o)) * block, block)
                source = refs[index].at[part]

                def copy(lo, hi, sem):
                    target = out_ref.at[pl.ds(at + lo, hi - lo), pl.ds(row, block)]
                    return pltpu.make_async_copy(source.at[lo:hi], target, sems.at[index, part, sem])

                getattr(copy(0, short, 0), act)()
                if short < count:
                    pl.when((space ^ mask) < parts - 1)(getattr(copy(short, count, 1), act))

    each("start")
    each("wait")


def assemble(pieces, marks, parts, groups, offsets, width, after, base=()):
    most = max(piece.shape[0] for piece in pieces)
    return pl.pallas_call(
        functools.partial(assemble_kernel, marks, parts, groups),
        out_shape=jax.ShapeDtypeStruct((offsets, width, width), BF),
        in_specs=[ANY] * (len(pieces) + len(after)) + [HBM] * len(base),
        out_specs=HBM,
        scratch_shapes=[pltpu.SemaphoreType.DMA((len(pieces), most, 2))],
        input_output_aliases={len(pieces) + len(after): 0} if base else {},
        compiler_params=params(),
        cost_estimate=cost(),
        name="assemble",
    )(*pieces, *after, *base)


def assemble_plain(pieces, marks, parts, groups, offsets, width):
    _, count, block, _ = pieces[0].shape
    total = jnp.zeros((parts * count, width, width), BF)
    for piece, (o, sources) in zip(pieces, marks):
        for part, (m, mask) in enumerate(sources):
            group, core, space = place()
            row = ((group ^ m) * 2 + (core ^ o)) * block
            total = lax.dynamic_update_slice(total, piece[part], ((space ^ mask) * count, row, 0))
    return total[:offsets]


def swap(value, axis, mask):
    return lax.ppermute(value, axis, [(i, i ^ mask) for i in range(lax.axis_size(axis))])


def met(value, turn):
    count = lax.axis_size("space")
    starts = range(turn, count - 1, 2)
    return lax.ppermute(value, "space", [(i, i + 1) for i in starts] + [(i + 1, i) for i in starts])


def shards(features, weights, cotangent, kernel_map, live, send_up, send_down):
    rows, width = features.shape
    offsets, halo = weights.shape[0], send_up.shape[1]
    groups = lax.axis_size("dp") // 2
    parts = lax.axis_size("space")
    count = -(-offsets // parts)
    slab = width // groups
    map_rows = -(-offsets // 16) * 16

    pack, first_rows, second_rows, *packs = prep(
        features, cotangent, kernel_map, send_up, send_down, map_rows, groups
    )
    packs = [swap(part, "dp", 2 * m) for m, part in enumerate(packs, 1)]
    pack, own_part = near_pack(pack, rows, slab)
    own_set = wgrad_own([own_part], offsets, slab, rows)
    halo_rows, own_halo, *halos = joined(met(first_rows, 0), met(second_rows, 1), groups, own_set[1])
    halos = [swap(part, "dp", 2 * m) for m, part in enumerate(halos, 1)]
    sets = [own_set, wgrad_own(packs, offsets, slab, rows)]
    keep, send = wgrad(sets, [own_halo, *halos], parts * count)
    mine, *coded = blocks(keep, swap(send, "dp", 1), parts)
    own_grad, first_grad, second_grad, token = backward(pack, weights, rows, halo, mine)
    first_back, second_back = met(first_grad, 0), met(second_grad, 1)
    scale = 1.0 / math.sqrt(rows * lax.axis_size("dp") * parts)
    rounded = scaled_total(mine, [swap(block, "space", m + 1) for m, block in enumerate(coded)], scale, (token, token))
    out_features, token = forward(pack, halo_rows, weights, rows, rounded)

    along = [swap(rounded, "space", m) for m in range(1, parts)]
    across = {m: swap(rounded, "dp", 2 * m) for m in range(1, groups)}
    lines = gate(stack(along, [token]), list(across.values()))
    far = {m: swap(lines, "dp", 2 * m) for m in range(1, groups)}
    line_masks = range(1, parts)
    grad_features, token = final(offsets, pack, own_grad, first_back, second_back, send_up, send_down, lines)
    near = stack([rounded, lines], [token])
    sides = stack([across[m] for m in range(1, groups)], [])
    near_marks = [(0, mask) for mask in range(parts)]
    side_marks = [(m, 0) for m in range(1, groups)]
    pieces = [near, swap(near, "dp", 1), sides, swap(sides, "dp", 1)]
    marks = [(0, near_marks), (1, near_marks), (0, side_marks), (1, side_marks)]
    dense = rounded.shape[1] % 16 == 0 and parts * count - offsets < count
    sizes = (parts, groups, offsets, width)
    first = ()
    if dense:
        first = (assemble(pieces, marks, *sizes, ()),)
        pieces, marks = [], []
    for m in range(1, groups):
        pieces += [far[m], swap(far[m], "dp", 1)]
        marks += [(o, [(m, mask) for mask in line_masks]) for o in range(2)]
    if dense:
        grad_weights = assemble(pieces, marks, *sizes, (token,), first)
    else:
        grad_weights = assemble_plain(pieces, marks, *sizes)
    return (out_features, grad_features, grad_weights)


def solution(mesh):
    placed = (
        P(("dp", "space"), None),
        P(),
        P(("dp", "space"), None),
        P(None, ("dp", "space")),
        P(("dp", "space")),
        P(("dp", "space"), None),
        P(("dp", "space"), None),
    )
    return jax.shard_map(
        shards,
        mesh=mesh,
        in_specs=placed,
        out_specs=(P(("dp", "space"), None), P(("dp", "space"), None), P()),
        check_vma=False,
    )
```

```python
import functools
import math

import jax
import jax.numpy as jnp
from jax import lax
from jax.experimental import pallas as pl
from jax.experimental.pallas import tpu as pltpu
from jax.sharding import PartitionSpec as P

BF = jnp.bfloat16
F32 = jnp.float32
VMEM_LIMIT = 32 * 1024 * 1024
PREP_LIMIT = 60 * 1024 * 1024
VMEM = pl.BlockSpec(memory_space=pltpu.VMEM)
ANY = pl.BlockSpec(memory_space=pl.ANY)
HBM = pl.BlockSpec(memory_space=pltpu.HBM)
TOKEN = jax.ShapeDtypeStruct((8, 128), F32)


def params(limit=VMEM_LIMIT):
    return pltpu.CompilerParams(vmem_limit_bytes=limit)


def cost():
    return pl.CostEstimate(flops=100_000_000, bytes_accessed=100_000, transcendentals=0)


def dot(a, b):
    return jnp.dot(a, b, preferred_element_type=F32)


def split(value, terms):
    parts = []
    for _ in range(terms):
        part = value.astype(BF)
        parts.append(part)
        value = value - part.astype(F32)
    return parts


def place():
    dp = lax.axis_index("dp")
    return dp // 2, lax.rem(dp, 2), lax.axis_index("space")


def turns(up, down):
    even = lax.rem(place()[2], 2) == 0
    return jnp.where(even, up, down), jnp.where(even, down, up)


def live_rows(maps, offsets, width, zero_slot):
    rows = maps.shape[1]
    centre = jnp.transpose(jnp.broadcast_to(maps[offsets // 2 : offsets // 2 + 1, :], (128, rows)))
    return jnp.concatenate([centre] * (width // 128), axis=1) != zero_slot


def prep_kernel(x_hbm, dy_hbm, map_hbm, up_hbm, down_hbm, pack_ref, first_ref, second_ref, *refs):
    part_refs, (x_ref, dy_ref, map_ref, up_ref, down_ref, map_scr, turned, sems) = refs[:-8], refs[-8:]
    sources = (x_hbm, dy_hbm, map_hbm, up_hbm, down_hbm)
    targets = (x_ref, dy_ref, map_ref, up_ref, down_ref)
    copies = [pltpu.make_async_copy(a, b, sems.at[i]) for i, (a, b) in enumerate(zip(sources, targets))]
    for copy in copies:
        copy.start()
    rows, width = x_ref.shape
    offsets = map_ref.shape[0]
    halo = up_ref.shape[1]
    zero_slot = rows + 2 * halo
    map_scr[...] = jnp.full(map_scr.shape, zero_slot, jnp.int32)
    for copy in copies:
        copy.wait()
    keep = live_rows(map_ref[...], offsets, width, zero_slot)
    x_live = jnp.where(keep, x_ref[...].astype(F32), 0.0).astype(BF)
    pack_ref[0:rows] = x_live
    iota = lax.broadcasted_iota(jnp.int32, (rows, halo), 0)
    for index, picked_ref in zip(turns(up_ref[...], down_ref[...]), (first_ref, second_ref)):
        chosen = (iota == index).astype(F32).astype(BF)
        picked_ref[...] = lax.dot_general(chosen, x_live, (((0,), (0,)), ((), ())), preferred_element_type=F32).astype(BF)
    pack_ref[rows : 2 * rows] = jnp.where(keep, dy_ref[...].astype(F32), 0.0).astype(BF)
    map_scr[0:offsets] = map_ref[...]
    slots = map_scr[...]
    pack_ref[2 * rows :] = jnp.where(slots > 256, 256 - slots, slots).astype(F32).astype(BF)
    turned[...] = jnp.transpose(x_live)
    for m, part_ref in enumerate(part_refs):
        slab = part_ref.shape[0] - (pack_ref.shape[0] - rows)
        part_ref[0:slab] = turned[pl.ds(pl.multiple_of((place()[0] ^ (m + 1)) * slab, slab), slab), :]
        part_ref[slab:] = pack_ref[rows:]


def prep(features, cotangent, kernel_map, send_up, send_down, map_rows, groups):
    rows, width = features.shape
    return pl.pallas_call(
        prep_kernel,
        out_shape=(
            jax.ShapeDtypeStruct((2 * rows + map_rows, width), BF),
            jax.ShapeDtypeStruct((send_up.shape[1], width), BF),
            jax.ShapeDtypeStruct((send_up.shape[1], width), BF),
            *(jax.ShapeDtypeStruct((width // groups + rows + map_rows, rows), BF),) * (groups - 1),
        ),
        in_specs=[HBM] * 5,
        out_specs=(VMEM,) * (2 + groups),
        scratch_shapes=[
            pltpu.VMEM((rows, width), BF),
            pltpu.VMEM((rows, width), BF),
            pltpu.VMEM(kernel_map.shape, jnp.int32),
            pltpu.VMEM(send_up.shape, jnp.int32),
            pltpu.VMEM(send_down.shape, jnp.int32),
            pltpu.VMEM((map_rows, rows), jnp.int32),
            pltpu.VMEM((width, rows), BF),
            pltpu.SemaphoreType.DMA((5,)),
        ],
        compiler_params=params(PREP_LIMIT),
        name="prep",
    )(features, cotangent, kernel_map, send_up, send_down)


def decoded(code):
    code = code.astype(F32).astype(jnp.int32)
    return jnp.where(code < 0, 256 - code, code)


def backward_kernel(group, pack_ref, w_ref, after_ref, own_ref, first_ref, second_ref, token_ref, *scratch):
    maps, chosen, terms, low_ref, high_ref = scratch
    offsets, width, _ = w_ref.shape
    rows = own_ref.shape[0]
    slots = chosen.shape[1]
    maps[...] = decoded(pack_ref[2 * rows :])
    dy = pack_ref[rows : 2 * rows]
    slot_down = lax.broadcasted_iota(jnp.int32, (slots, rows), 0)
    for k in range(offsets):
        at = slice(k % group * rows, (k % group + 1) * rows)
        chosen[k // group, :, at] = (slot_down == maps[k : k + 1, :]).astype(F32).astype(BF)
        back = lax.dot_general(dy, w_ref[k], (((1,), (1,)), ((), ())), preferred_element_type=F32)
        for t, part in enumerate(split(back, 2)):
            terms[k // group, t, at] = part
    for g in range(offsets // group):
        at = 0
        for out in (own_ref, low_ref, high_ref):
            some = chosen[g, at : at + out.shape[0]]
            value = dot(some, terms[g, 0]) + dot(some, terms[g, 1])
            out[...] = value if g == 0 else out[...] + value
            at += out.shape[0]
    first_ref[...], second_ref[...] = turns(high_ref[...], low_ref[...])
    token_ref[...] = jnp.zeros_like(token_ref)


def backward(pack, weights, rows, halo, after):
    offsets, width, _ = weights.shape
    slots = rows + 2 * halo
    group = 3 if offsets % 3 == 0 else 1
    return pl.pallas_call(
        functools.partial(backward_kernel, group),
        out_shape=tuple(jax.ShapeDtypeStruct((n, width), F32) for n in (rows, halo, halo)) + (TOKEN,),
        in_specs=[VMEM, VMEM, ANY],
        out_specs=(VMEM,) * 4,
        scratch_shapes=[
            pltpu.VMEM((pack.shape[0] - 2 * rows, rows), jnp.int32),
            pltpu.VMEM((offsets // group, slots, group * rows), BF),
            pltpu.VMEM((offsets // group, 2, group * rows, width), BF),
            pltpu.VMEM((halo, width), F32),
            pltpu.VMEM((halo, width), F32),
        ],
        compiler_params=params(),
        cost_estimate=cost(),
        name="backward",
    )(pack, weights, after)


def forward_kernel(group, pack_ref, halo_ref, w_ref, after_ref, out_ref, token_ref, table, maps, out_acc, picked):
    offsets, width, _ = w_ref.shape
    rows = out_ref.shape[0]
    slots = table.shape[0]
    table[0:rows] = pack_ref[0:rows]
    table[rows:] = halo_ref[...]
    codes = decoded(pack_ref[2 * rows :])
    maps[...] = jnp.transpose(jnp.concatenate([codes] * (maps.shape[1] // codes.shape[0]), axis=0))
    along = lax.broadcasted_iota(jnp.int32, (rows, 128), 1)
    for k in range(offsets):
        column = jnp.broadcast_to(maps[:, k : k + 1], (rows, 128))
        chosen = jnp.concatenate(
            [(along + 128 * b == column).astype(F32).astype(BF) for b in range(slots // 128)], axis=1
        )
        picked[k // group, :, k % group * width : (k % group + 1) * width] = dot(chosen, table[...]).astype(BF)
    for g in range(offsets // group):
        value = dot(picked[g], w_ref[g * group : (g + 1) * group].reshape(group * width, width))
        out_acc[...] = value if g == 0 else out_acc[...] + value
    keep = jnp.broadcast_to(maps[:, offsets // 2 : offsets // 2 + 1], (rows, width)) != slots
    out_ref[...] = jnp.where(keep, out_acc[...], 0.0).astype(BF)
    token_ref[...] = jnp.zeros_like(token_ref)


def forward(pack, halo_rows, weights, rows, after):
    offsets, width, _ = weights.shape
    slots = rows + halo_rows.shape[0]
    group = 3 if offsets % 3 == 0 else 1
    return pl.pallas_call(
        functools.partial(forward_kernel, group),
        out_shape=(jax.ShapeDtypeStruct((rows, width), BF), TOKEN),
        in_specs=[VMEM, VMEM, VMEM, ANY],
        out_specs=(VMEM, VMEM),
        scratch_shapes=[
            pltpu.VMEM((slots, width), BF),
            pltpu.VMEM((rows, 128), jnp.int32),
            pltpu.VMEM((rows, width), F32),
            pltpu.VMEM((offsets // group, rows, group * width), BF),
        ],
        compiler_params=params(),
        cost_estimate=cost(),
        name="forward",
    )(pack, halo_rows, weights, after)


def chosen_slots(maps, s, at, low, high, rows):
    slot = (lax.broadcasted_iota(jnp.int32, (high - low, rows), 0) + low).astype(jnp.int16)
    wanted = jnp.broadcast_to(maps[s, at : at + 1, :].astype(jnp.int16), (high - low, rows))
    return jnp.where(slot == wanted, jnp.ones((), BF), jnp.zeros((), BF))


def wgrad_own_kernel(offsets, *refs):
    packs, (picked_ref, dys, maps) = refs[:-3], refs[-3:]
    sources, _, rows = maps.shape
    slab = picked_ref.shape[1]
    for s in range(sources):
        dys[s * rows : (s + 1) * rows] = packs[s][slab : slab + rows]
        maps[s] = decoded(packs[s][slab + rows :])
    for j in range(offsets):
        for s in range(sources):
            chosen = chosen_slots(maps, s, j, 0, rows, rows)
            picked_ref[j, :, s * rows : (s + 1) * rows] = dot(packs[s][0:slab], chosen).astype(BF)


def wgrad_own(packs, offsets, slab, rows):
    sources, width = len(packs), packs[0].shape[1]
    return pl.pallas_call(
        functools.partial(wgrad_own_kernel, offsets),
        out_shape=(
            jax.ShapeDtypeStruct((offsets, slab, sources * rows), BF),
            jax.ShapeDtypeStruct((sources * rows, width), BF),
            jax.ShapeDtypeStruct((sources, packs[0].shape[0] - slab - rows, rows), jnp.int32),
        ),
        in_specs=[VMEM] * sources,
        out_specs=(VMEM, VMEM, VMEM),
        compiler_params=params(),
        cost_estimate=cost(),
        name="wgrad_own",
    )(*packs)


def picked_rows(out_ref, part, j, near_ref, maps, i, halo_ref):
    rows, half = maps.shape[2], near_ref.shape[1] // 2
    chosen = chosen_slots(maps, i, j, rows, rows + halo_ref.shape[1], rows)
    near = near_ref[j, :, i * rows : (i + 1) * rows].astype(F32)
    value = (dot(halo_ref[...], chosen) + near).astype(BF)
    for h in range(2):
        out_ref[h, j * half : (j + 1) * half, part * rows : (part + 1) * rows] = value[h * half : (h + 1) * half]


def clear_rest(out_ref, offsets, half):
    _, size, columns = out_ref.shape
    if offsets * half < size:
        out_ref[:, offsets * half :] = jnp.zeros((2, size - offsets * half, columns), BF)


def early_kernel(own_ref, own_maps, rest_ref, rest_maps, *refs):
    halos, out_ref = refs[:-1], refs[-1]
    offsets, slab, _ = own_ref.shape
    for j in range(offsets):
        for s, halo_ref in enumerate(halos):
            near = (own_ref, own_maps, 0) if s == 0 else (rest_ref, rest_maps, s - 1)
            picked_rows(out_ref, s, j, *near, halo_ref)
    clear_rest(out_ref, offsets, slab // 2)


def wgrad_early(own_set, rest_set, halos, count):
    own, _, own_maps = own_set
    rest, _, rest_maps = rest_set
    _, slab, rows = own.shape
    return pl.pallas_call(
        early_kernel,
        out_shape=jax.ShapeDtypeStruct((2, count * slab // 2, len(halos) * rows), BF),
        in_specs=[VMEM] * (4 + len(halos)),
        out_specs=VMEM,
        compiler_params=params(),
        cost_estimate=cost(),
        name="wgrad_early",
    )(own, own_maps, rest, rest_maps, *halos)


def wgrad_kernel(early_ref, own_dys, rest_ref, rest_dys, rest_maps, halo_ref, keep_ref, send_ref, picked):
    offsets, slab, _ = rest_ref.shape
    last, rows = rest_maps.shape[0] - 1, rest_maps.shape[2]
    core = place()[1]
    for j in range(offsets):
        picked_rows(picked, 0, j, rest_ref, rest_maps, last, halo_ref)
    clear_rest(picked, offsets, slab // 2)
    for out_ref, h in ((send_ref, 1 - core), (keep_ref, core)):
        total = dot(early_ref[h, :, 0:rows], own_dys[...]) + dot(early_ref[h, :, rows:], rest_dys[0 : last * rows])
        total = total + dot(picked[h], rest_dys[last * rows :])
        out_ref[...] = total.reshape(out_ref.shape)


def wgrad(early, own_set, rest_set, halo, count):
    rest, rest_dys, rest_maps = rest_set
    _, slab, _ = rest.shape
    shape = jax.ShapeDtypeStruct((count, slab // 2, rest_dys.shape[1]), F32)
    return pl.pallas_call(
        wgrad_kernel,
        out_shape=(shape, shape),
        in_specs=[VMEM] * 6,
        out_specs=(VMEM, VMEM),
        scratch_shapes=[pltpu.VMEM((2, count * slab // 2, rest_maps.shape[2]), BF)],
        compiler_params=params(),
        cost_estimate=cost(),
        name="wgrad",
    )(early, own_set[1], rest, rest_dys, rest_maps, halo)


def power(exponent):
    value = jnp.ones(exponent.shape, F32)
    size = jnp.abs(exponent)
    for bit in range(7):
        factor = jnp.where(exponent < 0, 0.5 ** (1 << bit), 2.0 ** (1 << bit))
        value = value * jnp.where((size >> bit) & 1 == 1, factor, 1.0)
    return value


def near_kernel(pack_ref, copy_ref, own_ref, turned):
    slab = own_ref.shape[0] - (pack_ref.shape[0] - turned.shape[1])
    rows = turned.shape[1]
    copy_ref[...] = pack_ref[...]
    turned[...] = jnp.transpose(pack_ref[0:rows])
    own_ref[0:slab] = turned[pl.ds(pl.multiple_of(place()[0] * slab, slab), slab), :]
    own_ref[slab:] = pack_ref[rows:]


def near_pack(pack, rows, slab):
    width = pack.shape[1]
    return pl.pallas_call(
        near_kernel,
        out_shape=(
            jax.ShapeDtypeStruct(pack.shape, BF),
            jax.ShapeDtypeStruct((slab + pack.shape[0] - rows, width), BF),
        ),
        in_specs=[VMEM],
        out_specs=(VMEM, VMEM),
        scratch_shapes=[pltpu.VMEM((width, rows), BF)],
        compiler_params=params(),
        cost_estimate=cost(),
        name="near_pack",
    )(pack)


def joined_kernel(first_ref, second_ref, after_ref, out_ref, *refs):
    turned, halo_refs = refs[-1], refs[:-1]
    halo = first_ref.shape[0]
    slab = halo_refs[0].shape[0]
    second, first = turns(0, halo)
    out_ref[pl.ds(pl.multiple_of(first, halo), halo)] = first_ref[...]
    out_ref[pl.ds(pl.multiple_of(second, halo), halo)] = second_ref[...]
    turned[...] = jnp.transpose(out_ref[...])
    for m, halo_ref in enumerate(halo_refs):
        halo_ref[...] = turned[pl.ds(pl.multiple_of((place()[0] ^ m) * slab, slab), slab), :]


def joined(first, second, groups, after):
    halo, width = first.shape
    slab = width // groups
    return pl.pallas_call(
        joined_kernel,
        out_shape=(
            jax.ShapeDtypeStruct((2 * halo, width), BF),
            *(jax.ShapeDtypeStruct((slab, 2 * halo), BF),) * groups,
        ),
        in_specs=[VMEM] * 2 + [ANY],
        out_specs=(VMEM,) * (1 + groups),
        scratch_shapes=[pltpu.VMEM((width, 2 * halo), BF)],
        compiler_params=params(),
        cost_estimate=cost(),
        name="joined",
    )(first, second, after)


def blocks_kernel(keep_ref, got_ref, mine_ref, *refs):
    coded_refs, exponents = refs[:-1], refs[-1]
    count, block, width = mine_ref.shape
    for m in range(len(coded_refs) + 1):
        at = (place()[2] ^ m) * count
        if m == 0:
            mine_ref[...] = keep_ref[pl.ds(at, count)] + got_ref[pl.ds(at, count)]
            continue
        exponents[...] = jnp.zeros_like(exponents)
        for j in range(count):
            value = keep_ref[at + j] + got_ref[at + j]
            largest = jnp.max(jnp.abs(value), axis=0, keepdims=True)
            exponent = jnp.ceil(jnp.log(jnp.maximum(largest, 2.0**-100)) * (1.0 / math.log(2.0)))
            exponent = jnp.clip(exponent, -100.0, 100.0).astype(jnp.int32) - 15
            exponents[j : j + 1, :] = exponent
            scaled = jnp.round(jnp.clip(value * power(-exponent), -32767.0, 32767.0))
            coded_refs[m - 1][j * block : (j + 1) * block] = scaled.astype(jnp.int32).astype(jnp.int16)
        coded_refs[m - 1][count * block :] = exponents[...].astype(jnp.int16)


def blocks(keep, got, parts):
    total, block, width = keep.shape
    count = total // parts
    extra = -(-count // 16) * 16
    return pl.pallas_call(
        blocks_kernel,
        out_shape=(
            jax.ShapeDtypeStruct((count, block, width), F32),
            *(jax.ShapeDtypeStruct((count * block + extra, width), jnp.int16),) * (parts - 1),
        ),
        in_specs=[VMEM, VMEM],
        out_specs=(VMEM,) * parts,
        scratch_shapes=[pltpu.VMEM((extra, width), jnp.int32)],
        compiler_params=params(),
        cost_estimate=cost(),
        name="blocks",
    )(keep, got)


def total_kernel(scale, mine_ref, *refs):
    *coded_refs, _, _, out_ref = refs
    count, block, width = mine_ref.shape
    powers = [power(ref[count * block :].astype(jnp.int32)) for ref in coded_refs]
    for j in range(count):
        total = mine_ref[j]
        for ref, factor in zip(coded_refs, powers):
            value = ref[j * block : (j + 1) * block].astype(jnp.int32).astype(F32)
            total = total + value * factor[j : j + 1, :]
        out_ref[j] = (total * scale).astype(BF)


def scaled_total(mine, coded, scale, after):
    return pl.pallas_call(
        functools.partial(total_kernel, scale),
        out_shape=jax.ShapeDtypeStruct(mine.shape, BF),
        in_specs=[VMEM] * (len(coded) + 1) + [ANY] * 2,
        out_specs=VMEM,
        compiler_params=params(),
        cost_estimate=cost(),
        name="total",
    )(mine, *coded, *after)


def final_kernel(offsets, pack_ref, own_ref, first_ref, second_ref, up_ref, down_ref, after_ref, out_ref, token_ref):
    rows, width = own_ref.shape
    halo = up_ref.shape[1]
    total = own_ref[...]
    iota = lax.broadcasted_iota(jnp.int32, (rows, halo), 0)
    chosen = [(iota == index).astype(F32) for index in turns(up_ref[...], down_ref[...])]
    chosen = jnp.concatenate(chosen, axis=1).astype(BF)
    for part in split(jnp.concatenate([first_ref[...], second_ref[...]], axis=0), 3):
        total = total + dot(chosen, part)
    keep = live_rows(decoded(pack_ref[2 * rows :]), offsets, width, rows + 2 * halo)
    out_ref[...] = jnp.where(keep, total, 0.0).astype(BF)
    token_ref[...] = jnp.zeros_like(token_ref)


def final(offsets, pack, own_grad, first_back, second_back, send_up, send_down, after):
    return pl.pallas_call(
        functools.partial(final_kernel, offsets),
        out_shape=(jax.ShapeDtypeStruct(own_grad.shape, BF), TOKEN),
        in_specs=[VMEM] * 6 + [ANY],
        out_specs=(VMEM, VMEM),
        compiler_params=params(),
        name="final",
    )(pack, own_grad, first_back, second_back, send_up, send_down, after)


def stack_kernel(count, *refs):
    at = 0
    for ref in refs[:count]:
        for m in range(ref.shape[0] if len(ref.shape) == 4 else 1):
            refs[-1][at] = ref[m] if len(ref.shape) == 4 else ref[...]
            at += 1


def stack(arrays, after):
    blocks = sum(array.shape[0] if array.ndim == 4 else 1 for array in arrays)
    return pl.pallas_call(
        functools.partial(stack_kernel, len(arrays)),
        out_shape=jax.ShapeDtypeStruct((blocks, *arrays[0].shape[-3:]), BF),
        in_specs=[VMEM] * len(arrays) + [ANY] * len(after),
        out_specs=VMEM,
        compiler_params=params(),
        cost_estimate=cost(),
        name="stack",
    )(*arrays, *after)


def gate_kernel(*refs):
    pass


def gate(value, after):
    return pl.pallas_call(
        gate_kernel,
        out_shape=jax.ShapeDtypeStruct(value.shape, value.dtype),
        in_specs=[ANY] * (1 + len(after)),
        out_specs=ANY,
        input_output_aliases={0: 0},
        compiler_params=params(),
        cost_estimate=cost(),
        name="gate",
    )(value, *after)


def assemble_kernel(marks, parts, groups, *refs):
    out_ref, sems = refs[-2:]
    _, count, block, _ = refs[0].shape
    short = out_ref.shape[0] - (parts - 1) * count

    def each(act):
        for index, (o, sources) in enumerate(marks):
            for part, (m, mask) in enumerate(sources):
                group, core, space = place()
                at = (space ^ mask) * count
                row = pl.multiple_of(((group ^ m) * 2 + (core ^ o)) * block, block)
                source = refs[index].at[part]

                def copy(lo, hi, sem):
                    target = out_ref.at[pl.ds(at + lo, hi - lo), pl.ds(row, block)]
                    return pltpu.make_async_copy(source.at[lo:hi], target, sems.at[index, part, sem])

                getattr(copy(0, short, 0), act)()
                if short < count:
                    pl.when((space ^ mask) < parts - 1)(getattr(copy(short, count, 1), act))

    each("start")
    each("wait")


def assemble(pieces, marks, parts, groups, offsets, width, after, base=()):
    most = max(piece.shape[0] for piece in pieces)
    return pl.pallas_call(
        functools.partial(assemble_kernel, marks, parts, groups),
        out_shape=jax.ShapeDtypeStruct((offsets, width, width), BF),
        in_specs=[ANY] * (len(pieces) + len(after)) + [HBM] * len(base),
        out_specs=HBM,
        scratch_shapes=[pltpu.SemaphoreType.DMA((len(pieces), most, 2))],
        input_output_aliases={len(pieces) + len(after): 0} if base else {},
        compiler_params=params(),
        cost_estimate=cost(),
        name="assemble",
    )(*pieces, *after, *base)


def assemble_plain(pieces, marks, parts, groups, offsets, width):
    _, count, block, _ = pieces[0].shape
    total = jnp.zeros((parts * count, width, width), BF)
    for piece, (o, sources) in zip(pieces, marks):
        for part, (m, mask) in enumerate(sources):
            group, core, space = place()
            row = ((group ^ m) * 2 + (core ^ o)) * block
            total = lax.dynamic_update_slice(total, piece[part], ((space ^ mask) * count, row, 0))
    return total[:offsets]


def swap(value, axis, mask):
    return lax.ppermute(value, axis, [(i, i ^ mask) for i in range(lax.axis_size(axis))])


def met(value, turn):
    count = lax.axis_size("space")
    starts = range(turn, count - 1, 2)
    return lax.ppermute(value, "space", [(i, i + 1) for i in starts] + [(i + 1, i) for i in starts])


def shards(features, weights, cotangent, kernel_map, live, send_up, send_down):
    rows, width = features.shape
    offsets, halo = weights.shape[0], send_up.shape[1]
    groups = lax.axis_size("dp") // 2
    parts = lax.axis_size("space")
    count = -(-offsets // parts)
    slab = width // groups
    map_rows = -(-offsets // 16) * 16

    pack, first_rows, second_rows, *packs = prep(
        features, cotangent, kernel_map, send_up, send_down, map_rows, groups
    )
    packs = [swap(part, "dp", 2 * m) for m, part in enumerate(packs, 1)]
    pack, own_part = near_pack(pack, rows, slab)
    own_set = wgrad_own([own_part], offsets, slab, rows)
    halo_rows, own_halo, *halos = joined(met(first_rows, 0), met(second_rows, 1), groups, own_set[1])
    halos = [swap(part, "dp", 2 * m) for m, part in enumerate(halos, 1)]
    rest_set = wgrad_own(packs, offsets, slab, rows)
    early = wgrad_early(own_set, rest_set, [own_halo, *halos[:-1]], parts * count)
    keep, send = wgrad(early, own_set, rest_set, halos[-1], parts * count)
    mine, *coded = blocks(keep, swap(send, "dp", 1), parts)
    own_grad, first_grad, second_grad, token = backward(pack, weights, rows, halo, mine)
    first_back, second_back = met(first_grad, 0), met(second_grad, 1)
    scale = 1.0 / math.sqrt(rows * lax.axis_size("dp") * parts)
    rounded = scaled_total(mine, [swap(block, "space", m + 1) for m, block in enumerate(coded)], scale, (token, token))
    out_features, token = forward(pack, halo_rows, weights, rows, rounded)

    along = [swap(rounded, "space", m) for m in range(1, parts)]
    across = {m: swap(rounded, "dp", 2 * m) for m in range(1, groups)}
    lines = gate(stack(along, [token]), list(across.values()))
    far = {m: swap(lines, "dp", 2 * m) for m in range(1, groups)}
    line_masks = range(1, parts)
    grad_features, token = final(offsets, pack, own_grad, first_back, second_back, send_up, send_down, lines)
    near = stack([rounded, lines], [token])
    sides = stack([across[m] for m in range(1, groups)], [])
    near_marks = [(0, mask) for mask in range(parts)]
    side_marks = [(m, 0) for m in range(1, groups)]
    pieces = [near, swap(near, "dp", 1), sides, swap(sides, "dp", 1)]
    marks = [(0, near_marks), (1, near_marks), (0, side_marks), (1, side_marks)]
    dense = rounded.shape[1] % 16 == 0 and parts * count - offsets < count
    sizes = (parts, groups, offsets, width)
    first = ()
    if dense:
        first = (assemble(pieces, marks, *sizes, ()),)
        pieces, marks = [], []
    for m in range(1, groups):
        pieces += [far[m], swap(far[m], "dp", 1)]
        marks += [(o, [(m, mask) for mask in line_masks]) for o in range(2)]
    if dense:
        grad_weights = assemble(pieces, marks, *sizes, (token,), first)
    else:
        grad_weights = assemble_plain(pieces, marks, *sizes)
    return (out_features, grad_features, grad_weights)


def solution(mesh):
    placed = (
        P(("dp", "space"), None),
        P(),
        P(("dp", "space"), None),
        P(None, ("dp", "space")),
        P(("dp", "space")),
        P(("dp", "space"), None),
        P(("dp", "space"), None),
    )
    return jax.shard_map(
        shards,
        mesh=mesh,
        in_specs=placed,
        out_specs=(P(("dp", "space"), None), P(("dp", "space"), None), P()),
        check_vma=False,
    )
```

```python
import functools
import math

import jax
import jax.numpy as jnp
from jax import lax
from jax.experimental import pallas as pl
from jax.experimental.pallas import tpu as pltpu
from jax.sharding import PartitionSpec as P

BF = jnp.bfloat16
F32 = jnp.float32
VMEM_LIMIT = 32 * 1024 * 1024
PREP_LIMIT = 60 * 1024 * 1024
VMEM = pl.BlockSpec(memory_space=pltpu.VMEM)
ANY = pl.BlockSpec(memory_space=pl.ANY)
HBM = pl.BlockSpec(memory_space=pltpu.HBM)
TOKEN = jax.ShapeDtypeStruct((8, 128), F32)


def params(limit=VMEM_LIMIT):
    return pltpu.CompilerParams(vmem_limit_bytes=limit)


def cost():
    return pl.CostEstimate(flops=100_000_000, bytes_accessed=100_000, transcendentals=0)


def dot(a, b):
    return jnp.dot(a, b, preferred_element_type=F32)


def split(value, terms):
    parts = []
    for _ in range(terms):
        part = value.astype(BF)
        parts.append(part)
        value = value - part.astype(F32)
    return parts


def place():
    dp = lax.axis_index("dp")
    return dp // 2, lax.rem(dp, 2), lax.axis_index("space")


def turns(up, down):
    even = lax.rem(place()[2], 2) == 0
    return jnp.where(even, up, down), jnp.where(even, down, up)


def live_rows(maps, offsets, width, zero_slot):
    rows = maps.shape[1]
    centre = jnp.transpose(jnp.broadcast_to(maps[offsets // 2 : offsets // 2 + 1, :], (128, rows)))
    return jnp.concatenate([centre] * (width // 128), axis=1) != zero_slot


def prep_kernel(x_hbm, dy_hbm, map_hbm, up_hbm, down_hbm, pack_ref, first_ref, second_ref, *refs):
    part_refs, (x_ref, dy_ref, map_ref, up_ref, down_ref, map_scr, turned, sems) = refs[:-8], refs[-8:]
    sources = (x_hbm, dy_hbm, map_hbm, up_hbm, down_hbm)
    targets = (x_ref, dy_ref, map_ref, up_ref, down_ref)
    copies = [pltpu.make_async_copy(a, b, sems.at[i]) for i, (a, b) in enumerate(zip(sources, targets))]
    for copy in copies:
        copy.start()
    rows, width = x_ref.shape
    offsets = map_ref.shape[0]
    halo = up_ref.shape[1]
    zero_slot = rows + 2 * halo
    map_scr[...] = jnp.full(map_scr.shape, zero_slot, jnp.int32)
    for copy in copies:
        copy.wait()
    keep = live_rows(map_ref[...], offsets, width, zero_slot)
    x_live = jnp.where(keep, x_ref[...].astype(F32), 0.0).astype(BF)
    pack_ref[0:rows] = x_live
    iota = lax.broadcasted_iota(jnp.int32, (rows, halo), 0)
    for index, picked_ref in zip(turns(up_ref[...], down_ref[...]), (first_ref, second_ref)):
        chosen = (iota == index).astype(F32).astype(BF)
        picked_ref[...] = lax.dot_general(chosen, x_live, (((0,), (0,)), ((), ())), preferred_element_type=F32).astype(BF)
    pack_ref[rows : 2 * rows] = jnp.where(keep, dy_ref[...].astype(F32), 0.0).astype(BF)
    map_scr[0:offsets] = map_ref[...]
    slots = map_scr[...]
    pack_ref[2 * rows :] = jnp.where(slots > 256, 256 - slots, slots).astype(F32).astype(BF)
    turned[...] = jnp.transpose(x_live)
    for m, part_ref in enumerate(part_refs):
        slab = part_ref.shape[0] - (pack_ref.shape[0] - rows)
        part_ref[0:slab] = turned[pl.ds(pl.multiple_of((place()[0] ^ (m + 1)) * slab, slab), slab), :]
        part_ref[slab:] = pack_ref[rows:]


def prep(features, cotangent, kernel_map, send_up, send_down, map_rows, groups):
    rows, width = features.shape
    return pl.pallas_call(
        prep_kernel,
        out_shape=(
            jax.ShapeDtypeStruct((2 * rows + map_rows, width), BF),
            jax.ShapeDtypeStruct((send_up.shape[1], width), BF),
            jax.ShapeDtypeStruct((send_up.shape[1], width), BF),
            *(jax.ShapeDtypeStruct((width // groups + rows + map_rows, rows), BF),) * (groups - 1),
        ),
        in_specs=[HBM] * 5,
        out_specs=(VMEM,) * (2 + groups),
        scratch_shapes=[
            pltpu.VMEM((rows, width), BF),
            pltpu.VMEM((rows, width), BF),
            pltpu.VMEM(kernel_map.shape, jnp.int32),
            pltpu.VMEM(send_up.shape, jnp.int32),
            pltpu.VMEM(send_down.shape, jnp.int32),
            pltpu.VMEM((map_rows, rows), jnp.int32),
            pltpu.VMEM((width, rows), BF),
            pltpu.SemaphoreType.DMA((5,)),
        ],
        compiler_params=params(PREP_LIMIT),
        name="prep",
    )(features, cotangent, kernel_map, send_up, send_down)


def decoded(code):
    code = code.astype(F32).astype(jnp.int32)
    return jnp.where(code < 0, 256 - code, code)


def backward_kernel(group, pack_ref, w_ref, after_ref, own_ref, first_ref, second_ref, token_ref, *scratch):
    maps, chosen, terms, low_ref, high_ref = scratch
    offsets, width, _ = w_ref.shape
    rows = own_ref.shape[0]
    slots = chosen.shape[1]
    maps[...] = decoded(pack_ref[2 * rows :])
    dy = pack_ref[rows : 2 * rows]
    slot_down = lax.broadcasted_iota(jnp.int32, (slots, rows), 0)
    for k in range(offsets):
        at = slice(k % group * rows, (k % group + 1) * rows)
        chosen[k // group, :, at] = (slot_down == maps[k : k + 1, :]).astype(F32).astype(BF)
        back = lax.dot_general(dy, w_ref[k], (((1,), (1,)), ((), ())), preferred_element_type=F32)
        for t, part in enumerate(split(back, 2)):
            terms[k // group, t, at] = part
    for g in range(offsets // group):
        at = 0
        for out in (own_ref, low_ref, high_ref):
            some = chosen[g, at : at + out.shape[0]]
            value = dot(some, terms[g, 0]) + dot(some, terms[g, 1])
            out[...] = value if g == 0 else out[...] + value
            at += out.shape[0]
    first_ref[...], second_ref[...] = turns(high_ref[...], low_ref[...])
    token_ref[...] = jnp.zeros_like(token_ref)


def backward(pack, weights, rows, halo, after):
    offsets, width, _ = weights.shape
    slots = rows + 2 * halo
    group = 3 if offsets % 3 == 0 else 1
    return pl.pallas_call(
        functools.partial(backward_kernel, group),
        out_shape=tuple(jax.ShapeDtypeStruct((n, width), F32) for n in (rows, halo, halo)) + (TOKEN,),
        in_specs=[VMEM, VMEM, ANY],
        out_specs=(VMEM,) * 4,
        scratch_shapes=[
            pltpu.VMEM((pack.shape[0] - 2 * rows, rows), jnp.int32),
            pltpu.VMEM((offsets // group, slots, group * rows), BF),
            pltpu.VMEM((offsets // group, 2, group * rows, width), BF),
            pltpu.VMEM((halo, width), F32),
            pltpu.VMEM((halo, width), F32),
        ],
        compiler_params=params(),
        cost_estimate=cost(),
        name="backward",
    )(pack, weights, after)


def forward_kernel(group, pack_ref, halo_ref, w_ref, after_ref, out_ref, token_ref, table, maps, out_acc, picked):
    offsets, width, _ = w_ref.shape
    rows = out_ref.shape[0]
    slots = table.shape[0]
    table[0:rows] = pack_ref[0:rows]
    table[rows:] = halo_ref[...]
    codes = decoded(pack_ref[2 * rows :])
    maps[...] = jnp.transpose(jnp.concatenate([codes] * (maps.shape[1] // codes.shape[0]), axis=0))
    along = lax.broadcasted_iota(jnp.int32, (rows, 128), 1)
    for k in range(offsets):
        column = jnp.broadcast_to(maps[:, k : k + 1], (rows, 128))
        chosen = jnp.concatenate(
            [(along + 128 * b == column).astype(F32).astype(BF) for b in range(slots // 128)], axis=1
        )
        picked[k // group, :, k % group * width : (k % group + 1) * width] = dot(chosen, table[...]).astype(BF)
    for g in range(offsets // group):
        value = dot(picked[g], w_ref[g * group : (g + 1) * group].reshape(group * width, width))
        out_acc[...] = value if g == 0 else out_acc[...] + value
    keep = jnp.broadcast_to(maps[:, offsets // 2 : offsets // 2 + 1], (rows, width)) != slots
    out_ref[...] = jnp.where(keep, out_acc[...], 0.0).astype(BF)
    token_ref[...] = jnp.zeros_like(token_ref)


def forward(pack, halo_rows, weights, rows, after):
    offsets, width, _ = weights.shape
    slots = rows + halo_rows.shape[0]
    group = 3 if offsets % 3 == 0 else 1
    return pl.pallas_call(
        functools.partial(forward_kernel, group),
        out_shape=(jax.ShapeDtypeStruct((rows, width), BF), TOKEN),
        in_specs=[VMEM, VMEM, VMEM, ANY],
        out_specs=(VMEM, VMEM),
        scratch_shapes=[
            pltpu.VMEM((slots, width), BF),
            pltpu.VMEM((rows, 128), jnp.int32),
            pltpu.VMEM((rows, width), F32),
            pltpu.VMEM((offsets // group, rows, group * width), BF),
        ],
        compiler_params=params(),
        cost_estimate=cost(),
        name="forward",
    )(pack, halo_rows, weights, after)


def chosen_slots(maps, s, at, low, high, rows):
    slot = (lax.broadcasted_iota(jnp.int32, (high - low, rows), 0) + low).astype(jnp.int16)
    wanted = jnp.broadcast_to(maps[s, at : at + 1, :].astype(jnp.int16), (high - low, rows))
    return jnp.where(slot == wanted, jnp.ones((), BF), jnp.zeros((), BF))


def wgrad_own_kernel(offsets, *refs):
    packs, (picked_ref, dys, maps) = refs[:-3], refs[-3:]
    sources, _, rows = maps.shape
    slab = picked_ref.shape[1]
    for s in range(sources):
        dys[s * rows : (s + 1) * rows] = packs[s][slab : slab + rows]
        maps[s] = decoded(packs[s][slab + rows :])
    for j in range(offsets):
        for s in range(sources):
            chosen = chosen_slots(maps, s, j, 0, rows, rows)
            picked_ref[j, :, s * rows : (s + 1) * rows] = dot(packs[s][0:slab], chosen).astype(BF)


def wgrad_own(packs, offsets, slab, rows):
    sources, width = len(packs), packs[0].shape[1]
    return pl.pallas_call(
        functools.partial(wgrad_own_kernel, offsets),
        out_shape=(
            jax.ShapeDtypeStruct((offsets, slab, sources * rows), BF),
            jax.ShapeDtypeStruct((sources * rows, width), BF),
            jax.ShapeDtypeStruct((sources, packs[0].shape[0] - slab - rows, rows), jnp.int32),
        ),
        in_specs=[VMEM] * sources,
        out_specs=(VMEM, VMEM, VMEM),
        compiler_params=params(),
        cost_estimate=cost(),
        name="wgrad_own",
    )(*packs)


def picked_rows(out_ref, part, j, near_ref, maps, i, halo_ref):
    rows, half = maps.shape[2], near_ref.shape[1] // 2
    chosen = chosen_slots(maps, i, j, rows, rows + halo_ref.shape[1], rows)
    near = near_ref[j, :, i * rows : (i + 1) * rows].astype(F32)
    value = (dot(halo_ref[...], chosen) + near).astype(BF)
    for h in range(2):
        out_ref[h, j * half : (j + 1) * half, part * rows : (part + 1) * rows] = value[h * half : (h + 1) * half]


def clear_rest(out_ref, offsets, half):
    _, size, columns = out_ref.shape
    if offsets * half < size:
        out_ref[:, offsets * half :] = jnp.zeros((2, size - offsets * half, columns), BF)


def early_kernel(own_ref, own_maps, rest_ref, rest_maps, *refs):
    halos, out_ref = refs[:-1], refs[-1]
    offsets, slab, _ = own_ref.shape
    for j in range(offsets):
        for s, halo_ref in enumerate(halos):
            near = (own_ref, own_maps, 0) if s == 0 else (rest_ref, rest_maps, s - 1)
            picked_rows(out_ref, s, j, *near, halo_ref)
    clear_rest(out_ref, offsets, slab // 2)


def wgrad_early(own_set, rest_set, halos, count):
    own, _, own_maps = own_set
    rest, _, rest_maps = rest_set
    _, slab, rows = own.shape
    return pl.pallas_call(
        early_kernel,
        out_shape=jax.ShapeDtypeStruct((2, count * slab // 2, len(halos) * rows), BF),
        in_specs=[VMEM] * (4 + len(halos)),
        out_specs=VMEM,
        compiler_params=params(),
        cost_estimate=cost(),
        name="wgrad_early",
    )(own, own_maps, rest, rest_maps, *halos)


def half_sum(early_ref, own_dys, rest_dys, picked_ref, h):
    rows = own_dys.shape[0]
    last = rest_dys.shape[0] - rows
    total = dot(early_ref[h, :, 0:rows], own_dys[...]) + dot(early_ref[h, :, rows:], rest_dys[0:last])
    return total + dot(picked_ref[h], rest_dys[last:])


def send_kernel(early_ref, own_dys, rest_ref, rest_dys, rest_maps, halo_ref, send_ref, picked_ref):
    offsets, slab, _ = rest_ref.shape
    for j in range(offsets):
        picked_rows(picked_ref, 0, j, rest_ref, rest_maps, rest_maps.shape[0] - 1, halo_ref)
    clear_rest(picked_ref, offsets, slab // 2)
    total = half_sum(early_ref, own_dys, rest_dys, picked_ref, 1 - place()[1])
    send_ref[...] = total.reshape(send_ref.shape)


def keep_kernel(early_ref, own_dys, rest_dys, picked_ref, after_ref, keep_ref):
    total = half_sum(early_ref, own_dys, rest_dys, picked_ref, place()[1])
    keep_ref[...] = total.reshape(keep_ref.shape)


def wgrad(early, own_set, rest_set, halo, count):
    rest, rest_dys, rest_maps = rest_set
    _, slab, _ = rest.shape
    shape = jax.ShapeDtypeStruct((count, slab // 2, rest_dys.shape[1]), F32)
    send, picked = pl.pallas_call(
        send_kernel,
        out_shape=(shape, jax.ShapeDtypeStruct((2, count * slab // 2, rest_maps.shape[2]), BF)),
        in_specs=[VMEM] * 6,
        out_specs=(VMEM, VMEM),
        compiler_params=params(),
        cost_estimate=cost(),
        name="wgrad_send",
    )(early, own_set[1], rest, rest_dys, rest_maps, halo)
    keep = pl.pallas_call(
        keep_kernel,
        out_shape=shape,
        in_specs=[VMEM] * 4 + [ANY],
        out_specs=VMEM,
        compiler_params=params(),
        cost_estimate=cost(),
        name="wgrad_keep",
    )(early, own_set[1], rest_dys, picked, send)
    return keep, send


def power(exponent):
    value = jnp.ones(exponent.shape, F32)
    size = jnp.abs(exponent)
    for bit in range(7):
        factor = jnp.where(exponent < 0, 0.5 ** (1 << bit), 2.0 ** (1 << bit))
        value = value * jnp.where((size >> bit) & 1 == 1, factor, 1.0)
    return value


def near_kernel(pack_ref, copy_ref, own_ref, turned):
    slab = own_ref.shape[0] - (pack_ref.shape[0] - turned.shape[1])
    rows = turned.shape[1]
    copy_ref[...] = pack_ref[...]
    turned[...] = jnp.transpose(pack_ref[0:rows])
    own_ref[0:slab] = turned[pl.ds(pl.multiple_of(place()[0] * slab, slab), slab), :]
    own_ref[slab:] = pack_ref[rows:]


def near_pack(pack, rows, slab):
    width = pack.shape[1]
    return pl.pallas_call(
        near_kernel,
        out_shape=(
            jax.ShapeDtypeStruct(pack.shape, BF),
            jax.ShapeDtypeStruct((slab + pack.shape[0] - rows, width), BF),
        ),
        in_specs=[VMEM],
        out_specs=(VMEM, VMEM),
        scratch_shapes=[pltpu.VMEM((width, rows), BF)],
        compiler_params=params(),
        cost_estimate=cost(),
        name="near_pack",
    )(pack)


def joined_kernel(first_ref, second_ref, after_ref, out_ref, *refs):
    turned, halo_refs = refs[-1], refs[:-1]
    halo = first_ref.shape[0]
    slab = halo_refs[0].shape[0]
    second, first = turns(0, halo)
    out_ref[pl.ds(pl.multiple_of(first, halo), halo)] = first_ref[...]
    out_ref[pl.ds(pl.multiple_of(second, halo), halo)] = second_ref[...]
    turned[...] = jnp.transpose(out_ref[...])
    for m, halo_ref in enumerate(halo_refs):
        halo_ref[...] = turned[pl.ds(pl.multiple_of((place()[0] ^ m) * slab, slab), slab), :]


def joined(first, second, groups, after):
    halo, width = first.shape
    slab = width // groups
    return pl.pallas_call(
        joined_kernel,
        out_shape=(
            jax.ShapeDtypeStruct((2 * halo, width), BF),
            *(jax.ShapeDtypeStruct((slab, 2 * halo), BF),) * groups,
        ),
        in_specs=[VMEM] * 2 + [ANY],
        out_specs=(VMEM,) * (1 + groups),
        scratch_shapes=[pltpu.VMEM((width, 2 * halo), BF)],
        compiler_params=params(),
        cost_estimate=cost(),
        name="joined",
    )(first, second, after)


def blocks_kernel(keep_ref, got_ref, mine_ref, *refs):
    coded_refs, exponents = refs[:-1], refs[-1]
    count, block, width = mine_ref.shape
    for m in range(len(coded_refs) + 1):
        at = (place()[2] ^ m) * count
        if m == 0:
            mine_ref[...] = keep_ref[pl.ds(at, count)] + got_ref[pl.ds(at, count)]
            continue
        exponents[...] = jnp.zeros_like(exponents)
        for j in range(count):
            value = keep_ref[at + j] + got_ref[at + j]
            largest = jnp.max(jnp.abs(value), axis=0, keepdims=True)
            exponent = jnp.ceil(jnp.log(jnp.maximum(largest, 2.0**-100)) * (1.0 / math.log(2.0)))
            exponent = jnp.clip(exponent, -100.0, 100.0).astype(jnp.int32) - 15
            exponents[j : j + 1, :] = exponent
            scaled = jnp.round(jnp.clip(value * power(-exponent), -32767.0, 32767.0))
            coded_refs[m - 1][j * block : (j + 1) * block] = scaled.astype(jnp.int32).astype(jnp.int16)
        coded_refs[m - 1][count * block :] = exponents[...].astype(jnp.int16)


def blocks(keep, got, parts):
    total, block, width = keep.shape
    count = total // parts
    extra = -(-count // 16) * 16
    return pl.pallas_call(
        blocks_kernel,
        out_shape=(
            jax.ShapeDtypeStruct((count, block, width), F32),
            *(jax.ShapeDtypeStruct((count * block + extra, width), jnp.int16),) * (parts - 1),
        ),
        in_specs=[VMEM, VMEM],
        out_specs=(VMEM,) * parts,
        scratch_shapes=[pltpu.VMEM((extra, width), jnp.int32)],
        compiler_params=params(),
        cost_estimate=cost(),
        name="blocks",
    )(keep, got)


def total_kernel(scale, mine_ref, *refs):
    *coded_refs, _, _, out_ref = refs
    count, block, width = mine_ref.shape
    powers = [power(ref[count * block :].astype(jnp.int32)) for ref in coded_refs]
    for j in range(count):
        total = mine_ref[j]
        for ref, factor in zip(coded_refs, powers):
            value = ref[j * block : (j + 1) * block].astype(jnp.int32).astype(F32)
            total = total + value * factor[j : j + 1, :]
        out_ref[j] = (total * scale).astype(BF)


def scaled_total(mine, coded, scale, after):
    return pl.pallas_call(
        functools.partial(total_kernel, scale),
        out_shape=jax.ShapeDtypeStruct(mine.shape, BF),
        in_specs=[VMEM] * (len(coded) + 1) + [ANY] * 2,
        out_specs=VMEM,
        compiler_params=params(),
        cost_estimate=cost(),
        name="total",
    )(mine, *coded, *after)


def final_kernel(offsets, pack_ref, own_ref, first_ref, second_ref, up_ref, down_ref, after_ref, out_ref, token_ref):
    rows, width = own_ref.shape
    halo = up_ref.shape[1]
    total = own_ref[...]
    iota = lax.broadcasted_iota(jnp.int32, (rows, halo), 0)
    chosen = [(iota == index).astype(F32) for index in turns(up_ref[...], down_ref[...])]
    chosen = jnp.concatenate(chosen, axis=1).astype(BF)
    for part in split(jnp.concatenate([first_ref[...], second_ref[...]], axis=0), 3):
        total = total + dot(chosen, part)
    keep = live_rows(decoded(pack_ref[2 * rows :]), offsets, width, rows + 2 * halo)
    out_ref[...] = jnp.where(keep, total, 0.0).astype(BF)
    token_ref[...] = jnp.zeros_like(token_ref)


def final(offsets, pack, own_grad, first_back, second_back, send_up, send_down, after):
    return pl.pallas_call(
        functools.partial(final_kernel, offsets),
        out_shape=(jax.ShapeDtypeStruct(own_grad.shape, BF), TOKEN),
        in_specs=[VMEM] * 6 + [ANY],
        out_specs=(VMEM, VMEM),
        compiler_params=params(),
        name="final",
    )(pack, own_grad, first_back, second_back, send_up, send_down, after)


def stack_kernel(count, *refs):
    at = 0
    for ref in refs[:count]:
        for m in range(ref.shape[0] if len(ref.shape) == 4 else 1):
            refs[-1][at] = ref[m] if len(ref.shape) == 4 else ref[...]
            at += 1


def stack(arrays, after):
    blocks = sum(array.shape[0] if array.ndim == 4 else 1 for array in arrays)
    return pl.pallas_call(
        functools.partial(stack_kernel, len(arrays)),
        out_shape=jax.ShapeDtypeStruct((blocks, *arrays[0].shape[-3:]), BF),
        in_specs=[VMEM] * len(arrays) + [ANY] * len(after),
        out_specs=VMEM,
        compiler_params=params(),
        cost_estimate=cost(),
        name="stack",
    )(*arrays, *after)


def gate_kernel(*refs):
    pass


def gate(value, after):
    return pl.pallas_call(
        gate_kernel,
        out_shape=jax.ShapeDtypeStruct(value.shape, value.dtype),
        in_specs=[ANY] * (1 + len(after)),
        out_specs=ANY,
        input_output_aliases={0: 0},
        compiler_params=params(),
        cost_estimate=cost(),
        name="gate",
    )(value, *after)


def assemble_kernel(marks, parts, groups, *refs):
    out_ref, sems = refs[-2:]
    _, count, block, _ = refs[0].shape
    short = out_ref.shape[0] - (parts - 1) * count

    def each(act):
        for index, (o, sources) in enumerate(marks):
            for part, (m, mask) in enumerate(sources):
                group, core, space = place()
                at = (space ^ mask) * count
                row = pl.multiple_of(((group ^ m) * 2 + (core ^ o)) * block, block)
                source = refs[index].at[part]

                def copy(lo, hi, sem):
                    target = out_ref.at[pl.ds(at + lo, hi - lo), pl.ds(row, block)]
                    return pltpu.make_async_copy(source.at[lo:hi], target, sems.at[index, part, sem])

                getattr(copy(0, short, 0), act)()
                if short < count:
                    pl.when((space ^ mask) < parts - 1)(getattr(copy(short, count, 1), act))

    each("start")
    each("wait")


def assemble(pieces, marks, parts, groups, offsets, width, after, base=()):
    most = max(piece.shape[0] for piece in pieces)
    return pl.pallas_call(
        functools.partial(assemble_kernel, marks, parts, groups),
        out_shape=jax.ShapeDtypeStruct((offsets, width, width), BF),
        in_specs=[ANY] * (len(pieces) + len(after)) + [HBM] * len(base),
        out_specs=HBM,
        scratch_shapes=[pltpu.SemaphoreType.DMA((len(pieces), most, 2))],
        input_output_aliases={len(pieces) + len(after): 0} if base else {},
        compiler_params=params(),
        cost_estimate=cost(),
        name="assemble",
    )(*pieces, *after, *base)


def assemble_plain(pieces, marks, parts, groups, offsets, width):
    _, count, block, _ = pieces[0].shape
    total = jnp.zeros((parts * count, width, width), BF)
    for piece, (o, sources) in zip(pieces, marks):
        for part, (m, mask) in enumerate(sources):
            group, core, space = place()
            row = ((group ^ m) * 2 + (core ^ o)) * block
            total = lax.dynamic_update_slice(total, piece[part], ((space ^ mask) * count, row, 0))
    return total[:offsets]


def swap(value, axis, mask):
    return lax.ppermute(value, axis, [(i, i ^ mask) for i in range(lax.axis_size(axis))])


def met(value, turn):
    count = lax.axis_size("space")
    starts = range(turn, count - 1, 2)
    return lax.ppermute(value, "space", [(i, i + 1) for i in starts] + [(i + 1, i) for i in starts])


def shards(features, weights, cotangent, kernel_map, live, send_up, send_down):
    rows, width = features.shape
    offsets, halo = weights.shape[0], send_up.shape[1]
    groups = lax.axis_size("dp") // 2
    parts = lax.axis_size("space")
    count = -(-offsets // parts)
    slab = width // groups
    map_rows = -(-offsets // 16) * 16

    pack, first_rows, second_rows, *packs = prep(
        features, cotangent, kernel_map, send_up, send_down, map_rows, groups
    )
    packs = [swap(part, "dp", 2 * m) for m, part in enumerate(packs, 1)]
    pack, own_part = near_pack(pack, rows, slab)
    own_set = wgrad_own([own_part], offsets, slab, rows)
    halo_rows, own_halo, *halos = joined(met(first_rows, 0), met(second_rows, 1), groups, own_set[1])
    halos = [swap(part, "dp", 2 * m) for m, part in enumerate(halos, 1)]
    rest_set = wgrad_own(packs, offsets, slab, rows)
    early = wgrad_early(own_set, rest_set, [own_halo, *halos[:-1]], parts * count)
    keep, send = wgrad(early, own_set, rest_set, halos[-1], parts * count)
    mine, *coded = blocks(keep, swap(send, "dp", 1), parts)
    own_grad, first_grad, second_grad, token = backward(pack, weights, rows, halo, mine)
    first_back, second_back = met(first_grad, 0), met(second_grad, 1)
    scale = 1.0 / math.sqrt(rows * lax.axis_size("dp") * parts)
    rounded = scaled_total(mine, [swap(block, "space", m + 1) for m, block in enumerate(coded)], scale, (token, token))
    out_features, token = forward(pack, halo_rows, weights, rows, rounded)

    along = [swap(rounded, "space", m) for m in range(1, parts)]
    across = {m: swap(rounded, "dp", 2 * m) for m in range(1, groups)}
    lines = gate(stack(along, [token]), list(across.values()))
    far = {m: swap(lines, "dp", 2 * m) for m in range(1, groups)}
    line_masks = range(1, parts)
    grad_features, token = final(offsets, pack, own_grad, first_back, second_back, send_up, send_down, lines)
    near = stack([rounded, lines], [token])
    sides = stack([across[m] for m in range(1, groups)], [])
    near_marks = [(0, mask) for mask in range(parts)]
    side_marks = [(m, 0) for m in range(1, groups)]
    pieces = [near, swap(near, "dp", 1), sides, swap(sides, "dp", 1)]
    marks = [(0, near_marks), (1, near_marks), (0, side_marks), (1, side_marks)]
    dense = rounded.shape[1] % 16 == 0 and parts * count - offsets < count
    sizes = (parts, groups, offsets, width)
    first = ()
    if dense:
        first = (assemble(pieces, marks, *sizes, ()),)
        pieces, marks = [], []
    for m in range(1, groups):
        pieces += [far[m], swap(far[m], "dp", 1)]
        marks += [(o, [(m, mask) for mask in line_masks]) for o in range(2)]
    if dense:
        grad_weights = assemble(pieces, marks, *sizes, (token,), first)
    else:
        grad_weights = assemble_plain(pieces, marks, *sizes)
    return (out_features, grad_features, grad_weights)


def solution(mesh):
    placed = (
        P(("dp", "space"), None),
        P(),
        P(("dp", "space"), None),
        P(None, ("dp", "space")),
        P(("dp", "space")),
        P(("dp", "space"), None),
        P(("dp", "space"), None),
    )
    return jax.shard_map(
        shards,
        mesh=mesh,
        in_specs=placed,
        out_specs=(P(("dp", "space"), None), P(("dp", "space"), None), P()),
        check_vma=False,
    )
```
